32 devices in a mesh: dp: 4 (over z), proto: 8 (over y, x, core).
Axes of the slice: x: 2, y: 2, z: 4, core: 2. Of those that a mesh axis runs over, the one named last changes fastest.
Arguments:
- student_feat: bfloat16 [384, 256], P(('dp', 'proto'))
- teacher_feat: bfloat16 [384, 256], P(('dp', 'proto'))
- prototypes: bfloat16 [8192, 256], P('proto')
- teacher_prototypes: bfloat16 [8192, 256], P('proto')
- live_count: int32 [4], replicated, may hold values from 24 to 96, as said below
Outputs:
- student_grad: float32 [384, 256], P(('dp', 'proto'))
- proto_grad: float32 [8, 1024, 256], P('proto', 'dp')
The draws below stay inside these ranges and needn't reach their ends.
Inputs may be any that keep to these rules, and one draw needn't show every extreme that they name: `live_count`: some group is full (96 live rows) in every draw; live rows are the first ones of each group.
All inputs are finite; a program needn't handle non-finite values.
Results may differ from the reference program's by a relative error of at most 0.0026.
Values may be sent and summed in bfloat16 or wider, within the bound.
No kernel may reach another device: no remote copies, remote signals or barrier semaphores. Data moves between devices by JAX's collectives and lax.ppermute only.
A program may use at most 64 MiB of HBM per device.

```python
import math
import jax
import jax.numpy as jnp
from jax import lax

D = 256
PROTO_DEV = 1024
ITERS = 3
PROTOS = 8192
GROUP_ROWS = 96
ROWS = 384
N_DP = 4
N_PROTO = 8


def shared_direction(key):
    return jax.random.normal(jax.random.fold_in(key, 11), (D,), jnp.float32) / math.sqrt(D)


def spread_rows(key, count_rows):
    return jax.random.normal(key, (count_rows, D), jnp.float32) / math.sqrt(D)


def banded_coordinate(key, block_count, block_size, center_reach, jitter_reach):
    centers = jax.random.uniform(jax.random.fold_in(key, 1), (block_count,), jnp.float32, -center_reach, center_reach)
    jitter = jax.random.uniform(jax.random.fold_in(key, 2), (block_count, block_size), jnp.float32, -jitter_reach, jitter_reach)
    return (centers[:, None] + jitter).reshape(block_count * block_size, 1)


def proto_base(key):
    direction = shared_direction(key)
    band_key = jax.random.fold_in(key, 21)
    along_axis = banded_coordinate(band_key, PROTOS // PROTO_DEV, PROTO_DEV, 2.5, 0.5)
    return along_axis * direction[None, :] + spread_rows(jax.random.fold_in(key, 22), PROTOS)


def feature_base(key):
    direction = shared_direction(key)
    band_key = jax.random.fold_in(key, 31)
    along_axis = banded_coordinate(band_key, ROWS // GROUP_ROWS, GROUP_ROWS, 2.0, 0.7)
    return along_axis * direction[None, :] + spread_rows(jax.random.fold_in(key, 32), ROWS)


def draw_prototypes(key, part):
    return proto_base(key).astype(jnp.bfloat16)


def draw_teacher_prototypes(key, part):
    jitter = jax.random.normal(jax.random.fold_in(key, 23), (PROTOS, D), jnp.float32) / math.sqrt(D)
    return (proto_base(key) + 0.3 * jitter).astype(jnp.bfloat16)


def draw_student_feat(key, part):
    jitter = jax.random.normal(jax.random.fold_in(key, 33), (ROWS, D), jnp.float32) / math.sqrt(D)
    return (feature_base(key) + 0.3 * jitter).astype(jnp.bfloat16)


def draw_teacher_feat(key, part):
    jitter = jax.random.normal(jax.random.fold_in(key, 34), (ROWS, D), jnp.float32) / math.sqrt(D)
    return (feature_base(key) + 0.3 * jitter).astype(jnp.bfloat16)


def draw_live_count(key, part):
    counts = jax.random.randint(jax.random.fold_in(key, 41), (N_DP,), GROUP_ROWS // 4, GROUP_ROWS + 1)
    full_group = jax.random.randint(jax.random.fold_in(key, 42), (), 0, N_DP)
    return jnp.where(jnp.arange(N_DP) == full_group, GROUP_ROWS, counts).astype(jnp.int32)


def setup_inputs(seed: int = 0) -> dict:
    key_list = jax.random.split(jax.random.key(seed), 6)
    return {
        "student_feat": draw_student_feat(jax.random.fold_in(key_list[5], 71), 0),
        "teacher_feat": draw_teacher_feat(jax.random.fold_in(key_list[5], 71), 0),
        "prototypes": draw_prototypes(jax.random.fold_in(key_list[5], 71), 0),
        "teacher_prototypes": draw_teacher_prototypes(jax.random.fold_in(key_list[5], 71), 0),
        "live_count": draw_live_count(jax.random.fold_in(key_list[5], 71), 0),
    }


student_temp = 0.1
teacher_temp = 0.07
eps_norm = 1e-06

def unit_rows(values):
    widened = values.astype(jnp.float32)
    length = jnp.sqrt(lax.optimization_barrier(jnp.sum(widened * widened, axis=1, keepdims=True)) + eps_norm)
    return (widened / length, length)

def reference(student_feat, teacher_feat, prototypes, teacher_prototypes, live_count):
    student_unit, student_length = unit_rows(student_feat)
    teacher_unit, teacher_length = unit_rows(teacher_feat)
    student_rows = student_unit.astype(jnp.bfloat16)
    teacher_rows = teacher_unit.astype(jnp.bfloat16)
    row_ids = jnp.arange(ROWS, dtype=jnp.int32)
    group_of = (row_ids // GROUP_ROWS).astype(jnp.int32)
    live_mask = row_ids % GROUP_ROWS < live_count[group_of]
    student_blocks = prototypes.reshape(N_PROTO, PROTO_DEV, D)
    teacher_blocks = teacher_prototypes.reshape(N_PROTO, PROTO_DEV, D)

    def teacher_weights(proto_block):
        unit_block, unused_length = unit_rows(proto_block)
        scores = jnp.dot(teacher_rows, unit_block.astype(jnp.bfloat16).T, preferred_element_type=jnp.float32) / teacher_temp
        return jnp.where(live_mask[:, None], jnp.exp(scores), 0.0)

    def student_logits(proto_block):
        unit_block, block_length = unit_rows(proto_block)
        logits = jnp.dot(student_rows, unit_block.astype(jnp.bfloat16).T, preferred_element_type=jnp.float32) / student_temp
        return (logits, unit_block, block_length)
    scale_rows = live_mask.astype(jnp.float32)
    scale_protos = jnp.zeros((N_PROTO, PROTO_DEV), jnp.float32)
    for iteration in range(ITERS):

        def sweep_block(proto_block, current=scale_rows):
            weights = teacher_weights(proto_block)
            inverse = 1.0 / lax.optimization_barrier(jnp.sum(weights * current[:, None], axis=0))
            return (inverse, jnp.dot(weights, inverse, precision=lax.Precision.HIGHEST))
        scale_protos, row_parts = lax.map(sweep_block, teacher_blocks)
        row_sums = lax.optimization_barrier(jnp.sum(row_parts, axis=0))
        scale_rows = jnp.where(live_mask, 1.0 / jnp.where(live_mask, row_sums, 1.0), 0.0)

    def partition_block(proto_block):
        logits, unit_block, block_length = student_logits(proto_block)
        return lax.optimization_barrier(jnp.sum(jnp.exp(logits), axis=1))
    partition = lax.optimization_barrier(jnp.sum(lax.map(partition_block, student_blocks), axis=0))
    log_partition = jnp.log(partition)

    def final_block(carried, inputs):
        student_block, teacher_block, inverse = inputs
        logits, unit_block, block_length = student_logits(student_block)
        targets = teacher_weights(teacher_block) * inverse[None, :] * scale_rows[:, None]
        probs = jnp.exp(logits - log_partition[:, None])
        grad_logits = jnp.where(live_mask[:, None], (probs - targets) / student_temp, 0.0).astype(jnp.bfloat16)
        carried = carried + jnp.dot(grad_logits, unit_block.astype(jnp.bfloat16), preferred_element_type=jnp.float32)
        pushed = jnp.dot(grad_logits.T, student_rows, preferred_element_type=jnp.float32)
        grad_block = (pushed - unit_block * lax.optimization_barrier(jnp.sum(unit_block * pushed, axis=1, keepdims=True))) / block_length
        return (carried, grad_block)
    pulled, grad_blocks = lax.scan(final_block, jnp.zeros((ROWS, D), jnp.float32), (student_blocks, teacher_blocks, scale_protos))
    student_grad = (pulled - student_unit * lax.optimization_barrier(jnp.sum(student_unit * pulled, axis=1, keepdims=True))) / student_length
    return (student_grad, grad_blocks)
```

```python
import functools

import jax
import jax.numpy as jnp
from jax import lax
from jax.experimental import pallas as pl
from jax.experimental.pallas import tpu as pltpu
from jax.sharding import PartitionSpec as P

ITERS = 3

student_temp = 0.1
teacher_temp = 0.07
eps_norm = 1e-06

SLOTS = 16
LANES = 128
CHUNK = 256
BLOCK_BYTES = 8 * 2**20


def unit_rows(values):
    widened = values.astype(jnp.float32)
    length = jnp.sqrt(jnp.sum(widened * widened, axis=1, keepdims=True) + eps_norm)
    return (widened / length, length)


def live_lanes(live_ref, lanes, group_lanes, rows):
    lane = lax.broadcasted_iota(jnp.int32, (1, lanes), 1)
    group = lane // group_lanes
    slot = lane % SLOTS
    row = (lane % group_lanes) // SLOTS * rows + slot
    count = jnp.zeros((1, lanes), jnp.int32)
    for g in range(lanes // group_lanes):
        count = jnp.where(group == g, live_ref[g], count)
    return (slot < rows) & (row < count)


def pack_lanes(values):
    pieces = [values[:, k : k + LANES] for k in range(0, values.shape[1], LANES)]
    return jnp.concatenate(pieces + [jnp.zeros((8 - len(pieces), LANES), jnp.float32)], axis=0)


def unpack_lanes(tile, lanes):
    return jnp.concatenate([tile[k : k + 1, :] for k in range(lanes // LANES)], axis=1)


def rows_kernel(student_ref, teacher_ref, out_ref, scratch):
    rows = student_ref.shape[0]
    for k, ref in enumerate((student_ref, teacher_ref)):
        unit, _ = unit_rows(ref[...])
        scratch[...] = jnp.zeros_like(scratch)
        scratch[:rows, :] = unit
        out_ref[k * SLOTS : (k + 1) * SLOTS, :] = scratch[...].astype(jnp.bfloat16)


def scores_of(proto_ref, start, rows_all):
    unit, _ = unit_rows(proto_ref[start : start + CHUNK, :])
    unit = unit.astype(jnp.bfloat16)
    return unit, lax.dot_general(
        unit, rows_all, (((1,), (1,)), ((), ())), preferred_element_type=jnp.float32
    )


def weights_kernel(group_lanes, rows, live_ref, gathered_ref, proto_ref, weights_ref, sums_ref):
    lanes = weights_ref.shape[1]
    live = live_lanes(live_ref, lanes, group_lanes, rows)
    rows_all = gathered_ref[:, SLOTS:, :].reshape(lanes, gathered_ref.shape[2])
    sums = jnp.zeros((1, lanes), jnp.float32)
    for start in range(0, proto_ref.shape[0], CHUNK):
        _, scores = scores_of(proto_ref, start, rows_all)
        weights = jnp.where(live, jnp.exp(scores / teacher_temp), 0.0)
        weights_ref[start : start + CHUNK, :] = weights
        inverse = 1.0 / jnp.sum(weights, axis=1, keepdims=True)
        sums = sums + jnp.sum(weights * inverse, axis=0, keepdims=True)
    sums_ref[...] = pack_lanes(sums)


def scale_rows_of(tile, live):
    total = unpack_lanes(tile, live.shape[1])
    return jnp.where(live, 1.0 / jnp.where(live, total, 1.0), 0.0)


def step_kernel(group_lanes, rows, live_ref, parts_ref, weights_ref, sums_ref):
    lanes = weights_ref.shape[1]
    live = live_lanes(live_ref, lanes, group_lanes, rows)
    scale = scale_rows_of(parts_ref[...], live)
    sums = jnp.zeros((1, lanes), jnp.float32)
    for start in range(0, weights_ref.shape[0], CHUNK):
        weights = weights_ref[start : start + CHUNK, :]
        inverse = 1.0 / jnp.sum(weights * scale, axis=1, keepdims=True)
        sums = sums + jnp.sum(weights * inverse, axis=0, keepdims=True)
    sums_ref[...] = pack_lanes(sums)


def split_dot(wide, narrow):
    high = wide.astype(jnp.bfloat16)
    low = (wide - high.astype(jnp.float32)).astype(jnp.bfloat16)
    contract_first = (((0,), (0,)), ((), ()))
    return lax.dot_general(
        high, narrow, contract_first, preferred_element_type=jnp.float32
    ) + lax.dot_general(low, narrow, contract_first, preferred_element_type=jnp.float32)


def last_kernel(
    group_lanes,
    rows,
    place_ref,
    live_ref,
    parts_ref,
    weights_ref,
    gathered_ref,
    proto_ref,
    out_ref,
    targets_ref,
    exps_ref,
    scaled_ref,
    units_ref,
    all_exps_ref,
):
    protos, lanes = weights_ref.shape
    width = proto_ref.shape[1]
    peers = out_ref.shape[0]
    live = live_lanes(live_ref, lanes, group_lanes, rows)
    scale = scale_rows_of(parts_ref[...], live)
    rows_all = gathered_ref[:, :SLOTS, :].reshape(lanes, width)
    sums = jnp.zeros((1, lanes), jnp.float32)
    partition = jnp.zeros((1, lanes), jnp.float32)
    for start in range(0, protos, CHUNK):
        weights = weights_ref[start : start + CHUNK, :]
        inverse = 1.0 / jnp.sum(weights * scale, axis=1, keepdims=True)
        scaled = weights * inverse
        scaled_ref[start : start + CHUNK, :] = scaled
        sums = sums + jnp.sum(scaled, axis=0, keepdims=True)
        unit, scores = scores_of(proto_ref, start, rows_all)
        units_ref[start : start + CHUNK, :] = unit
        exps = jnp.exp(scores / student_temp)
        all_exps_ref[start : start + CHUNK, :] = exps
        partition = partition + jnp.sum(exps, axis=0, keepdims=True)
    dp = place_ref[0]
    own = targets_ref.shape[0]
    first = pl.multiple_of(dp * own, own)
    targets_ref[...] = scaled_ref[pl.ds(first, own), :]
    exps_ref[...] = all_exps_ref[pl.ds(first, own), :]
    group = pl.ds(pl.multiple_of(dp * group_lanes, group_lanes), group_lanes)
    units = units_ref[...]
    exp_pull = split_dot(all_exps_ref[:, group], units)
    target_pull = split_dot(scaled_ref[:, group], units)
    out_ref[:, :SLOTS, :] = exp_pull.reshape(peers, SLOTS, width)
    out_ref[:, SLOTS : 2 * SLOTS, :] = target_pull.reshape(peers, SLOTS, width)
    tile = jnp.concatenate([pack_lanes(sums), pack_lanes(partition)], axis=1)
    out_ref[:, 2 * SLOTS :, :] = jnp.broadcast_to(tile[None], (peers, 8, width))


def grads_kernel(
    group_lanes,
    rows,
    place_ref,
    live_ref,
    got_ref,
    targets_ref,
    exps_ref,
    gathered_ref,
    feat_ref,
    proto_ref,
    student_out_ref,
    proto_out_ref,
    lane_scratch,
    row_scratch,
):
    own, lanes = targets_ref.shape
    width = feat_ref.shape[1]
    live = live_lanes(live_ref, lanes, group_lanes, rows)
    tile = jnp.sum(got_ref[:, 2 * SLOTS :, :], axis=0)
    total = unpack_lanes(tile[:, :LANES], lanes)
    target_scale = jnp.where(live, 1.0 / jnp.where(live, total, 1.0), 0.0)
    exp_scale = jnp.where(live, 1.0 / unpack_lanes(tile[:, LANES:], lanes), 0.0)

    rows_all = gathered_ref[:, :SLOTS, :].reshape(lanes, width)
    grad = (exps_ref[...] * exp_scale - targets_ref[...] * target_scale) / student_temp
    pushed = jnp.dot(grad.astype(jnp.bfloat16), rows_all, preferred_element_type=jnp.float32)
    dp = place_ref[0]
    unit, length = unit_rows(proto_ref[pl.ds(pl.multiple_of(dp * own, own), own), :])
    proto_out_ref[0] = (pushed - unit * jnp.sum(unit * pushed, axis=1, keepdims=True)) / length

    lane_scratch[0:1, :] = target_scale
    lane_scratch[1:2, :] = exp_scale
    group = pl.ds(pl.multiple_of(dp * group_lanes, group_lanes), group_lanes)
    slot = lax.broadcasted_iota(jnp.int32, (SLOTS, group_lanes), 0) + place_ref[1] * SLOTS
    here = lax.broadcasted_iota(jnp.int32, (SLOTS, group_lanes), 1) == slot
    columns = [
        jnp.sum(jnp.where(here, lane_scratch[k : k + 1, group], 0.0), axis=1, keepdims=True)
        for k in range(2)
    ]
    exp_pull = jnp.sum(got_ref[:, :SLOTS, :], axis=0)
    target_pull = jnp.sum(got_ref[:, SLOTS : 2 * SLOTS, :], axis=0)
    row_scratch[...] = (exp_pull * columns[1] - target_pull * columns[0]) / student_temp
    pulled = row_scratch[:rows, :]
    unit, length = unit_rows(feat_ref[...])
    student_out_ref[...] = (
        pulled - unit * jnp.sum(unit * pulled, axis=1, keepdims=True)
    ) / length


def call(kernel, out_shape, operands, smem=0, scratch=()):
    vmem = pl.BlockSpec(memory_space=pltpu.VMEM)
    return pl.pallas_call(
        kernel,
        out_shape=out_shape,
        in_specs=[pl.BlockSpec(memory_space=pltpu.SMEM)] * smem + [vmem] * (len(operands) - smem),
        out_specs=jax.tree.map(lambda _: vmem, out_shape),
        scratch_shapes=scratch,
        compiler_params=pltpu.CompilerParams(vmem_limit_bytes=48 * 2**20),
    )(*operands)


def gather_by_exchange(values, axis):
    copies = jnp.broadcast_to(values[None], (lax.axis_size(axis),) + values.shape)
    return lax.all_to_all(copies, axis, split_axis=0, concat_axis=0, tiled=True)


def pairs(distance):
    return [(k, k ^ distance) for k in range(lax.axis_size("proto"))]


def pairwise_total(values):
    distance = 1
    while distance < lax.axis_size("proto"):
        values = values + lax.ppermute(values, "proto", pairs(distance))
        distance *= 2
    return values


def direct_total(values):
    others = [lax.ppermute(values, "proto", pairs(d)) for d in range(1, lax.axis_size("proto"))]
    return functools.reduce(jnp.add, others, values)


def on_device_all_rows(student_feat, teacher_feat, prototypes, teacher_prototypes, live_count):
    n_dp, n_proto = lax.axis_size("dp"), lax.axis_size("proto")
    rows, width = student_feat.shape
    protos = prototypes.shape[0]
    own = protos // n_dp
    group_lanes = n_proto * SLOTS
    lanes = n_dp * group_lanes
    f32 = functools.partial(jax.ShapeDtypeStruct, dtype=jnp.float32)
    sizes = (group_lanes, rows)
    place = jnp.stack([lax.axis_index("dp"), lax.axis_index("proto")]).astype(jnp.int32)

    unit = call(
        rows_kernel,
        jax.ShapeDtypeStruct((2 * SLOTS, width), jnp.bfloat16),
        (student_feat, teacher_feat),
        scratch=[pltpu.VMEM((SLOTS, width), jnp.float32)],
    )
    gathered = jnp.swapaxes(gather_by_exchange(gather_by_exchange(unit, "dp"), "proto"), 0, 1)
    gathered = gathered.reshape(n_dp * n_proto, 2 * SLOTS, width)
    weights, sums = call(
        functools.partial(weights_kernel, *sizes),
        (f32((protos, lanes)), f32((8, LANES))),
        (live_count, gathered, teacher_prototypes),
        smem=1,
    )
    parts = pairwise_total(sums)
    for _ in range(ITERS - 2):
        sums = call(
            functools.partial(step_kernel, *sizes),
            f32((8, LANES)),
            (live_count, parts, weights),
            smem=1,
        )
        parts = direct_total(sums)
    sent, targets, exps = call(
        functools.partial(last_kernel, *sizes),
        (f32((n_proto, 2 * SLOTS + 8, width)), f32((own, lanes)), f32((own, lanes))),
        (place, live_count, parts, weights, gathered, prototypes),
        smem=2,
        scratch=[
            pltpu.VMEM((protos, lanes), jnp.float32),
            pltpu.VMEM((protos, width), jnp.bfloat16),
            pltpu.VMEM((protos, lanes), jnp.float32),
        ],
    )
    got = lax.all_to_all(sent, "proto", split_axis=0, concat_axis=0, tiled=True)
    return call(
        functools.partial(grads_kernel, *sizes),
        (f32((rows, width)), f32((1, own, width))),
        (place, live_count, got, targets, exps, gathered, student_feat, prototypes),
        smem=2,
        scratch=[
            pltpu.VMEM((8, lanes), jnp.float32),
            pltpu.VMEM((SLOTS, width), jnp.float32),
        ],
    )


def sample_totals(values):
    return lax.psum(values, "proto")


def proto_totals(values):
    return lax.psum(values, "dp")


def on_device_group_rows(student_feat, teacher_feat, prototypes, teacher_prototypes, live_count):
    student_unit, student_length = unit_rows(student_feat)
    teacher_unit, teacher_length = unit_rows(teacher_feat)
    proto_unit, proto_length = unit_rows(prototypes)
    teacher_proto, teacher_proto_length = unit_rows(teacher_prototypes)
    proto_bf = proto_unit.astype(jnp.bfloat16)
    teacher_proto_bf = teacher_proto.astype(jnp.bfloat16)
    student_rows, teacher_rows = (
        lax.all_gather(student_unit.astype(jnp.bfloat16), "proto", axis=0, tiled=True),
        lax.all_gather(teacher_unit.astype(jnp.bfloat16), "proto", axis=0, tiled=True),
    )
    group_size = student_rows.shape[0]
    live_rows = live_count[lax.axis_index("dp")]
    live_mask = jnp.arange(group_size, dtype=jnp.int32) < live_rows
    live_column = live_mask[:, None]
    contract_last = (((1,), (1,)), ((), ()))
    logits = (
        lax.dot_general(student_rows, proto_bf, contract_last, preferred_element_type=jnp.float32)
        / student_temp
    )
    teacher_scores = (
        lax.dot_general(
            teacher_rows, teacher_proto_bf, contract_last, preferred_element_type=jnp.float32
        )
        / teacher_temp
    )
    weights = jnp.where(live_column, jnp.exp(teacher_scores), 0.0)
    partition = sample_totals(jnp.sum(jnp.exp(logits), axis=1))
    targets = weights
    for iteration in range(ITERS):
        targets = targets / proto_totals(jnp.sum(targets, axis=0))[None, :]
        row_sums = sample_totals(jnp.sum(targets, axis=1))
        targets = targets / jnp.where(live_mask, row_sums, 1.0)[:, None]
    student_probs = jnp.exp(logits - jnp.log(partition)[:, None])
    grad_block = jnp.where(live_column, (student_probs - targets) / student_temp, 0.0).astype(
        jnp.bfloat16
    )
    pulled = lax.psum_scatter(
        jnp.dot(grad_block, proto_bf, preferred_element_type=jnp.float32),
        "proto",
        scatter_dimension=0,
        tiled=True,
    )
    student_grad = (
        pulled - student_unit * jnp.sum(student_unit * pulled, axis=1, keepdims=True)
    ) / student_length
    own_protos = prototypes.shape[0] // lax.axis_size("dp")
    contract_first = (((0,), (0,)), ((), ()))
    pushed = lax.psum_scatter(
        lax.dot_general(
            grad_block, student_rows, contract_first, preferred_element_type=jnp.float32
        ),
        "dp",
        scatter_dimension=0,
        tiled=True,
    )
    first_proto = lax.axis_index("dp") * own_protos
    own_units = lax.dynamic_slice_in_dim(proto_unit, first_proto, own_protos, 0)
    own_lengths = lax.dynamic_slice_in_dim(proto_length, first_proto, own_protos, 0)
    proto_grad = (
        pushed - own_units * jnp.sum(own_units * pushed, axis=1, keepdims=True)
    ) / own_lengths
    return (student_grad, proto_grad[None])


def on_device(student_feat, teacher_feat, prototypes, teacher_prototypes, live_count):
    n_dp, n_proto = lax.axis_size("dp"), lax.axis_size("proto")
    rows, width = student_feat.shape
    protos = prototypes.shape[0]
    lanes = n_dp * n_proto * SLOTS
    fits = (
        rows <= SLOTS
        and n_proto & (n_proto - 1) == 0
        and n_proto * SLOTS % LANES == 0
        and lanes <= 8 * LANES
        and width == 2 * LANES
        and protos % CHUNK == 0
        and protos % (n_dp * 16) == 0
        and protos * lanes * 4 <= BLOCK_BYTES
    )
    plan = on_device_all_rows if fits else on_device_group_rows
    return plan(student_feat, teacher_feat, prototypes, teacher_prototypes, live_count)


def solution(mesh):
    return jax.shard_map(
        on_device,
        mesh=mesh,
        in_specs=(
            P(("dp", "proto"), None),
            P(("dp", "proto"), None),
            P("proto", None),
            P("proto", None),
            P(),
        ),
        out_specs=(P(("dp", "proto"), None), P("proto", "dp", None)),
        check_vma=False,
    )
```

```python
import functools

import jax
import jax.numpy as jnp
from jax import lax
from jax.experimental import pallas as pl
from jax.experimental.pallas import tpu as pltpu
from jax.sharding import PartitionSpec as P

ITERS = 3

student_temp = 0.1
teacher_temp = 0.07
eps_norm = 1e-06

LANES = 128
BLOCK_BYTES = 8 * 2**20


def unit_rows(values):
    widened = values.astype(jnp.float32)
    length = jnp.sqrt(jnp.sum(widened * widened, axis=1, keepdims=True) + eps_norm)
    return (widened / length, length)


CORE, X, Y = 1, 2, 4


def quick_unit(values):
    widened = values.astype(jnp.float32)
    squares = jnp.sum(widened * widened, axis=1, keepdims=True) + eps_norm
    scale = lax.rsqrt(squares)
    return widened * scale, scale


def live_lanes(place_ref, lanes, n_dp, rows):
    lane = lax.broadcasted_iota(jnp.int32, (1, lanes), 1)
    live = jnp.zeros((1, lanes), jnp.float32)
    start = 0
    for t in range(n_dp):
        count = place_ref[2 + (place_ref[0] ^ t)]
        for c in range(2):
            for x in range(2):
                for y in range(2):
                    proto = ((place_ref[1] ^ c) & CORE) + X * x + Y * y
                    end = start + jnp.clip(count - proto * rows, 0, rows)
                    live = jnp.where((lane >= start) & (lane < end), 1.0, live)
                    start += rows
    return live


def pack_lanes(values):
    pieces = [values[:, k : k + LANES] for k in range(0, values.shape[1], LANES)]
    return jnp.concatenate(pieces + [jnp.zeros((8 - len(pieces), LANES), jnp.float32)], axis=0)


def unpack_lanes(tile, lanes):
    return jnp.concatenate([tile[k : k + 1, :] for k in range(lanes // LANES)], axis=1)


def as_column(values):
    return jnp.broadcast_to(values, (LANES, values.shape[1])).T


def as_tile(partial):
    return pack_lanes(jnp.sum(partial.T, axis=0, keepdims=True))


def inverse_rows(tile, rows):
    total = unpack_lanes(tile, rows)
    live = total > 0.0
    return jnp.where(live, 1.0 / jnp.where(live, total, 1.0), 0.0)


def units_kernel(student_ref, teacher_ref, student_out_ref, teacher_out_ref):
    for ref, out_ref in ((teacher_ref, teacher_out_ref), (student_ref, student_out_ref)):
        unit, _ = quick_unit(ref[...])
        out_ref[...] = unit.astype(jnp.bfloat16)


def place_rows(place_ref, near_ref, far_ref, which, rows, scratch):
    mine_x = (place_ref[1] >> 1) & 1
    mine_y = (place_ref[1] >> 2) & 1
    start = 0
    for t in range(near_ref.shape[1]):
        for ref in (near_ref, far_ref):
            for x in range(2):
                for y in range(2):
                    block = ref[mine_y ^ y, t, mine_x ^ x].astype(jnp.float32)
                    scratch[start : start + rows, :] = block[which * rows : (which + 1) * rows]
                    start += rows
    unit, _ = quick_unit(scratch[...])
    return unit.astype(jnp.bfloat16)


def scores_of(rows_all, units):
    return lax.dot_general(
        rows_all, units, (((1,), (1,)), ((), ())), preferred_element_type=jnp.float32
    )


def twice(column):
    return jnp.concatenate([column, column], axis=1)


def weighted_rows(weights_ref, scale_ref, part_ref):
    tiles = weights_ref.shape[1] // LANES
    scales = [scale_ref[:, k * LANES : (k + 1) * LANES] for k in range(tiles)]

    def body(i, _):
        at = pl.ds(pl.multiple_of(i * 8, 8), 8)
        sums = [None] * 4
        for k in range(tiles):
            term = weights_ref[at, k * LANES : (k + 1) * LANES] * scales[k]
            sums[k % 4] = term if sums[k % 4] is None else sums[k % 4] + term
        part_ref[at, :] = (sums[0] + sums[1]) + (sums[2] + sums[3])
        return 0

    lax.fori_loop(0, weights_ref.shape[0] // 8, body, 0, unroll=4)


def column_scales(weights_ref, row_ref, scale_ref):
    tiles = weights_ref.shape[1] // LANES

    def body(i, sums):
        at = pl.ds(pl.multiple_of(i * 8, 8), 8)
        row = row_ref[at, :]
        return [
            total + weights_ref[at, k * LANES : (k + 1) * LANES] * row
            for k, total in enumerate(sums)
        ]

    zeros = [jnp.zeros((8, LANES), jnp.float32)] * tiles
    sums = lax.fori_loop(0, weights_ref.shape[0] // 8, body, zeros, unroll=4)
    for k, total in enumerate(sums):
        inverse = 1.0 / jnp.sum(total, axis=0, keepdims=True)
        scale_ref[:, k * LANES : (k + 1) * LANES] = jnp.broadcast_to(inverse, (8, LANES))


def weights_kernel(chunk, place_ref, near_ref, far_ref, *refs):
    *unit_refs, weights_ref, sums_ref, scratch, scale_ref, part_ref = refs
    all_rows = weights_ref.shape[0]
    protos = unit_refs[0].shape[0]
    rows = near_ref.shape[3] // 2
    rows_all = place_rows(place_ref, near_ref, far_ref, 0, rows, scratch)
    live = twice(as_column(live_lanes(place_ref, all_rows, near_ref.shape[1], rows)))
    for k, unit_ref in enumerate(unit_refs):
        for start in range(0, protos, chunk):
            scores = scores_of(rows_all, unit_ref[start : start + chunk, :])
            weights = jnp.exp(scores * (1 / teacher_temp)) * live
            at = k * protos + start
            weights_ref[:, at : at + chunk] = weights
            inverse = 1.0 / jnp.sum(weights, axis=0, keepdims=True)
            scale_ref[:, at : at + chunk] = jnp.broadcast_to(inverse, (8, chunk))
    weighted_rows(weights_ref, scale_ref, part_ref)
    sums_ref[...] = as_tile(part_ref[...])


def step_kernel(mine_ref, other_ref, weights_ref, sums_ref, row_ref, scale_ref, part_ref):
    all_rows = weights_ref.shape[0]
    row_ref[...] = as_column(inverse_rows(mine_ref[...] + other_ref[...], all_rows))
    column_scales(weights_ref, row_ref, scale_ref)
    weighted_rows(weights_ref, scale_ref, part_ref)
    sums_ref[...] = as_tile(part_ref[...])


def split(values):
    high = values.astype(jnp.bfloat16)
    low = (values - high.astype(jnp.float32)).astype(jnp.bfloat16)
    return jnp.concatenate([high, low], axis=0)


def exps_kernel(chunk, place_ref, near_ref, far_ref, *refs):
    *unit_refs, rows_ref, exps_ref, pull_ref, sums_ref, scratch, own_ref = refs
    all_rows = exps_ref.shape[0]
    protos = unit_refs[0].shape[0]
    first = pull_ref.shape[0]
    rows_ref[...] = place_rows(place_ref, near_ref, far_ref, 1, near_ref.shape[3] // 2, scratch)
    rows_all = rows_ref[...]
    part = jnp.zeros((all_rows, LANES), jnp.float32)
    pull = jnp.zeros((2 * first, pull_ref.shape[1]), jnp.float32)
    for k, unit_ref in enumerate(unit_refs):
        for start in range(0, protos, chunk):
            units = unit_ref[start : start + chunk, :]
            exps = jnp.exp(scores_of(rows_all, units) * (1 / student_temp))
            if k == 0:
                own_ref[:, start : start + chunk] = exps
            for at in range(0, chunk, LANES):
                part = part + exps[:, at : at + LANES]
            pull = pull + jnp.dot(split(exps[:first]), units, preferred_element_type=jnp.float32)
    own = exps_ref.shape[1]
    exps_ref[...] = own_ref[:, pl.ds(pl.multiple_of(place_ref[0] * own, own), own)]
    pull_ref[...] = pull[:first] + pull[first:]
    sums_ref[...] = as_tile(part)


def last_kernel(chunk, sum_x, place_ref, mine_ref, other_ref, weights_ref, *refs):
    *unit_refs, exp_pull_ref, exp_sums_ref, targets_ref, keep_ref, send_ref = refs[:-3]
    row_ref, scale_ref, part_ref = refs[-3:]
    all_rows = weights_ref.shape[0]
    first = exp_pull_ref.shape[0]
    protos = unit_refs[0].shape[0]
    row_ref[...] = as_column(inverse_rows(mine_ref[...] + other_ref[...], all_rows))
    column_scales(weights_ref, row_ref, scale_ref)
    weighted_rows(weights_ref, scale_ref, part_ref)
    sums = as_tile(part_ref[...])
    pull = jnp.zeros((2 * first, exp_pull_ref.shape[1]), jnp.float32)
    for k, unit_ref in enumerate(unit_refs):
        for start in range(0, protos, chunk):
            at = k * protos + start
            scaled = weights_ref[:first, at : at + chunk] * scale_ref[:1, at : at + chunk]
            pull = pull + jnp.dot(
                split(scaled), unit_ref[start : start + chunk, :], preferred_element_type=jnp.float32
            )
    own = pl.ds(pl.multiple_of(place_ref[0] * chunk, chunk), chunk)
    targets_ref[...] = weights_ref[:, own] * scale_ref[:1, own]
    half = first // 2
    upper = (place_ref[1] & X) > 0
    for k, pull in enumerate((pull[:first] + pull[first:], exp_pull_ref[...])):
        at = slice(k * half, (k + 1) * half)
        keep_ref[at, :] = jnp.where(upper, pull[half:], pull[:half])
        send_ref[at, :] = jnp.where(upper, pull[:half], pull[half:])
    for ref in (keep_ref, send_ref):
        ref[first:, :LANES] = exp_sums_ref[...]
        ref[first:, LANES:] = sums
    if not sum_x:
        send_ref[first:, LANES:] = jnp.zeros_like(sums)


def grads_kernel(
    place_ref,
    mine_ref,
    other_ref,
    targets_ref,
    exps_ref,
    rows_ref,
    feat_ref,
    proto_ref,
    student_out_ref,
    proto_out_ref,
):
    all_rows, own = targets_ref.shape
    rows = feat_ref.shape[0]
    total = mine_ref[...] + other_ref[...]
    first = total.shape[0] - 8
    target_scale = inverse_rows(total[first:, LANES:], all_rows) * (1 / student_temp)
    exp_scale = (1 / student_temp) / unpack_lanes(total[first:, :LANES], all_rows)
    exp_scale = as_column(jnp.where(target_scale > 0.0, exp_scale, 0.0))
    target_scale = as_column(target_scale)

    grad = exps_ref[...] * twice(exp_scale) - targets_ref[...] * twice(target_scale)
    pushed = lax.dot_general(
        grad.astype(jnp.bfloat16),
        rows_ref[...],
        (((0,), (0,)), ((), ())),
        preferred_element_type=jnp.float32,
    )
    unit, scale = quick_unit(proto_ref[pl.ds(pl.multiple_of(place_ref[0] * own, own), own), :])
    along = jnp.sum(unit * pushed, axis=1, keepdims=True)
    proto_out_ref[0] = (pushed - unit * along) * scale

    upper_x, upper_y = (place_ref[1] & X) > 0, (place_ref[1] & Y) > 0

    def own_rows(values):
        return jnp.where(upper_y, values[rows : 2 * rows], values[:rows])

    def own_scale(column):
        return own_rows(jnp.where(upper_x, column[2 * rows : 4 * rows], column[: 2 * rows]))

    half = first // 2
    pulled = own_rows(total[half:first]) * twice(own_scale(exp_scale))
    pulled = pulled - own_rows(total[:half]) * twice(own_scale(target_scale))
    unit, scale = quick_unit(feat_ref[...])
    student_out_ref[...] = (
        pulled - unit * jnp.sum(unit * pulled, axis=1, keepdims=True)
    ) * scale


def call(kernel, out_shape, operands, smem=0, scratch=(), work=0):
    vmem = pl.BlockSpec(memory_space=pltpu.VMEM)
    return pl.pallas_call(
        kernel,
        out_shape=out_shape,
        in_specs=[pl.BlockSpec(memory_space=pltpu.SMEM)] * smem + [vmem] * (len(operands) - smem),
        out_specs=jax.tree.map(lambda _: vmem, out_shape),
        scratch_shapes=scratch,
        compiler_params=pltpu.CompilerParams(vmem_limit_bytes=48 * 2**20),
        cost_estimate=pl.CostEstimate(
            flops=512 * work, bytes_accessed=4 * work, transcendentals=work
        ),
    )(*operands)


def swap(values, axis, distance):
    others = [(k, k ^ distance) for k in range(lax.axis_size(axis))]
    return lax.ppermute(values, axis, others)


def gather_rows(values):
    held = jnp.stack([values, swap(values, "proto", X)])
    held = jnp.stack([held] + [swap(held, "dp", t) for t in range(1, lax.axis_size("dp"))])
    held = jnp.stack([held, swap(held, "proto", Y)])
    return held, swap(held, "proto", CORE)


def share_units(units):
    return units, swap(units, "proto", CORE)


def row_totals(values):
    values = values + swap(values, "proto", X)
    return values, swap(values, "proto", Y)


def on_device_all_rows(student_feat, teacher_feat, prototypes, teacher_prototypes, live_count):
    n_dp, n_proto = lax.axis_size("dp"), lax.axis_size("proto")
    rows, width = student_feat.shape
    protos = prototypes.shape[0]
    own = protos // n_dp
    all_rows = n_dp * n_proto * rows
    first = 4 * rows
    f32 = functools.partial(jax.ShapeDtypeStruct, dtype=jnp.float32)
    bf16 = functools.partial(jax.ShapeDtypeStruct, dtype=jnp.bfloat16)
    place = jnp.stack([lax.axis_index("dp"), lax.axis_index("proto")]).astype(jnp.int32)
    place = jnp.concatenate([place, live_count])
    tile = f32((8, LANES))
    message = f32((first + 8, width))
    row_scratch = pltpu.VMEM((all_rows, width), jnp.float32)
    column = pltpu.VMEM((all_rows, LANES), jnp.float32)

    near, far = gather_rows(jnp.concatenate([teacher_feat, student_feat], axis=0))
    student_units, teacher_units = call(
        units_kernel,
        (bf16((protos, width)), bf16((protos, width))),
        (prototypes, teacher_prototypes),
        work=protos * width // 8,
    )
    teacher_units = share_units(teacher_units)
    student_units = share_units(student_units)
    held = len(teacher_units) * protos
    scale_row = pltpu.VMEM((8, held), jnp.float32)

    weights, sums = call(
        functools.partial(weights_kernel, own),
        (f32((all_rows, held)), tile),
        (place, near, far, *teacher_units),
        smem=1,
        scratch=[row_scratch, scale_row, column],
        work=held * all_rows,
    )
    near, far, sums = lax.optimization_barrier((near, far, sums))
    parts = row_totals(sums)
    student_rows, exps, exp_pull, exp_sums = call(
        functools.partial(exps_kernel, own),
        (bf16((all_rows, width)), f32((all_rows, own)), f32((first, width)), tile),
        (place, near, far, *student_units),
        smem=1,
        scratch=[row_scratch, pltpu.VMEM((all_rows, protos), jnp.float32)],
        work=len(student_units) * protos * all_rows,
    )
    for _ in range(ITERS - 2):
        sums = call(
            step_kernel,
            tile,
            (*parts, weights),
            scratch=[column, scale_row, column],
            work=held * all_rows // 2,
        )
        parts = row_totals(sums)
    targets, keep, send = call(
        functools.partial(last_kernel, own, True),
        (f32((all_rows, own)), message, message),
        (place, *parts, weights, *student_units, exp_pull, exp_sums),
        smem=1,
        scratch=[column, scale_row, column],
        work=held * all_rows // 2,
    )
    total = keep + swap(send, "proto", X)
    return call(
        grads_kernel,
        (f32((rows, width)), f32((1, own, width))),
        (
            place,
            total,
            swap(total, "proto", Y),
            targets,
            exps,
            student_rows,
            student_feat,
            prototypes,
        ),
        smem=1,
        work=own * all_rows,
    )


def sample_totals(values):
    return lax.psum(values, "proto")


def proto_totals(values):
    return lax.psum(values, "dp")


def on_device_group_rows(student_feat, teacher_feat, prototypes, teacher_prototypes, live_count):
    student_unit, student_length = unit_rows(student_feat)
    teacher_unit, teacher_length = unit_rows(teacher_feat)
    proto_unit, proto_length = unit_rows(prototypes)
    teacher_proto, teacher_proto_length = unit_rows(teacher_prototypes)
    proto_bf = proto_unit.astype(jnp.bfloat16)
    teacher_proto_bf = teacher_proto.astype(jnp.bfloat16)
    student_rows, teacher_rows = (
        lax.all_gather(student_unit.astype(jnp.bfloat16), "proto", axis=0, tiled=True),
        lax.all_gather(teacher_unit.astype(jnp.bfloat16), "proto", axis=0, tiled=True),
    )
    group_size = student_rows.shape[0]
    live_rows = live_count[lax.axis_index("dp")]
    live_mask = jnp.arange(group_size, dtype=jnp.int32) < live_rows
    live_column = live_mask[:, None]
    contract_last = (((1,), (1,)), ((), ()))
    logits = (
        lax.dot_general(student_rows, proto_bf, contract_last, preferred_element_type=jnp.float32)
        / student_temp
    )
    teacher_scores = (
        lax.dot_general(
            teacher_rows, teacher_proto_bf, contract_last, preferred_element_type=jnp.float32
        )
        / teacher_temp
    )
    weights = jnp.where(live_column, jnp.exp(teacher_scores), 0.0)
    partition = sample_totals(jnp.sum(jnp.exp(logits), axis=1))
    targets = weights
    for iteration in range(ITERS):
        targets = targets / proto_totals(jnp.sum(targets, axis=0))[None, :]
        row_sums = sample_totals(jnp.sum(targets, axis=1))
        targets = targets / jnp.where(live_mask, row_sums, 1.0)[:, None]
    student_probs = jnp.exp(logits - jnp.log(partition)[:, None])
    grad_block = jnp.where(live_column, (student_probs - targets) / student_temp, 0.0).astype(
        jnp.bfloat16
    )
    pulled = lax.psum_scatter(
        jnp.dot(grad_block, proto_bf, preferred_element_type=jnp.float32),
        "proto",
        scatter_dimension=0,
        tiled=True,
    )
    student_grad = (
        pulled - student_unit * jnp.sum(student_unit * pulled, axis=1, keepdims=True)
    ) / student_length
    own_protos = prototypes.shape[0] // lax.axis_size("dp")
    contract_first = (((0,), (0,)), ((), ()))
    pushed = lax.psum_scatter(
        lax.dot_general(
            grad_block, student_rows, contract_first, preferred_element_type=jnp.float32
        ),
        "dp",
        scatter_dimension=0,
        tiled=True,
    )
    first_proto = lax.axis_index("dp") * own_protos
    own_units = lax.dynamic_slice_in_dim(proto_unit, first_proto, own_protos, 0)
    own_lengths = lax.dynamic_slice_in_dim(proto_length, first_proto, own_protos, 0)
    proto_grad = (
        pushed - own_units * jnp.sum(own_units * pushed, axis=1, keepdims=True)
    ) / own_lengths
    return (student_grad, proto_grad[None])


def on_device(student_feat, teacher_feat, prototypes, teacher_prototypes, live_count):
    n_dp, n_proto = lax.axis_size("dp"), lax.axis_size("proto")
    rows, width = student_feat.shape
    protos = prototypes.shape[0]
    lanes = n_dp * n_proto * rows
    fits = (
        n_proto == 2 * Y
        and n_dp & (n_dp - 1) == 0
        and rows % 4 == 0
        and lanes % LANES == 0
        and lanes <= 8 * LANES
        and width == 2 * LANES
        and protos == n_dp * 2 * LANES
        and 4 * protos * lanes * 4 <= BLOCK_BYTES
    )
    plan = on_device_all_rows if fits else on_device_group_rows
    return plan(student_feat, teacher_feat, prototypes, teacher_prototypes, live_count)


def solution(mesh):
    return jax.shard_map(
        on_device,
        mesh=mesh,
        in_specs=(
            P(("dp", "proto"), None),
            P(("dp", "proto"), None),
            P("proto", None),
            P("proto", None),
            P(),
        ),
        out_specs=(P(("dp", "proto"), None), P("proto", "dp", None)),
        check_vma=False,
    )
```

```python
import functools

import jax
import jax.numpy as jnp
from jax import lax
from jax.experimental import pallas as pl
from jax.experimental.pallas import tpu as pltpu
from jax.sharding import PartitionSpec as P

ITERS = 3

student_temp = 0.1
teacher_temp = 0.07
eps_norm = 1e-06

LANES = 128
BLOCK_BYTES = 8 * 2**20


def unit_rows(values):
    widened = values.astype(jnp.float32)
    length = jnp.sqrt(jnp.sum(widened * widened, axis=1, keepdims=True) + eps_norm)
    return (widened / length, length)


CORE, X, Y = 1, 2, 4
X_CROSS, Y_CROSS = X | CORE, Y | CORE


def block_of(proto):
    return (proto & CORE) * 4 + (proto & X) + ((proto >> 2) & 1)


def quick_unit(values):
    widened = values.astype(jnp.float32)
    squares = jnp.sum(widened * widened, axis=1, keepdims=True) + eps_norm
    scale = lax.rsqrt(squares)
    return widened * scale, scale


def live_lanes(place_ref, lanes, n_dp, rows):
    lane = lax.broadcasted_iota(jnp.int32, (1, lanes), 1)
    live = jnp.zeros((1, lanes), jnp.float32)
    start = 0
    for t in range(n_dp):
        count = place_ref[2 + (place_ref[0] ^ t)]
        for c in range(2):
            for x in range(2):
                for y in range(2):
                    proto = CORE * c + X * x + Y * y
                    end = start + jnp.clip(count - proto * rows, 0, rows)
                    live = jnp.where((lane >= start) & (lane < end), 1.0, live)
                    start += rows
    return live


def pack_lanes(values):
    pieces = [values[:, k : k + LANES] for k in range(0, values.shape[1], LANES)]
    return jnp.concatenate(pieces + [jnp.zeros((8 - len(pieces), LANES), jnp.float32)], axis=0)


def unpack_lanes(tile, lanes):
    return jnp.concatenate([tile[k : k + 1, :] for k in range(lanes // LANES)], axis=1)


def as_column(values):
    return jnp.broadcast_to(values, (LANES, values.shape[1])).T


def as_tile(partial):
    return pack_lanes(jnp.sum(partial.T, axis=0, keepdims=True))


def inverse_rows(tile, rows):
    total = unpack_lanes(tile, rows)
    live = total > 0.0
    return jnp.where(live, 1.0 / jnp.where(live, total, 1.0), 0.0)


def units_kernel(place_ref, student_ref, teacher_ref, student_out_ref, teacher_out_ref, *scratch):
    del place_ref
    *held, sems = scratch
    copies = []
    for k, ref in enumerate((teacher_ref, student_ref)):
        copies.append(pltpu.make_async_copy(ref, held[k], sems.at[k]))
        copies[k].start()
    for k, out_ref in enumerate((teacher_out_ref, student_out_ref)):
        copies[k].wait()
        unit, _ = quick_unit(held[k][...])
        out_ref[...] = unit.astype(jnp.bfloat16)


def place_rows(place_ref, near_ref, far_ref, which, rows, scratch):
    mine_core, mine_x, mine_y = (place_ref[1] & 1, (place_ref[1] >> 1) & 1, (place_ref[1] >> 2) & 1)
    cut = slice(which * rows, (which + 1) * rows)
    for t in range(near_ref.shape[1]):
        for x in range(2):
            for y in range(2):
                rel_x, rel_y = mine_x ^ x, mine_y ^ y
                near = near_ref[rel_y, t, rel_x].astype(jnp.float32)[cut]
                far = far_ref[rel_y, t, rel_x].astype(jnp.float32)[cut]
                near_core = mine_core ^ rel_x ^ rel_y ^ (1 if t else 0)
                for c in range(2):
                    start = (t * 8 + block_of(CORE * c + X * x + Y * y)) * rows
                    scratch[start : start + rows, :] = jnp.where(near_core == c, near, far)
    unit, _ = quick_unit(scratch[...])
    return unit.astype(jnp.bfloat16)


def scores_of(rows_all, units):
    return lax.dot_general(
        rows_all, units, (((1,), (1,)), ((), ())), preferred_element_type=jnp.float32
    )


def twice(column):
    return jnp.concatenate([column, column], axis=1)


def weighted_rows(weights_ref, scale_ref, part_ref):
    tiles = weights_ref.shape[1] // LANES
    scales = [scale_ref[:, k * LANES : (k + 1) * LANES] for k in range(tiles)]

    def body(i, _):
        at = pl.ds(pl.multiple_of(i * 8, 8), 8)
        sums = [None] * 4
        for k in range(tiles):
            term = weights_ref[at, k * LANES : (k + 1) * LANES] * scales[k]
            sums[k % 4] = term if sums[k % 4] is None else sums[k % 4] + term
        part_ref[at, :] = (sums[0] + sums[1]) + (sums[2] + sums[3])
        return 0

    lax.fori_loop(0, weights_ref.shape[0] // 8, body, 0, unroll=4)


def column_scales(weights_ref, row_ref, scale_ref):
    tiles = weights_ref.shape[1] // LANES

    def body(i, sums):
        at = pl.ds(pl.multiple_of(i * 8, 8), 8)
        row = row_ref[at, :]
        return [
            total + weights_ref[at, k * LANES : (k + 1) * LANES] * row
            for k, total in enumerate(sums)
        ]

    zeros = [jnp.zeros((8, LANES), jnp.float32)] * tiles
    sums = lax.fori_loop(0, weights_ref.shape[0] // 8, body, zeros, unroll=4)
    for k, total in enumerate(sums):
        inverse = 1.0 / jnp.sum(total, axis=0, keepdims=True)
        scale_ref[:, k * LANES : (k + 1) * LANES] = jnp.broadcast_to(inverse, (8, LANES))


def weights_kernel(chunk, place_ref, near_ref, far_ref, *refs):
    *unit_refs, weights_ref, sums_ref, scratch, scale_ref, part_ref = refs
    all_rows = weights_ref.shape[0]
    protos = unit_refs[0].shape[0]
    rows = near_ref.shape[3] // 2
    rows_all = place_rows(place_ref, near_ref, far_ref, 0, rows, scratch)
    live = twice(as_column(live_lanes(place_ref, all_rows, near_ref.shape[1], rows)))
    for k, unit_ref in enumerate(unit_refs):
        for start in range(0, protos, chunk):
            scores = scores_of(rows_all, unit_ref[start : start + chunk, :])
            weights = jnp.exp(scores * (1 / teacher_temp)) * live
            at = k * protos + start
            weights_ref[:, at : at + chunk] = weights
            inverse = 1.0 / jnp.sum(weights, axis=0, keepdims=True)
            scale_ref[:, at : at + chunk] = jnp.broadcast_to(inverse, (8, chunk))
    weighted_rows(weights_ref, scale_ref, part_ref)
    sums_ref[...] = as_tile(part_ref[...])


def step_kernel(mine_ref, other_ref, weights_ref, sums_ref, row_ref, scale_ref, part_ref):
    all_rows = weights_ref.shape[0]
    row_ref[...] = as_column(inverse_rows(mine_ref[...] + other_ref[...], all_rows))
    column_scales(weights_ref, row_ref, scale_ref)
    weighted_rows(weights_ref, scale_ref, part_ref)
    sums_ref[...] = as_tile(part_ref[...])


def split(values):
    high = values.astype(jnp.bfloat16)
    low = (values - high.astype(jnp.float32)).astype(jnp.bfloat16)
    return jnp.concatenate([high, low], axis=0)


def exps_kernel(chunk, place_ref, near_ref, far_ref, *refs):
    *unit_refs, rows_ref, exps_ref, pull_ref, sums_ref, scratch, own_ref = refs
    all_rows = exps_ref.shape[0]
    protos = unit_refs[0].shape[0]
    first = pull_ref.shape[0]
    rows_ref[...] = place_rows(place_ref, near_ref, far_ref, 1, near_ref.shape[3] // 2, scratch)
    rows_all = rows_ref[...]
    part = jnp.zeros((all_rows, LANES), jnp.float32)
    pull = jnp.zeros((2 * first, pull_ref.shape[1]), jnp.float32)
    for k, unit_ref in enumerate(unit_refs):
        for start in range(0, protos, chunk):
            units = unit_ref[start : start + chunk, :]
            exps = jnp.exp(scores_of(rows_all, units) * (1 / student_temp))
            if k == 0:
                own_ref[:, start : start + chunk] = exps
            for at in range(0, chunk, LANES):
                part = part + exps[:, at : at + LANES]
            pull = pull + jnp.dot(split(exps[:first]), units, preferred_element_type=jnp.float32)
    own = exps_ref.shape[1]
    exps_ref[...] = own_ref[:, pl.ds(pl.multiple_of(place_ref[0] * own, own), own)]
    pull_ref[...] = pull[:first] + pull[first:]
    sums_ref[...] = as_tile(part)


def last_kernel(chunk, rows, place_ref, mine_ref, other_ref, weights_ref, *refs):
    *unit_refs, exp_pull_ref, exp_sums_ref, targets_ref, keep_ref, send_ref = refs[:-4]
    row_ref, scale_ref, part_ref, blocks_ref = refs[-4:]
    all_rows = weights_ref.shape[0]
    first = exp_pull_ref.shape[0]
    protos = unit_refs[0].shape[0]
    row_ref[...] = as_column(inverse_rows(mine_ref[...] + other_ref[...], all_rows))
    column_scales(weights_ref, row_ref, scale_ref)
    weighted_rows(weights_ref, scale_ref, part_ref)
    sums = as_tile(part_ref[...])
    pull = jnp.zeros((2 * first, exp_pull_ref.shape[1]), jnp.float32)
    for k, unit_ref in enumerate(unit_refs):
        for start in range(0, protos, chunk):
            at = k * protos + start
            scaled = weights_ref[:first, at : at + chunk] * scale_ref[:1, at : at + chunk]
            pull = pull + jnp.dot(
                split(scaled), unit_ref[start : start + chunk, :], preferred_element_type=jnp.float32
            )
    own = pl.ds(pl.multiple_of(place_ref[0] * chunk, chunk), chunk)
    targets_ref[...] = weights_ref[:, own] * scale_ref[:1, own]
    pulls = (pull[:first] + pull[first:], exp_pull_ref[...])
    for k, pull in enumerate(pulls):
        for block in range(first // rows):
            blocks_ref[k, block, :rows, :] = pull[block * rows : (block + 1) * rows]
    mine = place_ref[1]
    for ref, proto in ((keep_ref, mine), (send_ref, mine ^ X_CROSS)):
        for j, owner in enumerate((proto, proto ^ Y_CROSS)):
            for k in range(2):
                start = (2 * j + k) * rows
                ref[start : start + rows, :] = blocks_ref[k, block_of(owner), :rows, :]
        ref[4 * rows :, :LANES] = exp_sums_ref[...]
        ref[4 * rows :, LANES:] = sums


def grads_kernel(
    place_ref,
    mine_ref,
    other_ref,
    targets_ref,
    exps_ref,
    rows_ref,
    feat_ref,
    proto_ref,
    student_out_ref,
    proto_out_ref,
):
    all_rows, own = targets_ref.shape
    rows = feat_ref.shape[0]
    sums = mine_ref[4 * rows :, :] + other_ref[2 * rows :, :]
    target_scale = inverse_rows(sums[:, LANES:], all_rows) * (1 / student_temp)
    exp_scale = (1 / student_temp) / unpack_lanes(sums[:, :LANES], all_rows)
    exp_scale = as_column(jnp.where(target_scale > 0.0, exp_scale, 0.0))
    target_scale = as_column(target_scale)

    grad = exps_ref[...] * twice(exp_scale) - targets_ref[...] * twice(target_scale)
    pushed = lax.dot_general(
        grad.astype(jnp.bfloat16),
        rows_ref[...],
        (((0,), (0,)), ((), ())),
        preferred_element_type=jnp.float32,
    )
    unit, scale = quick_unit(proto_ref[pl.ds(pl.multiple_of(place_ref[0] * own, own), own), :])
    along = jnp.sum(unit * pushed, axis=1, keepdims=True)
    proto_out_ref[0] = (pushed - unit * along) * scale

    def own_scale(column):
        block = block_of(place_ref[1])
        scale = column[:rows]
        for k in range(1, 8):
            scale = jnp.where(block == k, column[k * rows : (k + 1) * rows], scale)
        return twice(scale)

    target_pull, exp_pull = [
        mine_ref[k * rows : (k + 1) * rows, :] + other_ref[k * rows : (k + 1) * rows, :]
        for k in range(2)
    ]
    pulled = exp_pull * own_scale(exp_scale) - target_pull * own_scale(target_scale)
    unit, scale = quick_unit(feat_ref[...])
    student_out_ref[...] = (
        pulled - unit * jnp.sum(unit * pulled, axis=1, keepdims=True)
    ) * scale


def call(kernel, out_shape, operands, smem=0, scratch=(), work=0, space=pltpu.VMEM):
    vmem = pl.BlockSpec(memory_space=pltpu.VMEM)
    rest = pl.BlockSpec(memory_space=space)
    return pl.pallas_call(
        kernel,
        out_shape=out_shape,
        in_specs=[pl.BlockSpec(memory_space=pltpu.SMEM)] * smem + [rest] * (len(operands) - smem),
        out_specs=jax.tree.map(lambda _: vmem, out_shape),
        scratch_shapes=scratch,
        compiler_params=pltpu.CompilerParams(vmem_limit_bytes=48 * 2**20),
        cost_estimate=pl.CostEstimate(
            flops=512 * work, bytes_accessed=4 * work, transcendentals=work
        ),
    )(*operands)


def swap(values, axis, distance):
    others = [(k, k ^ distance) for k in range(lax.axis_size(axis))]
    return lax.ppermute(values, axis, others)


def swap_dp(values, t):
    n_dp, n_proto = lax.axis_size("dp"), lax.axis_size("proto")
    others = [
        (d * n_proto + p, (d ^ t) * n_proto + (p ^ CORE)) for d in range(n_dp) for p in range(n_proto)
    ]
    return lax.ppermute(values, ("dp", "proto"), others)


def gather_rows(values, units):
    held = jnp.stack([values, swap(values, "proto", X_CROSS)])
    held, *operands = lax.optimization_barrier((held, *units[1]))
    units = units[0](*operands)
    held = jnp.stack([held] + [swap_dp(held, t) for t in range(1, lax.axis_size("dp"))])
    held = jnp.stack([held, swap(held, "proto", Y_CROSS)])
    held, *units = lax.optimization_barrier((held, *units))
    return held, swap(held, "proto", CORE), *((unit, swap(unit, "proto", CORE)) for unit in units)


def row_totals(values):
    values = values + swap(values, "proto", X_CROSS)
    return values, swap(values, "proto", Y_CROSS)


def on_device_all_rows(student_feat, teacher_feat, prototypes, teacher_prototypes, live_count):
    n_dp, n_proto = lax.axis_size("dp"), lax.axis_size("proto")
    rows, width = student_feat.shape
    protos = prototypes.shape[0]
    own = protos // n_dp
    all_rows = n_dp * n_proto * rows
    first = n_proto * rows
    f32 = functools.partial(jax.ShapeDtypeStruct, dtype=jnp.float32)
    bf16 = functools.partial(jax.ShapeDtypeStruct, dtype=jnp.bfloat16)
    place = jnp.stack([lax.axis_index("dp"), lax.axis_index("proto")]).astype(jnp.int32)
    place = jnp.concatenate([place, live_count])
    tile = f32((8, LANES))
    message = f32((4 * rows + 8, width))
    row_scratch = pltpu.VMEM((all_rows, width), jnp.float32)
    column = pltpu.VMEM((all_rows, LANES), jnp.float32)

    units = functools.partial(
        call,
        units_kernel,
        (bf16((protos, width)), bf16((protos, width))),
        smem=1,
        scratch=[pltpu.VMEM((protos, width), jnp.bfloat16)] * 2 + [pltpu.SemaphoreType.DMA((2,))],
        work=protos * width // 8,
        space=pltpu.HBM,
    )
    near, far, student_units, teacher_units = gather_rows(
        jnp.concatenate([teacher_feat, student_feat], axis=0),
        (lambda *operands: units(operands), (place, prototypes, teacher_prototypes)),
    )
    held = len(teacher_units) * protos
    scale_row = pltpu.VMEM((8, held), jnp.float32)

    weights, sums = call(
        functools.partial(weights_kernel, own),
        (f32((all_rows, held)), tile),
        (place, near, far, *teacher_units),
        smem=1,
        scratch=[row_scratch, scale_row, column],
        work=held * all_rows,
    )
    near, far, sums = lax.optimization_barrier((near, far, sums))
    parts = row_totals(sums)
    student_rows, exps, exp_pull, exp_sums = call(
        functools.partial(exps_kernel, own),
        (bf16((all_rows, width)), f32((all_rows, own)), f32((first, width)), tile),
        (place, near, far, *student_units),
        smem=1,
        scratch=[row_scratch, pltpu.VMEM((all_rows, protos), jnp.float32)],
        work=len(student_units) * protos * all_rows,
    )
    for _ in range(ITERS - 2):
        sums = call(
            step_kernel,
            tile,
            (*parts, weights),
            scratch=[column, scale_row, column],
            work=held * all_rows // 2,
        )
        parts = row_totals(sums)
    targets, keep, send = call(
        functools.partial(last_kernel, own, rows),
        (f32((all_rows, own)), message, message),
        (place, *parts, weights, *student_units, exp_pull, exp_sums),
        smem=1,
        scratch=[column, scale_row, column, pltpu.VMEM((2, n_proto, 16, width), jnp.float32)],
        work=held * all_rows // 2,
    )
    total = keep + swap(send, "proto", X_CROSS)
    return call(
        grads_kernel,
        (f32((rows, width)), f32((1, own, width))),
        (
            place,
            total,
            swap(total[2 * rows :], "proto", Y_CROSS),
            targets,
            exps,
            student_rows,
            student_feat,
            prototypes,
        ),
        smem=1,
        work=own * all_rows,
    )


def sample_totals(values):
    return lax.psum(values, "proto")


def proto_totals(values):
    return lax.psum(values, "dp")


def on_device_group_rows(student_feat, teacher_feat, prototypes, teacher_prototypes, live_count):
    student_unit, student_length = unit_rows(student_feat)
    teacher_unit, teacher_length = unit_rows(teacher_feat)
    proto_unit, proto_length = unit_rows(prototypes)
    teacher_proto, teacher_proto_length = unit_rows(teacher_prototypes)
    proto_bf = proto_unit.astype(jnp.bfloat16)
    teacher_proto_bf = teacher_proto.astype(jnp.bfloat16)
    student_rows, teacher_rows = (
        lax.all_gather(student_unit.astype(jnp.bfloat16), "proto", axis=0, tiled=True),
        lax.all_gather(teacher_unit.astype(jnp.bfloat16), "proto", axis=0, tiled=True),
    )
    group_size = student_rows.shape[0]
    live_rows = live_count[lax.axis_index("dp")]
    live_mask = jnp.arange(group_size, dtype=jnp.int32) < live_rows
    live_column = live_mask[:, None]
    contract_last = (((1,), (1,)), ((), ()))
    logits = (
        lax.dot_general(student_rows, proto_bf, contract_last, preferred_element_type=jnp.float32)
        / student_temp
    )
    teacher_scores = (
        lax.dot_general(
            teacher_rows, teacher_proto_bf, contract_last, preferred_element_type=jnp.float32
        )
        / teacher_temp
    )
    weights = jnp.where(live_column, jnp.exp(teacher_scores), 0.0)
    partition = sample_totals(jnp.sum(jnp.exp(logits), axis=1))
    targets = weights
    for iteration in range(ITERS):
        targets = targets / proto_totals(jnp.sum(targets, axis=0))[None, :]
        row_sums = sample_totals(jnp.sum(targets, axis=1))
        targets = targets / jnp.where(live_mask, row_sums, 1.0)[:, None]
    student_probs = jnp.exp(logits - jnp.log(partition)[:, None])
    grad_block = jnp.where(live_column, (student_probs - targets) / student_temp, 0.0).astype(
        jnp.bfloat16
    )
    pulled = lax.psum_scatter(
        jnp.dot(grad_block, proto_bf, preferred_element_type=jnp.float32),
        "proto",
        scatter_dimension=0,
        tiled=True,
    )
    student_grad = (
        pulled - student_unit * jnp.sum(student_unit * pulled, axis=1, keepdims=True)
    ) / student_length
    own_protos = prototypes.shape[0] // lax.axis_size("dp")
    contract_first = (((0,), (0,)), ((), ()))
    pushed = lax.psum_scatter(
        lax.dot_general(
            grad_block, student_rows, contract_first, preferred_element_type=jnp.float32
        ),
        "dp",
        scatter_dimension=0,
        tiled=True,
    )
    first_proto = lax.axis_index("dp") * own_protos
    own_units = lax.dynamic_slice_in_dim(proto_unit, first_proto, own_protos, 0)
    own_lengths = lax.dynamic_slice_in_dim(proto_length, first_proto, own_protos, 0)
    proto_grad = (
        pushed - own_units * jnp.sum(own_units * pushed, axis=1, keepdims=True)
    ) / own_lengths
    return (student_grad, proto_grad[None])


def on_device(student_feat, teacher_feat, prototypes, teacher_prototypes, live_count):
    n_dp, n_proto = lax.axis_size("dp"), lax.axis_size("proto")
    rows, width = student_feat.shape
    protos = prototypes.shape[0]
    lanes = n_dp * n_proto * rows
    fits = (
        n_proto == 2 * Y
        and n_dp & (n_dp - 1) == 0
        and rows % 4 == 0
        and rows <= 16
        and lanes % LANES == 0
        and lanes <= 8 * LANES
        and width == 2 * LANES
        and protos == n_dp * 2 * LANES
        and 4 * protos * lanes * 4 <= BLOCK_BYTES
    )
    plan = on_device_all_rows if fits else on_device_group_rows
    return plan(student_feat, teacher_feat, prototypes, teacher_prototypes, live_count)


def solution(mesh):
    return jax.shard_map(
        on_device,
        mesh=mesh,
        in_specs=(
            P(("dp", "proto"), None),
            P(("dp", "proto"), None),
            P("proto", None),
            P("proto", None),
            P(),
        ),
        out_specs=(P(("dp", "proto"), None), P("proto", "dp", None)),
        check_vma=False,
    )
```

```python
import functools

import jax
import jax.numpy as jnp
from jax import lax
from jax.experimental import pallas as pl
from jax.experimental.pallas import tpu as pltpu
from jax.sharding import PartitionSpec as P

ITERS = 3

student_temp = 0.1
teacher_temp = 0.07
eps_norm = 1e-06

LANES = 128
BLOCK_BYTES = 8 * 2**20


def unit_rows(values):
    widened = values.astype(jnp.float32)
    length = jnp.sqrt(jnp.sum(widened * widened, axis=1, keepdims=True) + eps_norm)
    return (widened / length, length)


CORE, X, Y = 1, 2, 4
X_CROSS, Y_CROSS = X | CORE, Y | CORE


def block_of(proto):
    return (proto & X) + ((proto >> 2) & 1)


def quick_unit(values):
    widened = values.astype(jnp.float32)
    squares = jnp.sum(widened * widened, axis=1, keepdims=True) + eps_norm
    scale = lax.rsqrt(squares)
    return widened * scale, scale


def dp_order(n_dp):
    return [0, *reversed(range(1, n_dp))]


def live_lanes(place_ref, half, lanes, n_dp, rows):
    mine = place_ref[1]
    parity = (mine ^ (mine >> 1) ^ (mine >> 2)) & 1
    lane = lax.broadcasted_iota(jnp.int32, (1, lanes), 1)
    live = jnp.zeros((1, lanes), jnp.float32)
    start = 0
    for t in dp_order(n_dp):
        count = place_ref[2 + (place_ref[0] ^ t)]
        for x in range(2):
            for y in range(2):
                core = parity ^ x ^ y ^ half ^ (1 if t else 0)
                proto = core + X * x + Y * y
                end = start + jnp.clip(count - proto * rows, 0, rows)
                live = jnp.where((lane >= start) & (lane < end), 1.0, live)
                start += rows
    return live


def pack_lanes(values):
    pieces = [values[:, k : k + LANES] for k in range(0, values.shape[1], LANES)]
    return jnp.concatenate(pieces + [jnp.zeros((8 - len(pieces), LANES), jnp.float32)], axis=0)


def unpack_lanes(tile, lanes):
    return jnp.concatenate([tile[k : k + 1, :] for k in range(lanes // LANES)], axis=1)


def as_column(values):
    return jnp.broadcast_to(values, (LANES, values.shape[1])).T


def as_tile(partial):
    return pack_lanes(jnp.sum(partial.T, axis=0, keepdims=True))


def inverse_rows(tile, rows):
    total = unpack_lanes(tile, rows)
    live = total > 0.0
    return jnp.where(live, 1.0 / jnp.where(live, total, 1.0), 0.0)


def place_rows(place_ref, ref, which, rows, scratch):
    mine_x, mine_y = (place_ref[1] >> 1) & 1, (place_ref[1] >> 2) & 1
    start = 0
    for t in range(ref.shape[1]):
        for x in range(2):
            for y in range(2):
                block = ref[mine_y ^ y, t, mine_x ^ x].astype(jnp.float32)
                scratch[start : start + rows, :] = block[which * rows : (which + 1) * rows]
                start += rows
    unit, _ = quick_unit(scratch[...])
    return unit.astype(jnp.bfloat16)


def scores_of(rows_all, units):
    return lax.dot_general(
        rows_all, units, (((1,), (1,)), ((), ())), preferred_element_type=jnp.float32
    )


def twice(column):
    return jnp.concatenate([column, column], axis=1)


def weighted_rows(panels, left, scale_ref, part_ref, add=False):
    tiles = panels[0].shape[1] // LANES
    scales = [scale_ref[:, left + k * LANES : left + (k + 1) * LANES] for k in range(tiles)]
    top = 0
    for ref in panels:

        def body(i, _, ref=ref, top=top):
            at = pl.ds(pl.multiple_of(i * 8, 8), 8)
            to = pl.ds(pl.multiple_of(i * 8 + top, 8), 8)
            sums = [None] * 4
            for k in range(tiles):
                term = ref[at, k * LANES : (k + 1) * LANES] * scales[k]
                sums[k % 4] = term if sums[k % 4] is None else sums[k % 4] + term
            total = (sums[0] + sums[1]) + (sums[2] + sums[3])
            part_ref[to, :] = part_ref[to, :] + total if add else total
            return 0

        lax.fori_loop(0, ref.shape[0] // 8, body, 0, unroll=4)
        top += ref.shape[0]


def column_scales(panels, left, row_ref, scale_ref):
    tiles = panels[0].shape[1] // LANES
    sums = [jnp.zeros((8, LANES), jnp.float32)] * tiles
    top = 0
    for ref in panels:

        def body(i, sums, ref=ref, top=top):
            at = pl.ds(pl.multiple_of(i * 8, 8), 8)
            row = row_ref[pl.ds(pl.multiple_of(i * 8 + top, 8), 8), :]
            return [
                total + ref[at, k * LANES : (k + 1) * LANES] * row for k, total in enumerate(sums)
            ]

        sums = lax.fori_loop(0, ref.shape[0] // 8, body, sums, unroll=4)
        top += ref.shape[0]
    for k, total in enumerate(sums):
        inverse = 1.0 / jnp.sum(total, axis=0, keepdims=True)
        at = slice(left + k * LANES, left + (k + 1) * LANES)
        scale_ref[:, at] = jnp.broadcast_to(inverse, (8, LANES))


def weights_of(rows, units, live):
    weights = jnp.exp(scores_of(rows, units) * (1 / teacher_temp)) * live
    return weights, fold(weights)


def fold(values):
    return jnp.sum(values.reshape(values.shape[0] // 8, 8, values.shape[1]), axis=0)


def units_kernel(proto_ref, units_ref):
    units_ref[...] = quick_unit(proto_ref[...])[0].astype(jnp.bfloat16)


def near_kernel(chunk, place_ref, near_ref, *refs):
    *unit_refs, weights_ref, sums_ref, rows_ref, scratch = refs
    half = rows_ref.shape[0]
    rows = near_ref.shape[3] // 2
    protos = unit_refs[0].shape[0]
    rows_near = place_rows(place_ref, near_ref, 0, rows, scratch)
    rows_ref[...] = rows_near
    live = twice(as_column(live_lanes(place_ref, 0, half, near_ref.shape[1], rows)))
    for k, unit_ref in enumerate(unit_refs):
        for start in range(0, protos, chunk):
            at = slice(k * protos + start, k * protos + start + chunk)
            weights_ref[:, at], sums_ref[:, at] = weights_of(
                rows_near, unit_ref[start : start + chunk, :], live
            )


def far_kernel(chunk, place_ref, far_ref, near_rows_ref, near_weights_ref, near_sums_ref, *refs):
    *unit_refs, weights_ref, rows_ref, live_ref, sums_ref, scratch, scale_ref, part_ref = refs
    half = near_rows_ref.shape[0]
    rows = far_ref.shape[3] // 2
    protos = unit_refs[0].shape[0]
    rows_far = place_rows(place_ref, far_ref, 0, rows, scratch)
    rows_ref[:half, :] = near_rows_ref[...]
    rows_ref[half:, :] = rows_far
    live = as_column(live_lanes(place_ref, 1, half, far_ref.shape[1], rows))
    live_ref[half:, :] = live
    for k, unit_ref in enumerate(unit_refs):
        for start in range(0, protos, chunk):
            at = slice(k * protos + start, k * protos + start + chunk)
            weights, sums = weights_of(rows_far, unit_ref[start : start + chunk, :], twice(live))
            weights_ref[:, at] = weights
            inverse = 1.0 / jnp.sum(near_sums_ref[:, at] + sums, axis=0, keepdims=True)
            scale_ref[:, at] = jnp.broadcast_to(inverse, (8, chunk))
    weighted_rows([near_weights_ref, weights_ref], 0, scale_ref, part_ref)
    sums_ref[...] = as_tile(part_ref[...])
    live_ref[:half, :] = as_column(live_lanes(place_ref, 0, half, far_ref.shape[1], rows))


def across_kernel(chunk, rows_ref, live_ref, *refs):
    *proto_refs, weights_ref = refs
    protos = proto_refs[0].shape[0]
    rows_all = rows_ref[...]
    live = twice(live_ref[...])
    for k, proto_ref in enumerate(proto_refs):
        for start in range(0, protos, chunk):
            units = quick_unit(proto_ref[start : start + chunk, :])[0].astype(jnp.bfloat16)
            at = slice(k * protos + start, k * protos + start + chunk)
            weights_ref[:, at], _ = weights_of(rows_all, units, live)


def sweep(sums, near_ref, far_ref, across_ref, row_ref, scale_ref, part_ref):
    held = near_ref.shape[1]
    row_ref[...] = as_column(inverse_rows(sums, row_ref.shape[0]))
    own = [near_ref, far_ref]
    column_scales(own, 0, row_ref, scale_ref)
    column_scales([across_ref], held, row_ref, scale_ref)
    weighted_rows(own, 0, scale_ref, part_ref)
    weighted_rows([across_ref], held, scale_ref, part_ref, add=True)
    return as_tile(part_ref[...])


def step_kernel(mine_ref, other_ref, near_ref, far_ref, across_ref, sums_ref, *scratch):
    sums_ref[...] = sweep(mine_ref[...] + other_ref[...], near_ref, far_ref, across_ref, *scratch)


def split(values):
    high = values.astype(jnp.bfloat16)
    low = (values - high.astype(jnp.float32)).astype(jnp.bfloat16)
    return jnp.concatenate([high, low], axis=0)


def exps_kernel(chunk, place_ref, near_ref, far_ref, *refs):
    *proto_refs, rows_ref, units_ref, pull_ref, sums_ref, scratch, exps_ref = refs
    all_rows, half = rows_ref.shape[0], rows_ref.shape[0] // 2
    protos = proto_refs[0].shape[0]
    first = pull_ref.shape[0]
    for k, ref in enumerate((near_ref, far_ref)):
        rows_half = place_rows(place_ref, ref, 1, ref.shape[3] // 2, scratch)
        rows_ref[k * half : (k + 1) * half, :] = rows_half
    rows_all = rows_ref[...]
    part = jnp.zeros((all_rows, LANES), jnp.float32)
    pull = jnp.zeros((2 * first, pull_ref.shape[1]), jnp.float32)
    for k, proto_ref in enumerate(proto_refs):
        for start in range(0, protos, chunk):
            units = quick_unit(proto_ref[start : start + chunk, :])[0].astype(jnp.bfloat16)
            units_ref[k * protos + start : k * protos + start + chunk, :] = units
            exps_ref[...] = jnp.exp(scores_of(rows_all, units) * (1 / student_temp))
            for at in range(0, chunk, LANES):
                part = part + exps_ref[:, at : at + LANES]
            exps = split(exps_ref[:first, :])
            pull = pull + jnp.dot(exps, units, preferred_element_type=jnp.float32)
    pull_ref[...] = pull[:first] + pull[first:]
    sums_ref[...] = as_tile(part)


def last_kernel(chunk, rows, place_ref, mine_ref, other_ref, near_ref, far_ref, across_ref, *refs):
    units_ref, exp_pull_ref, exp_sums_ref, keep_ref, send_ref, *scratch, blocks_ref = refs
    scale_ref = scratch[1]
    first = exp_pull_ref.shape[0]
    sums = sweep(mine_ref[...] + other_ref[...], near_ref, far_ref, across_ref, *scratch)
    pull = jnp.zeros((2 * first, exp_pull_ref.shape[1]), jnp.float32)
    for start in range(0, units_ref.shape[0], chunk):
        at = slice(start, start + chunk)
        scaled = split(near_ref[:first, at] * scale_ref[:1, at])
        pull = pull + jnp.dot(scaled, units_ref[at, :], preferred_element_type=jnp.float32)
    pulls = (pull[:first] + pull[first:], exp_pull_ref[...])
    for k, pull in enumerate(pulls):
        for block in range(4):
            blocks_ref[k, block, :rows, :] = pull[block * rows : (block + 1) * rows]
    mine = place_ref[1]
    for ref, proto in ((keep_ref, mine), (send_ref, mine ^ X)):
        for j, owner in enumerate((proto, proto ^ Y)):
            for k in range(2):
                start = (2 * j + k) * rows
                ref[start : start + rows, :] = blocks_ref[k, block_of(owner), :rows, :]
        ref[4 * rows :, :LANES] = exp_sums_ref[...]
    keep_ref[4 * rows :, LANES:] = sums
    send_ref[4 * rows :, LANES:] = jnp.zeros_like(sums)


def own_kernel(place_ref, mine_ref, other_ref, teacher_rows_ref, student_rows_ref, *refs):
    teacher_proto_ref, proto_ref, targets_ref, exps_ref, unit_ref, scale_ref = refs
    own, all_rows = targets_ref.shape
    row_scale = inverse_rows(mine_ref[...] + other_ref[...], all_rows)
    live = jnp.where(row_scale > 0.0, 1.0, 0.0)
    first = pl.ds(pl.multiple_of(place_ref[0] * own, own), own)
    units = quick_unit(teacher_proto_ref[first, :])[0].astype(jnp.bfloat16)
    weights = jnp.exp(scores_of(units, teacher_rows_ref[...]) * (1 / teacher_temp)) * live
    inverse = 1.0 / jnp.sum(weights * row_scale, axis=1, keepdims=True)
    targets_ref[...] = weights * (inverse * (1 / student_temp))
    unit, scale = quick_unit(proto_ref[first, :])
    unit_ref[...] = unit
    scale_ref[...] = jnp.broadcast_to(scale, scale_ref.shape)
    units = unit.astype(jnp.bfloat16)
    exps = jnp.exp(scores_of(units, student_rows_ref[...]) * (1 / student_temp))
    exps_ref[...] = exps * (1 / student_temp)


def grads_kernel(place_ref, mine_ref, other_ref, targets_ref, exps_ref, unit_ref, *refs):
    scale_ref, rows_ref, feat_ref, student_out_ref, proto_out_ref = refs
    all_rows = targets_ref.shape[1]
    rows = feat_ref.shape[0]
    sums = mine_ref[4 * rows :, :] + other_ref[2 * rows :, :]
    target_scale = inverse_rows(sums[:, LANES:], all_rows)
    exp_scale = jnp.where(target_scale > 0.0, 1.0 / unpack_lanes(sums[:, :LANES], all_rows), 0.0)

    grad = exps_ref[...] * exp_scale - targets_ref[...] * target_scale
    pushed = jnp.dot(grad.astype(jnp.bfloat16), rows_ref[...], preferred_element_type=jnp.float32)
    unit = unit_ref[...]
    along = jnp.sum(unit * pushed, axis=1, keepdims=True)
    proto_out_ref[0] = (pushed - unit * along) * twice(scale_ref[...])

    row = lax.broadcasted_iota(jnp.int32, (rows, LANES), 0) + block_of(place_ref[1]) * rows
    here = lax.broadcasted_iota(jnp.int32, (rows, LANES), 1) == row
    target_column, exp_column = [
        jnp.sum(jnp.where(here, scale[:, :LANES], 0.0), axis=1, keepdims=True) * (1 / student_temp)
        for scale in (target_scale, exp_scale)
    ]
    target_pull, exp_pull = [
        mine_ref[k * rows : (k + 1) * rows, :] + other_ref[k * rows : (k + 1) * rows, :]
        for k in range(2)
    ]
    pulled = exp_pull * exp_column - target_pull * target_column
    unit, scale = quick_unit(feat_ref[...])
    student_out_ref[...] = (
        pulled - unit * jnp.sum(unit * pulled, axis=1, keepdims=True)
    ) * scale


def call(kernel, out_shape, operands, smem=0, scratch=(), work=0):
    vmem = pl.BlockSpec(memory_space=pltpu.VMEM)
    return pl.pallas_call(
        kernel,
        out_shape=out_shape,
        in_specs=[pl.BlockSpec(memory_space=pltpu.SMEM)] * smem + [vmem] * (len(operands) - smem),
        out_specs=jax.tree.map(lambda _: vmem, out_shape),
        scratch_shapes=scratch,
        compiler_params=pltpu.CompilerParams(vmem_limit_bytes=24 * 2**20),
        cost_estimate=pl.CostEstimate(
            flops=512 * work, bytes_accessed=4 * work, transcendentals=work
        ),
    )(*operands)


def swap(values, axis, distance):
    others = [(k, k ^ distance) for k in range(lax.axis_size(axis))]
    return lax.ppermute(values, axis, others)


def swap_dp(values, t):
    n_dp, n_proto = lax.axis_size("dp"), lax.axis_size("proto")
    others = [
        (d * n_proto + p, (d ^ t) * n_proto + (p ^ CORE)) for d in range(n_dp) for p in range(n_proto)
    ]
    return lax.ppermute(values, ("dp", "proto"), others)


def on_device_all_rows(student_feat, teacher_feat, prototypes, teacher_prototypes, live_count):
    n_dp, n_proto = lax.axis_size("dp"), lax.axis_size("proto")
    rows, width = student_feat.shape
    protos = prototypes.shape[0]
    own = protos // n_dp
    all_rows = n_dp * n_proto * rows
    half = all_rows // 2
    first = 4 * rows
    held = 2 * protos
    f32 = functools.partial(jax.ShapeDtypeStruct, dtype=jnp.float32)
    bf16 = functools.partial(jax.ShapeDtypeStruct, dtype=jnp.bfloat16)
    place = jnp.stack([lax.axis_index("dp"), lax.axis_index("proto")]).astype(jnp.int32)
    place = jnp.concatenate([place, live_count])
    tile = f32((8, LANES))
    message = f32((4 * rows + 8, width))
    row_scratch = pltpu.VMEM((half, width), jnp.float32)
    column = pltpu.VMEM((all_rows, LANES), jnp.float32)
    scale_row = pltpu.VMEM((8, held), jnp.float32)
    sweep_scratch = [column, pltpu.VMEM((8, 2 * held), jnp.float32), column]

    both = lax.optimization_barrier(jnp.concatenate([teacher_feat, student_feat], axis=0))
    across_x = swap(both, "proto", X_CROSS)
    across_x, own_protos, place = lax.optimization_barrier((across_x, teacher_prototypes, place))
    across_protos = swap(own_protos, "proto", X_CROSS)
    student_protos = (prototypes, swap(prototypes, "proto", CORE))
    near = jnp.stack([both, across_x])
    teacher_units = call(units_kernel, bf16((protos, width)), (own_protos,), work=protos * width)
    teacher_units = (teacher_units, swap(teacher_units, "proto", CORE))
    near = jnp.stack([near] + [swap_dp(near, t) for t in dp_order(n_dp)[1:]])
    near = jnp.stack([near, swap(near, "proto", Y_CROSS)])
    far = swap(near, "proto", CORE)

    near_weights, near_sums, near_rows = call(
        functools.partial(near_kernel, own),
        (f32((half, held)), f32((8, held)), bf16((half, width))),
        (place, near, *teacher_units),
        smem=1,
        scratch=[row_scratch],
        work=held * half,
    )
    far_weights, teacher_rows, live, sums = call(
        functools.partial(far_kernel, own),
        (f32((half, held)), bf16((all_rows, width)), f32((all_rows, LANES)), tile),
        (place, far, near_rows, near_weights, near_sums, *teacher_units),
        smem=1,
        scratch=[row_scratch, scale_row, column],
        work=held * half,
    )
    sums = sums + swap(sums, "proto", Y_CROSS)
    sums, across_protos = lax.optimization_barrier((sums, across_protos))
    parts = (sums, swap(sums, "proto", X_CROSS))
    across_weights = call(
        functools.partial(across_kernel, own),
        f32((all_rows, held)),
        (teacher_rows, live, across_protos, swap(across_protos, "proto", CORE)),
        work=held * all_rows,
    )
    weights = (near_weights, far_weights, across_weights)
    for _ in range(ITERS - 2):
        sums = call(
            step_kernel,
            tile,
            (*parts, *weights),
            scratch=sweep_scratch,
            work=held * all_rows,
        )
        sums, near, far, *student_protos = lax.optimization_barrier(
            (sums, near, far, *student_protos)
        )
        parts = (sums, swap(sums, "proto", Y_CROSS))
    student_rows, student_units, exp_pull, exp_sums = call(
        functools.partial(exps_kernel, own),
        (bf16((all_rows, width)), bf16((held, width)), f32((first, width)), tile),
        (place, near, far, *student_protos),
        smem=1,
        scratch=[row_scratch, pltpu.VMEM((all_rows, own), jnp.float32)],
        work=held * all_rows,
    )
    keep, send = call(
        functools.partial(last_kernel, own, rows),
        (message, message),
        (place, *parts, *weights, student_units, exp_pull, exp_sums),
        smem=1,
        scratch=[*sweep_scratch, pltpu.VMEM((2, 4, 16, width), jnp.float32)],
        work=held * all_rows,
    )
    *parts, send = lax.optimization_barrier((*parts, send))
    targets, exps, own_units, own_scales = call(
        own_kernel,
        (f32((own, all_rows)), f32((own, all_rows)), f32((own, width)), f32((own, LANES))),
        (place, *parts, teacher_rows, student_rows, teacher_prototypes, prototypes),
        smem=1,
        work=own * all_rows,
    )
    total = keep + swap(send, "proto", X_CROSS)
    return call(
        grads_kernel,
        (f32((rows, width)), f32((1, own, width))),
        (
            place,
            total,
            swap(total[2 * rows :], "proto", Y_CROSS),
            targets,
            exps,
            own_units,
            own_scales,
            student_rows,
            student_feat,
        ),
        smem=1,
        work=own * all_rows,
    )


def sample_totals(values):
    return lax.psum(values, "proto")


def proto_totals(values):
    return lax.psum(values, "dp")


def on_device_group_rows(student_feat, teacher_feat, prototypes, teacher_prototypes, live_count):
    student_unit, student_length = unit_rows(student_feat)
    teacher_unit, teacher_length = unit_rows(teacher_feat)
    proto_unit, proto_length = unit_rows(prototypes)
    teacher_proto, teacher_proto_length = unit_rows(teacher_prototypes)
    proto_bf = proto_unit.astype(jnp.bfloat16)
    teacher_proto_bf = teacher_proto.astype(jnp.bfloat16)
    student_rows, teacher_rows = (
        lax.all_gather(student_unit.astype(jnp.bfloat16), "proto", axis=0, tiled=True),
        lax.all_gather(teacher_unit.astype(jnp.bfloat16), "proto", axis=0, tiled=True),
    )
    group_size = student_rows.shape[0]
    live_rows = live_count[lax.axis_index("dp")]
    live_mask = jnp.arange(group_size, dtype=jnp.int32) < live_rows
    live_column = live_mask[:, None]
    contract_last = (((1,), (1,)), ((), ()))
    logits = (
        lax.dot_general(student_rows, proto_bf, contract_last, preferred_element_type=jnp.float32)
        / student_temp
    )
    teacher_scores = (
        lax.dot_general(
            teacher_rows, teacher_proto_bf, contract_last, preferred_element_type=jnp.float32
        )
        / teacher_temp
    )
    weights = jnp.where(live_column, jnp.exp(teacher_scores), 0.0)
    partition = sample_totals(jnp.sum(jnp.exp(logits), axis=1))
    targets = weights
    for iteration in range(ITERS):
        targets = targets / proto_totals(jnp.sum(targets, axis=0))[None, :]
        row_sums = sample_totals(jnp.sum(targets, axis=1))
        targets = targets / jnp.where(live_mask, row_sums, 1.0)[:, None]
    student_probs = jnp.exp(logits - jnp.log(partition)[:, None])
    grad_block = jnp.where(live_column, (student_probs - targets) / student_temp, 0.0).astype(
        jnp.bfloat16
    )
    pulled = lax.psum_scatter(
        jnp.dot(grad_block, proto_bf, preferred_element_type=jnp.float32),
        "proto",
        scatter_dimension=0,
        tiled=True,
    )
    student_grad = (
        pulled - student_unit * jnp.sum(student_unit * pulled, axis=1, keepdims=True)
    ) / student_length
    own_protos = prototypes.shape[0] // lax.axis_size("dp")
    contract_first = (((0,), (0,)), ((), ()))
    pushed = lax.psum_scatter(
        lax.dot_general(
            grad_block, student_rows, contract_first, preferred_element_type=jnp.float32
        ),
        "dp",
        scatter_dimension=0,
        tiled=True,
    )
    first_proto = lax.axis_index("dp") * own_protos
    own_units = lax.dynamic_slice_in_dim(proto_unit, first_proto, own_protos, 0)
    own_lengths = lax.dynamic_slice_in_dim(proto_length, first_proto, own_protos, 0)
    proto_grad = (
        pushed - own_units * jnp.sum(own_units * pushed, axis=1, keepdims=True)
    ) / own_lengths
    return (student_grad, proto_grad[None])


def on_device(student_feat, teacher_feat, prototypes, teacher_prototypes, live_count):
    n_dp, n_proto = lax.axis_size("dp"), lax.axis_size("proto")
    rows, width = student_feat.shape
    protos = prototypes.shape[0]
    lanes = n_dp * n_proto * rows
    fits = (
        n_proto == 2 * Y
        and n_dp & (n_dp - 1) == 0
        and rows % 4 == 0
        and rows <= 16
        and lanes % LANES == 0
        and lanes <= 8 * LANES
        and width == 2 * LANES
        and protos == n_dp * 2 * LANES
        and 4 * protos * lanes * 4 <= BLOCK_BYTES
    )
    plan = on_device_all_rows if fits else on_device_group_rows
    return plan(student_feat, teacher_feat, prototypes, teacher_prototypes, live_count)


def solution(mesh):
    return jax.shard_map(
        on_device,
        mesh=mesh,
        in_specs=(
            P(("dp", "proto"), None),
            P(("dp", "proto"), None),
            P("proto", None),
            P("proto", None),
            P(),
        ),
        out_specs=(P(("dp", "proto"), None), P("proto", "dp", None)),
        check_vma=False,
    )
```

```python
import functools

import jax
import jax.numpy as jnp
from jax import lax
from jax.experimental import pallas as pl
from jax.experimental.pallas import tpu as pltpu
from jax.sharding import PartitionSpec as P

ITERS = 3

student_temp = 0.1
teacher_temp = 0.07
eps_norm = 1e-06

LANES = 128
BLOCK_BYTES = 8 * 2**20


def unit_rows(values):
    widened = values.astype(jnp.float32)
    length = jnp.sqrt(jnp.sum(widened * widened, axis=1, keepdims=True) + eps_norm)
    return (widened / length, length)


CORE, X, Y = 1, 2, 4
X_CROSS, Y_CROSS = X | CORE, Y | CORE


def block_of(proto):
    return (proto & X) + ((proto >> 2) & 1)


def quick_unit(values):
    widened = values.astype(jnp.float32)
    squares = jnp.sum(widened * widened, axis=1, keepdims=True) + eps_norm
    scale = lax.rsqrt(squares)
    return widened * scale, scale


def dp_order(n_dp):
    return [0, *reversed(range(1, n_dp))]


def live_lanes(place_ref, half, lanes, n_dp, rows):
    mine = place_ref[1]
    parity = (mine ^ (mine >> 1) ^ (mine >> 2)) & 1
    lane = lax.broadcasted_iota(jnp.int32, (1, lanes), 1)
    live = jnp.zeros((1, lanes), jnp.float32)
    start = 0
    for t in dp_order(n_dp):
        count = place_ref[2 + (place_ref[0] ^ t)]
        for x in range(2):
            for y in range(2):
                core = parity ^ x ^ y ^ half ^ (1 if t else 0)
                proto = core + X * x + Y * y
                end = start + jnp.clip(count - proto * rows, 0, rows)
                live = jnp.where((lane >= start) & (lane < end), 1.0, live)
                start += rows
    return live


def pack_lanes(values):
    pieces = [values[:, k : k + LANES] for k in range(0, values.shape[1], LANES)]
    return jnp.concatenate(pieces + [jnp.zeros((8 - len(pieces), LANES), jnp.float32)], axis=0)


def unpack_lanes(tile, lanes):
    return jnp.concatenate([tile[k : k + 1, :] for k in range(lanes // LANES)], axis=1)


def as_column(values):
    return jnp.broadcast_to(values, (LANES, values.shape[1])).T


def as_tile(partial):
    return pack_lanes(jnp.sum(partial.T, axis=0, keepdims=True))


def inverse_rows(tile, rows):
    total = unpack_lanes(tile, rows)
    live = total > 0.0
    return jnp.where(live, 1.0 / jnp.where(live, total, 1.0), 0.0)


def place_rows(place_ref, ref, which, rows, scratch):
    mine_x, mine_y = (place_ref[1] >> 1) & 1, (place_ref[1] >> 2) & 1
    start = 0
    for t in range(ref.shape[1]):
        for x in range(2):
            for y in range(2):
                block = ref[mine_y ^ y, t, mine_x ^ x].astype(jnp.float32)
                scratch[start : start + rows, :] = block[which * rows : (which + 1) * rows]
                start += rows
    unit, _ = quick_unit(scratch[...])
    return unit.astype(jnp.bfloat16)


def scores_of(rows_all, units):
    return lax.dot_general(
        rows_all, units, (((1,), (1,)), ((), ())), preferred_element_type=jnp.float32
    )


def twice(column):
    return jnp.concatenate([column, column], axis=1)


def weighted_rows(panels, left, scale_ref, part_ref, add=False):
    tiles = panels[0].shape[1] // LANES
    scales = [scale_ref[:, left + k * LANES : left + (k + 1) * LANES] for k in range(tiles)]
    top = 0
    for ref in panels:

        def body(i, _, ref=ref, top=top):
            at = pl.ds(pl.multiple_of(i * 8, 8), 8)
            to = pl.ds(pl.multiple_of(i * 8 + top, 8), 8)
            sums = [None] * 4
            for k in range(tiles):
                term = ref[at, k * LANES : (k + 1) * LANES] * scales[k]
                sums[k % 4] = term if sums[k % 4] is None else sums[k % 4] + term
            total = (sums[0] + sums[1]) + (sums[2] + sums[3])
            part_ref[to, :] = part_ref[to, :] + total if add else total
            return 0

        lax.fori_loop(0, ref.shape[0] // 8, body, 0, unroll=8)
        top += ref.shape[0]


def column_scales(panels, left, row_ref, scale_ref):
    tiles = panels[0].shape[1] // LANES
    sums = [jnp.zeros((8, LANES), jnp.float32)] * tiles
    top = 0
    for ref in panels:

        def body(i, sums, ref=ref, top=top):
            at = pl.ds(pl.multiple_of(i * 8, 8), 8)
            row = row_ref[pl.ds(pl.multiple_of(i * 8 + top, 8), 8), :]
            return [
                total + ref[at, k * LANES : (k + 1) * LANES] * row for k, total in enumerate(sums)
            ]

        sums = lax.fori_loop(0, ref.shape[0] // 8, body, sums, unroll=8)
        top += ref.shape[0]
    for k, total in enumerate(sums):
        inverse = 1.0 / jnp.sum(total, axis=0, keepdims=True)
        at = slice(left + k * LANES, left + (k + 1) * LANES)
        scale_ref[:, at] = jnp.broadcast_to(inverse, (8, LANES))


def weights_of(rows, units, live):
    weights = jnp.exp(scores_of(rows, units) * (1 / teacher_temp)) * live
    return weights, fold(weights)


def fold(values):
    return jnp.sum(values.reshape(values.shape[0] // 8, 8, values.shape[1]), axis=0)


def units_kernel(proto_ref, units_ref):
    units_ref[...] = quick_unit(proto_ref[...])[0].astype(jnp.bfloat16)


def near_kernel(chunk, place_ref, near_ref, *refs):
    *unit_refs, weights_ref, sums_ref, rows_ref, live_ref, scratch = refs
    half = rows_ref.shape[0]
    rows = near_ref.shape[3] // 2
    protos = unit_refs[0].shape[0]
    rows_near = place_rows(place_ref, near_ref, 0, rows, scratch)
    rows_ref[...] = rows_near
    live = as_column(live_lanes(place_ref, 0, half, near_ref.shape[1], rows))
    live_ref[...] = live
    live = twice(live)
    for k, unit_ref in enumerate(unit_refs):
        for start in range(0, protos, chunk):
            at = slice(k * protos + start, k * protos + start + chunk)
            weights_ref[:, at], sums_ref[:, at] = weights_of(
                rows_near, unit_ref[start : start + chunk, :], live
            )


def far_kernel(chunk, place_ref, far_ref, near_rows_ref, near_weights_ref, near_sums_ref, *refs):
    *unit_refs, weights_ref, rows_ref, live_ref, sums_ref, scratch, scale_ref, part_ref = refs
    half = near_rows_ref.shape[0]
    rows = far_ref.shape[3] // 2
    protos = unit_refs[0].shape[0]
    rows_far = place_rows(place_ref, far_ref, 0, rows, scratch)
    rows_ref[...] = rows_far
    live = as_column(live_lanes(place_ref, 1, half, far_ref.shape[1], rows))
    live_ref[...] = live
    for k, unit_ref in enumerate(unit_refs):
        for start in range(0, protos, chunk):
            at = slice(k * protos + start, k * protos + start + chunk)
            weights, sums = weights_of(rows_far, unit_ref[start : start + chunk, :], twice(live))
            weights_ref[:, at] = weights
            inverse = 1.0 / jnp.sum(near_sums_ref[:, at] + sums, axis=0, keepdims=True)
            scale_ref[:, at] = jnp.broadcast_to(inverse, (8, chunk))
    weighted_rows([near_weights_ref, weights_ref], 0, scale_ref, part_ref)
    sums_ref[...] = as_tile(part_ref[...])


def across_kernel(chunk, near_rows_ref, far_rows_ref, near_live_ref, far_live_ref, *refs):
    *proto_refs, weights_ref = refs
    protos = proto_refs[0].shape[0]
    rows_all = jnp.concatenate([near_rows_ref[...], far_rows_ref[...]], axis=0)
    live = twice(jnp.concatenate([near_live_ref[...], far_live_ref[...]], axis=0))
    for k, proto_ref in enumerate(proto_refs):
        for start in range(0, protos, chunk):
            units = quick_unit(proto_ref[start : start + chunk, :])[0].astype(jnp.bfloat16)
            at = slice(k * protos + start, k * protos + start + chunk)
            weights_ref[:, at], _ = weights_of(rows_all, units, live)


def scale_columns(sums, near_ref, far_ref, across_ref, row_ref, scale_ref):
    row_ref[...] = as_column(inverse_rows(sums, row_ref.shape[0]))
    column_scales([near_ref, far_ref], 0, row_ref, scale_ref)
    column_scales([across_ref], near_ref.shape[1], row_ref, scale_ref)


def next_sums(near_ref, far_ref, across_ref, scale_ref, part_ref):
    weighted_rows([near_ref, far_ref], 0, scale_ref, part_ref)
    weighted_rows([across_ref], near_ref.shape[1], scale_ref, part_ref, add=True)
    return as_tile(part_ref[...])


def step_kernel(mine_ref, other_ref, near_ref, far_ref, across_ref, sums_ref, *scratch):
    row_ref, scale_ref, part_ref = scratch
    sums = mine_ref[...] + other_ref[...]
    scale_columns(sums, near_ref, far_ref, across_ref, row_ref, scale_ref)
    sums_ref[...] = next_sums(near_ref, far_ref, across_ref, scale_ref, part_ref)


def split(values):
    high = values.astype(jnp.bfloat16)
    low = (values - high.astype(jnp.float32)).astype(jnp.bfloat16)
    return jnp.concatenate([high, low], axis=0)


def exps_kernel(chunk, place_ref, near_ref, far_ref, *refs):
    *proto_refs, rows_ref, units_ref, pull_ref, sums_ref, scratch, exps_ref = refs
    all_rows, half = rows_ref.shape[0], rows_ref.shape[0] // 2
    protos = proto_refs[0].shape[0]
    first = pull_ref.shape[0]
    for k, ref in enumerate((near_ref, far_ref)):
        rows_half = place_rows(place_ref, ref, 1, ref.shape[3] // 2, scratch)
        rows_ref[k * half : (k + 1) * half, :] = rows_half
    rows_all = rows_ref[...]
    part = jnp.zeros((all_rows, LANES), jnp.float32)
    pull = jnp.zeros((2 * first, pull_ref.shape[1]), jnp.float32)
    for k, proto_ref in enumerate(proto_refs):
        for start in range(0, protos, chunk):
            units = quick_unit(proto_ref[start : start + chunk, :])[0].astype(jnp.bfloat16)
            units_ref[k * protos + start : k * protos + start + chunk, :] = units
            exps_ref[...] = jnp.exp(scores_of(rows_all, units) * (1 / student_temp))
            for at in range(0, chunk, LANES):
                part = part + exps_ref[:, at : at + LANES]
            exps = split(exps_ref[:first, :])
            pull = pull + jnp.dot(exps, units, preferred_element_type=jnp.float32)
    pull_ref[...] = pull[:first] + pull[first:]
    sums_ref[...] = as_tile(part)


def last_kernel(chunk, rows, place_ref, mine_ref, other_ref, near_ref, far_ref, across_ref, *refs):
    units_ref, exp_pull_ref, exp_sums_ref, scale_ref, keep_ref, send_ref, row_ref, blocks_ref = refs
    first = exp_pull_ref.shape[0]
    sums = mine_ref[...] + other_ref[...]
    scale_columns(sums, near_ref, far_ref, across_ref, row_ref, scale_ref)
    pull = jnp.zeros((2 * first, exp_pull_ref.shape[1]), jnp.float32)
    for start in range(0, units_ref.shape[0], chunk):
        at = slice(start, start + chunk)
        scaled = split(near_ref[:first, at] * scale_ref[:1, at])
        pull = pull + jnp.dot(scaled, units_ref[at, :], preferred_element_type=jnp.float32)
    pulls = (pull[:first] + pull[first:], exp_pull_ref[...])
    for k, pull in enumerate(pulls):
        for block in range(4):
            blocks_ref[k, block, :rows, :] = pull[block * rows : (block + 1) * rows]
    mine = place_ref[1]
    for ref, proto in ((keep_ref, mine), (send_ref, mine ^ X)):
        for j, owner in enumerate((proto, proto ^ Y)):
            for k in range(2):
                start = (2 * j + k) * rows
                ref[start : start + rows, :] = blocks_ref[k, block_of(owner), :rows, :]
        ref[4 * rows :, :LANES] = exp_sums_ref[...]
        ref[4 * rows :, LANES:] = jnp.zeros_like(exp_sums_ref)


def last_sums_kernel(near_ref, far_ref, across_ref, scale_ref, sums_ref, part_ref):
    sums_ref[:, :LANES] = jnp.zeros_like(sums_ref[:, :LANES])
    sums_ref[:, LANES:] = next_sums(near_ref, far_ref, across_ref, scale_ref, part_ref)


def own_kernel(place_ref, mine_ref, other_ref, near_rows_ref, far_rows_ref, *refs):
    student_rows_ref, teacher_proto_ref, proto_ref, *refs = refs
    targets_ref, exps_ref, unit_ref, scale_ref = refs
    teacher_rows = jnp.concatenate([near_rows_ref[...], far_rows_ref[...]], axis=0)
    own, all_rows = targets_ref.shape
    row_scale = inverse_rows(mine_ref[...] + other_ref[...], all_rows)
    live = jnp.where(row_scale > 0.0, 1.0, 0.0)
    first = pl.ds(pl.multiple_of(place_ref[0] * own, own), own)
    units = quick_unit(teacher_proto_ref[first, :])[0].astype(jnp.bfloat16)
    weights = jnp.exp(scores_of(units, teacher_rows) * (1 / teacher_temp)) * live
    inverse = 1.0 / jnp.sum(weights * row_scale, axis=1, keepdims=True)
    targets_ref[...] = weights * (inverse * (1 / student_temp))
    unit, scale = quick_unit(proto_ref[first, :])
    unit_ref[...] = unit
    scale_ref[...] = jnp.broadcast_to(scale, scale_ref.shape)
    units = unit.astype(jnp.bfloat16)
    exps = jnp.exp(scores_of(units, student_rows_ref[...]) * (1 / student_temp))
    exps_ref[...] = exps * (1 / student_temp)


def grads_kernel(place_ref, mine_ref, sums_ref, other_ref, targets_ref, exps_ref, *refs):
    unit_ref, scale_ref, rows_ref, feat_ref, student_out_ref, proto_out_ref = refs
    all_rows = targets_ref.shape[1]
    rows = feat_ref.shape[0]
    sums = sums_ref[...] + other_ref[2 * rows :, :]
    target_scale = inverse_rows(sums[:, LANES:], all_rows)
    exp_scale = jnp.where(target_scale > 0.0, 1.0 / unpack_lanes(sums[:, :LANES], all_rows), 0.0)

    grad = exps_ref[...] * exp_scale - targets_ref[...] * target_scale
    pushed = jnp.dot(grad.astype(jnp.bfloat16), rows_ref[...], preferred_element_type=jnp.float32)
    unit = unit_ref[...]
    along = jnp.sum(unit * pushed, axis=1, keepdims=True)
    proto_out_ref[0] = (pushed - unit * along) * twice(scale_ref[...])

    row = lax.broadcasted_iota(jnp.int32, (rows, LANES), 0) + block_of(place_ref[1]) * rows
    here = lax.broadcasted_iota(jnp.int32, (rows, LANES), 1) == row
    target_column, exp_column = [
        jnp.sum(jnp.where(here, scale[:, :LANES], 0.0), axis=1, keepdims=True) * (1 / student_temp)
        for scale in (target_scale, exp_scale)
    ]
    target_pull, exp_pull = [
        mine_ref[k * rows : (k + 1) * rows, :] + other_ref[k * rows : (k + 1) * rows, :]
        for k in range(2)
    ]
    pulled = exp_pull * exp_column - target_pull * target_column
    unit, scale = quick_unit(feat_ref[...])
    student_out_ref[...] = (
        pulled - unit * jnp.sum(unit * pulled, axis=1, keepdims=True)
    ) * scale


def call(kernel, out_shape, operands, smem=0, scratch=(), work=0):
    vmem = pl.BlockSpec(memory_space=pltpu.VMEM)
    return pl.pallas_call(
        kernel,
        out_shape=out_shape,
        in_specs=[pl.BlockSpec(memory_space=pltpu.SMEM)] * smem + [vmem] * (len(operands) - smem),
        out_specs=jax.tree.map(lambda _: vmem, out_shape),
        scratch_shapes=scratch,
        compiler_params=pltpu.CompilerParams(vmem_limit_bytes=24 * 2**20),
        cost_estimate=pl.CostEstimate(
            flops=512 * work, bytes_accessed=4 * work, transcendentals=work
        ),
    )(*operands)


def swap(values, axis, distance):
    others = [(k, k ^ distance) for k in range(lax.axis_size(axis))]
    return lax.ppermute(values, axis, others)


def swap_dp(values, t):
    n_dp, n_proto = lax.axis_size("dp"), lax.axis_size("proto")
    others = [
        (d * n_proto + p, (d ^ t) * n_proto + (p ^ CORE)) for d in range(n_dp) for p in range(n_proto)
    ]
    return lax.ppermute(values, ("dp", "proto"), others)


def on_device_all_rows(student_feat, teacher_feat, prototypes, teacher_prototypes, live_count):
    n_dp, n_proto = lax.axis_size("dp"), lax.axis_size("proto")
    rows, width = student_feat.shape
    protos = prototypes.shape[0]
    own = protos // n_dp
    all_rows = n_dp * n_proto * rows
    half = all_rows // 2
    first = 4 * rows
    held = 2 * protos
    f32 = functools.partial(jax.ShapeDtypeStruct, dtype=jnp.float32)
    bf16 = functools.partial(jax.ShapeDtypeStruct, dtype=jnp.bfloat16)
    place = jnp.stack([lax.axis_index("dp"), lax.axis_index("proto")]).astype(jnp.int32)
    place = jnp.concatenate([place, live_count])
    tile = f32((8, LANES))
    message = f32((4 * rows + 8, width))
    row_scratch = pltpu.VMEM((half, width), jnp.float32)
    column = pltpu.VMEM((all_rows, LANES), jnp.float32)
    scale_row = pltpu.VMEM((8, held), jnp.float32)
    sweep_scratch = [column, pltpu.VMEM((8, 2 * held), jnp.float32), column]

    both = lax.optimization_barrier(jnp.concatenate([teacher_feat, student_feat], axis=0))
    across_x = swap(both, "proto", X_CROSS)
    across_x, own_protos, place = lax.optimization_barrier((across_x, teacher_prototypes, place))
    across_protos = swap(own_protos, "proto", X_CROSS)
    student_protos = (prototypes, swap(prototypes, "proto", CORE))
    near = jnp.stack([both, across_x])
    teacher_units = call(units_kernel, bf16((protos, width)), (own_protos,), work=protos * width)
    teacher_units = (teacher_units, swap(teacher_units, "proto", CORE))
    near = jnp.stack([near] + [swap_dp(near, t) for t in dp_order(n_dp)[1:]])
    near = jnp.stack([near, swap(near, "proto", Y_CROSS)])
    far = swap(near, "proto", CORE)

    near_weights, near_sums, near_rows, near_live = call(
        functools.partial(near_kernel, own),
        (f32((half, held)), f32((8, held)), bf16((half, width)), f32((half, LANES))),
        (place, near, *teacher_units),
        smem=1,
        scratch=[row_scratch],
        work=held * half,
    )
    far_weights, far_rows, far_live, sums = call(
        functools.partial(far_kernel, own),
        (f32((half, held)), bf16((half, width)), f32((half, LANES)), tile),
        (place, far, near_rows, near_weights, near_sums, *teacher_units),
        smem=1,
        scratch=[row_scratch, scale_row, column],
        work=held * half,
    )
    sums = sums + swap(sums, "proto", Y_CROSS)
    sums, across_protos = lax.optimization_barrier((sums, across_protos))
    parts = (sums, swap(sums, "proto", X_CROSS))
    across_weights = call(
        functools.partial(across_kernel, own),
        f32((all_rows, held)),
        (near_rows, far_rows, near_live, far_live, across_protos, swap(across_protos, "proto", CORE)),
        work=held * all_rows,
    )
    weights = (near_weights, far_weights, across_weights)
    for _ in range(ITERS - 2):
        sums = call(
            step_kernel,
            tile,
            (*parts, *weights),
            scratch=sweep_scratch,
            work=held * all_rows,
        )
        sums, near, far, *student_protos = lax.optimization_barrier(
            (sums, near, far, *student_protos)
        )
        parts = (sums, swap(sums, "proto", Y_CROSS))
    student_rows, student_units, exp_pull, exp_sums = call(
        functools.partial(exps_kernel, own),
        (bf16((all_rows, width)), bf16((held, width)), f32((first, width)), tile),
        (place, near, far, *student_protos),
        smem=1,
        scratch=[row_scratch, pltpu.VMEM((all_rows, own), jnp.float32)],
        work=held * all_rows,
    )
    scales, keep, send = call(
        functools.partial(last_kernel, own, rows),
        (f32((8, 2 * held)), message, message),
        (place, *parts, *weights, student_units, exp_pull, exp_sums),
        smem=1,
        scratch=[column, pltpu.VMEM((2, 4, 16, width), jnp.float32)],
        work=held * all_rows,
    )
    last_sums = call(
        last_sums_kernel,
        f32((8, width)),
        (*weights, scales),
        scratch=[column],
        work=held * all_rows,
    )
    *parts, send = lax.optimization_barrier((*parts, send))
    targets, exps, own_units, own_scales = call(
        own_kernel,
        (f32((own, all_rows)), f32((own, all_rows)), f32((own, width)), f32((own, LANES))),
        (place, *parts, near_rows, far_rows, student_rows, teacher_prototypes, prototypes),
        smem=1,
        work=own * all_rows,
    )
    total = keep + swap(send, "proto", X_CROSS)
    last_sums = total[4 * rows :] + last_sums
    return call(
        grads_kernel,
        (f32((rows, width)), f32((1, own, width))),
        (
            place,
            total,
            last_sums,
            swap(jnp.concatenate([total[2 * rows : 4 * rows], last_sums]), "proto", Y_CROSS),
            targets,
            exps,
            own_units,
            own_scales,
            student_rows,
            student_feat,
        ),
        smem=1,
        work=own * all_rows,
    )


def sample_totals(values):
    return lax.psum(values, "proto")


def proto_totals(values):
    return lax.psum(values, "dp")


def on_device_group_rows(student_feat, teacher_feat, prototypes, teacher_prototypes, live_count):
    student_unit, student_length = unit_rows(student_feat)
    teacher_unit, teacher_length = unit_rows(teacher_feat)
    proto_unit, proto_length = unit_rows(prototypes)
    teacher_proto, teacher_proto_length = unit_rows(teacher_prototypes)
    proto_bf = proto_unit.astype(jnp.bfloat16)
    teacher_proto_bf = teacher_proto.astype(jnp.bfloat16)
    student_rows, teacher_rows = (
        lax.all_gather(student_unit.astype(jnp.bfloat16), "proto", axis=0, tiled=True),
        lax.all_gather(teacher_unit.astype(jnp.bfloat16), "proto", axis=0, tiled=True),
    )
    group_size = student_rows.shape[0]
    live_rows = live_count[lax.axis_index("dp")]
    live_mask = jnp.arange(group_size, dtype=jnp.int32) < live_rows
    live_column = live_mask[:, None]
    contract_last = (((1,), (1,)), ((), ()))
    logits = (
        lax.dot_general(student_rows, proto_bf, contract_last, preferred_element_type=jnp.float32)
        / student_temp
    )
    teacher_scores = (
        lax.dot_general(
            teacher_rows, teacher_proto_bf, contract_last, preferred_element_type=jnp.float32
        )
        / teacher_temp
    )
    weights = jnp.where(live_column, jnp.exp(teacher_scores), 0.0)
    partition = sample_totals(jnp.sum(jnp.exp(logits), axis=1))
    targets = weights
    for iteration in range(ITERS):
        targets = targets / proto_totals(jnp.sum(targets, axis=0))[None, :]
        row_sums = sample_totals(jnp.sum(targets, axis=1))
        targets = targets / jnp.where(live_mask, row_sums, 1.0)[:, None]
    student_probs = jnp.exp(logits - jnp.log(partition)[:, None])
    grad_block = jnp.where(live_column, (student_probs - targets) / student_temp, 0.0).astype(
        jnp.bfloat16
    )
    pulled = lax.psum_scatter(
        jnp.dot(grad_block, proto_bf, preferred_element_type=jnp.float32),
        "proto",
        scatter_dimension=0,
        tiled=True,
    )
    student_grad = (
        pulled - student_unit * jnp.sum(student_unit * pulled, axis=1, keepdims=True)
    ) / student_length
    own_protos = prototypes.shape[0] // lax.axis_size("dp")
    contract_first = (((0,), (0,)), ((), ()))
    pushed = lax.psum_scatter(
        lax.dot_general(
            grad_block, student_rows, contract_first, preferred_element_type=jnp.float32
        ),
        "dp",
        scatter_dimension=0,
        tiled=True,
    )
    first_proto = lax.axis_index("dp") * own_protos
    own_units = lax.dynamic_slice_in_dim(proto_unit, first_proto, own_protos, 0)
    own_lengths = lax.dynamic_slice_in_dim(proto_length, first_proto, own_protos, 0)
    proto_grad = (
        pushed - own_units * jnp.sum(own_units * pushed, axis=1, keepdims=True)
    ) / own_lengths
    return (student_grad, proto_grad[None])


def on_device(student_feat, teacher_feat, prototypes, teacher_prototypes, live_count):
    n_dp, n_proto = lax.axis_size("dp"), lax.axis_size("proto")
    rows, width = student_feat.shape
    protos = prototypes.shape[0]
    lanes = n_dp * n_proto * rows
    fits = (
        n_proto == 2 * Y
        and n_dp & (n_dp - 1) == 0
        and rows % 4 == 0
        and rows <= 16
        and lanes % LANES == 0
        and lanes <= 8 * LANES
        and width == 2 * LANES
        and protos == n_dp * 2 * LANES
        and 4 * protos * lanes * 4 <= BLOCK_BYTES
    )
    plan = on_device_all_rows if fits else on_device_group_rows
    return plan(student_feat, teacher_feat, prototypes, teacher_prototypes, live_count)


def solution(mesh):
    return jax.shard_map(
        on_device,
        mesh=mesh,
        in_specs=(
            P(("dp", "proto"), None),
            P(("dp", "proto"), None),
            P("proto", None),
            P("proto", None),
            P(),
        ),
        out_specs=(P(("dp", "proto"), None), P("proto", "dp", None)),
        check_vma=False,
    )
```

```python
import functools

import jax
import jax.numpy as jnp
from jax import lax
from jax.experimental import pallas as pl
from jax.experimental.pallas import tpu as pltpu
from jax.sharding import PartitionSpec as P

ITERS = 3

student_temp = 0.1
teacher_temp = 0.07
eps_norm = 1e-06

LANES = 128
BLOCK_BYTES = 8 * 2**20


def unit_rows(values):
    widened = values.astype(jnp.float32)
    length = jnp.sqrt(jnp.sum(widened * widened, axis=1, keepdims=True) + eps_norm)
    return (widened / length, length)


CORE, X, Y = 1, 2, 4
X_CROSS, Y_CROSS = X | CORE, Y | CORE


def block_of(proto):
    return (proto & X) + ((proto >> 2) & 1)


def quick_unit(values):
    widened = values.astype(jnp.float32)
    squares = jnp.sum(widened * widened, axis=1, keepdims=True) + eps_norm
    scale = lax.rsqrt(squares)
    return widened * scale, scale


def dp_order(n_dp):
    return [0, *reversed(range(1, n_dp))]


def live_lanes(place_ref, half, lanes, n_dp, rows):
    mine = place_ref[1]
    parity = (mine ^ (mine >> 1) ^ (mine >> 2)) & 1
    lane = lax.broadcasted_iota(jnp.int32, (1, lanes), 1)
    live = jnp.zeros((1, lanes), jnp.float32)
    start = 0
    for t in dp_order(n_dp):
        count = place_ref[2 + (place_ref[0] ^ t)]
        for x in range(2):
            for y in range(2):
                core = parity ^ x ^ y ^ half ^ (1 if t else 0)
                proto = core + X * x + Y * y
                end = start + jnp.clip(count - proto * rows, 0, rows)
                live = jnp.where((lane >= start) & (lane < end), 1.0, live)
                start += rows
    return live


def pack_lanes(values):
    pieces = [values[:, k : k + LANES] for k in range(0, values.shape[1], LANES)]
    return jnp.concatenate(pieces + [jnp.zeros((8 - len(pieces), LANES), jnp.float32)], axis=0)


def unpack_lanes(tile, lanes):
    return jnp.concatenate([tile[k : k + 1, :] for k in range(lanes // LANES)], axis=1)


def as_column(values):
    return jnp.broadcast_to(values, (LANES, values.shape[1])).T


def as_tile(partial):
    return pack_lanes(jnp.sum(partial.T, axis=0, keepdims=True))


def inverse_rows(tile, rows):
    total = unpack_lanes(tile, rows)
    live = total > 0.0
    return jnp.where(live, 1.0 / jnp.where(live, total, 1.0), 0.0)


def place_rows(place_ref, ref, which, rows, scratch):
    mine_x, mine_y = (place_ref[1] >> 1) & 1, (place_ref[1] >> 2) & 1
    start = 0
    for t in range(ref.shape[1]):
        for x in range(2):
            for y in range(2):
                block = ref[mine_y ^ y, t, mine_x ^ x].astype(jnp.float32)
                scratch[start : start + rows, :] = block[which * rows : (which + 1) * rows]
                start += rows
    unit, _ = quick_unit(scratch[...])
    return unit.astype(jnp.bfloat16)


def scores_of(rows_all, units):
    return lax.dot_general(
        rows_all, units, (((1,), (1,)), ((), ())), preferred_element_type=jnp.float32
    )


def twice(column):
    return jnp.concatenate([column, column], axis=1)


def weighted_rows(panels, left, scale_ref, part_ref, add=False):
    tiles = panels[0].shape[1] // LANES
    scales = [scale_ref[:, left + k * LANES : left + (k + 1) * LANES] for k in range(tiles)]
    top = 0
    for ref in panels:

        def body(i, _, ref=ref, top=top):
            at = pl.ds(pl.multiple_of(i * 8, 8), 8)
            to = pl.ds(pl.multiple_of(i * 8 + top, 8), 8)
            sums = [None] * 4
            for k in range(tiles):
                term = ref[at, k * LANES : (k + 1) * LANES] * scales[k]
                sums[k % 4] = term if sums[k % 4] is None else sums[k % 4] + term
            total = (sums[0] + sums[1]) + (sums[2] + sums[3])
            part_ref[to, :] = part_ref[to, :] + total if add else total
            return 0

        lax.fori_loop(0, ref.shape[0] // 8, body, 0, unroll=8)
        top += ref.shape[0]


def column_scales(panels, left, row_ref, scale_ref):
    tiles = panels[0].shape[1] // LANES
    sums = [jnp.zeros((8, LANES), jnp.float32)] * tiles
    top = 0
    for ref in panels:

        def body(i, sums, ref=ref, top=top):
            at = pl.ds(pl.multiple_of(i * 8, 8), 8)
            row = row_ref[pl.ds(pl.multiple_of(i * 8 + top, 8), 8), :]
            return [
                total + ref[at, k * LANES : (k + 1) * LANES] * row for k, total in enumerate(sums)
            ]

        sums = lax.fori_loop(0, ref.shape[0] // 8, body, sums, unroll=8)
        top += ref.shape[0]
    for k, total in enumerate(sums):
        inverse = 1.0 / jnp.sum(total, axis=0, keepdims=True)
        at = slice(left + k * LANES, left + (k + 1) * LANES)
        scale_ref[:, at] = jnp.broadcast_to(inverse, (8, LANES))


def weights_of(rows, units, live):
    weights = jnp.exp(scores_of(rows, units) * (1 / teacher_temp)) * live
    return weights, fold(weights)


def fold(values):
    return jnp.sum(values.reshape(values.shape[0] // 8, 8, values.shape[1]), axis=0)


def units_kernel(proto_ref, units_ref):
    units_ref[...] = quick_unit(proto_ref[...])[0].astype(jnp.bfloat16)


def near_kernel(chunk, place_ref, near_ref, *refs):
    *unit_refs, weights_ref, sums_ref, rows_ref, live_ref, scratch = refs
    half = rows_ref.shape[0]
    rows = near_ref.shape[3] // 2
    protos = unit_refs[0].shape[0]
    rows_near = place_rows(place_ref, near_ref, 0, rows, scratch)
    rows_ref[...] = rows_near
    live = as_column(live_lanes(place_ref, 0, half, near_ref.shape[1], rows))
    live_ref[...] = live
    live = twice(live)
    for k, unit_ref in enumerate(unit_refs):
        for start in range(0, protos, chunk):
            at = slice(k * protos + start, k * protos + start + chunk)
            weights_ref[:, at], sums_ref[:, at] = weights_of(
                rows_near, unit_ref[start : start + chunk, :], live
            )


def far_kernel(chunk, place_ref, far_ref, near_rows_ref, near_weights_ref, near_sums_ref, *refs):
    *unit_refs, weights_ref, rows_ref, live_ref, sums_ref, scratch, scale_ref, part_ref = refs
    half = near_rows_ref.shape[0]
    rows = far_ref.shape[3] // 2
    protos = unit_refs[0].shape[0]
    rows_far = place_rows(place_ref, far_ref, 0, rows, scratch)
    rows_ref[...] = rows_far
    live = as_column(live_lanes(place_ref, 1, half, far_ref.shape[1], rows))
    live_ref[...] = live
    for k, unit_ref in enumerate(unit_refs):
        for start in range(0, protos, chunk):
            at = slice(k * protos + start, k * protos + start + chunk)
            weights, sums = weights_of(rows_far, unit_ref[start : start + chunk, :], twice(live))
            weights_ref[:, at] = weights
            inverse = 1.0 / jnp.sum(near_sums_ref[:, at] + sums, axis=0, keepdims=True)
            scale_ref[:, at] = jnp.broadcast_to(inverse, (8, chunk))
    weighted_rows([near_weights_ref, weights_ref], 0, scale_ref, part_ref)
    sums_ref[...] = as_tile(part_ref[...])


def across_kernel(chunk, place_ref, near_ref, far_ref, *refs):
    near_rows_ref, far_rows_ref, near_live_ref, far_live_ref, *refs = refs
    *proto_refs, weights_ref, student_ref, scratch = refs
    protos = proto_refs[0].shape[0]
    rows_all = jnp.concatenate([near_rows_ref[...], far_rows_ref[...]], axis=0)
    live = twice(jnp.concatenate([near_live_ref[...], far_live_ref[...]], axis=0))
    for k, proto_ref in enumerate(proto_refs):
        for start in range(0, protos, chunk):
            units = quick_unit(proto_ref[start : start + chunk, :])[0].astype(jnp.bfloat16)
            at = slice(k * protos + start, k * protos + start + chunk)
            weights_ref[:, at], _ = weights_of(rows_all, units, live)
    half = student_ref.shape[0] // 2
    for k, ref in enumerate((near_ref, far_ref)):
        rows_half = place_rows(place_ref, ref, 1, ref.shape[3] // 2, scratch)
        student_ref[k * half : (k + 1) * half, :] = rows_half


def scale_columns(sums, near_ref, far_ref, across_ref, row_ref, scale_ref):
    row_ref[...] = as_column(inverse_rows(sums, row_ref.shape[0]))
    column_scales([near_ref, far_ref], 0, row_ref, scale_ref)
    column_scales([across_ref], near_ref.shape[1], row_ref, scale_ref)


def next_sums(near_ref, far_ref, across_ref, scale_ref, part_ref):
    weighted_rows([near_ref, far_ref], 0, scale_ref, part_ref)
    weighted_rows([across_ref], near_ref.shape[1], scale_ref, part_ref, add=True)
    return as_tile(part_ref[...])


def step_kernel(mine_ref, other_ref, near_ref, far_ref, across_ref, sums_ref, *scratch):
    row_ref, scale_ref, part_ref = scratch
    sums = mine_ref[...] + other_ref[...]
    scale_columns(sums, near_ref, far_ref, across_ref, row_ref, scale_ref)
    sums_ref[...] = next_sums(near_ref, far_ref, across_ref, scale_ref, part_ref)


def split(values):
    high = values.astype(jnp.bfloat16)
    low = (values - high.astype(jnp.float32)).astype(jnp.bfloat16)
    return jnp.concatenate([high, low], axis=0)


def exps_kernel(chunk, rows_ref, *refs):
    *proto_refs, units_ref, pull_ref, sums_ref, exps_ref = refs
    all_rows = rows_ref.shape[0]
    protos = proto_refs[0].shape[0]
    first = pull_ref.shape[0]
    rows_all = rows_ref[...]
    part = jnp.zeros((all_rows, LANES), jnp.float32)
    pull = jnp.zeros((2 * first, pull_ref.shape[1]), jnp.float32)
    for k, proto_ref in enumerate(proto_refs):
        for start in range(0, protos, chunk):
            units = quick_unit(proto_ref[start : start + chunk, :])[0].astype(jnp.bfloat16)
            units_ref[k * protos + start : k * protos + start + chunk, :] = units
            exps_ref[...] = jnp.exp(scores_of(rows_all, units) * (1 / student_temp))
            for at in range(0, chunk, LANES):
                part = part + exps_ref[:, at : at + LANES]
            exps = split(exps_ref[:first, :])
            pull = pull + jnp.dot(exps, units, preferred_element_type=jnp.float32)
    pull_ref[...] = pull[:first] + pull[first:]
    sums_ref[...] = as_tile(part)


def last_kernel(chunk, rows, place_ref, mine_ref, other_ref, near_ref, far_ref, across_ref, *refs):
    units_ref, exp_pull_ref, exp_sums_ref, scale_ref, keep_ref, send_ref, row_ref, blocks_ref = refs
    first = exp_pull_ref.shape[0]
    sums = mine_ref[...] + other_ref[...]
    scale_columns(sums, near_ref, far_ref, across_ref, row_ref, scale_ref)
    pull = jnp.zeros((2 * first, exp_pull_ref.shape[1]), jnp.float32)
    for start in range(0, units_ref.shape[0], chunk):
        at = slice(start, start + chunk)
        scaled = split(near_ref[:first, at] * scale_ref[:1, at])
        pull = pull + jnp.dot(scaled, units_ref[at, :], preferred_element_type=jnp.float32)
    pulls = (pull[:first] + pull[first:], exp_pull_ref[...])
    for k, pull in enumerate(pulls):
        for block in range(4):
            blocks_ref[k, block, :rows, :] = pull[block * rows : (block + 1) * rows]
    mine = place_ref[1]
    for ref, proto in ((keep_ref, mine), (send_ref, mine ^ X)):
        for j, owner in enumerate((proto, proto ^ Y)):
            for k in range(2):
                start = (2 * j + k) * rows
                ref[start : start + rows, :] = blocks_ref[k, block_of(owner), :rows, :]
        ref[4 * rows :, :LANES] = exp_sums_ref[...]
        ref[4 * rows :, LANES:] = jnp.zeros_like(exp_sums_ref)


def last_sums_kernel(near_ref, far_ref, across_ref, scale_ref, sums_ref, part_ref):
    sums_ref[:, :LANES] = jnp.zeros_like(sums_ref[:, :LANES])
    sums_ref[:, LANES:] = next_sums(near_ref, far_ref, across_ref, scale_ref, part_ref)


def own_kernel(place_ref, mine_ref, other_ref, near_rows_ref, far_rows_ref, *refs):
    student_rows_ref, teacher_proto_ref, proto_ref, *refs = refs
    targets_ref, exps_ref, unit_ref, scale_ref = refs
    teacher_rows = jnp.concatenate([near_rows_ref[...], far_rows_ref[...]], axis=0)
    own, all_rows = targets_ref.shape
    row_scale = inverse_rows(mine_ref[...] + other_ref[...], all_rows)
    live = jnp.where(row_scale > 0.0, 1.0, 0.0)
    first = pl.ds(pl.multiple_of(place_ref[0] * own, own), own)
    units = quick_unit(teacher_proto_ref[first, :])[0].astype(jnp.bfloat16)
    weights = jnp.exp(scores_of(units, teacher_rows) * (1 / teacher_temp)) * live
    inverse = 1.0 / jnp.sum(weights * row_scale, axis=1, keepdims=True)
    targets_ref[...] = weights * (inverse * (1 / student_temp))
    unit, scale = quick_unit(proto_ref[first, :])
    unit_ref[...] = unit
    scale_ref[...] = jnp.broadcast_to(scale, scale_ref.shape)
    units = unit.astype(jnp.bfloat16)
    exps = jnp.exp(scores_of(units, student_rows_ref[...]) * (1 / student_temp))
    exps_ref[...] = exps * (1 / student_temp)


def grads_kernel(place_ref, mine_ref, sums_ref, other_ref, targets_ref, exps_ref, *refs):
    unit_ref, scale_ref, rows_ref, feat_ref, student_out_ref, proto_out_ref = refs
    all_rows = targets_ref.shape[1]
    rows = feat_ref.shape[0]
    sums = sums_ref[...] + other_ref[2 * rows :, :]
    target_scale = inverse_rows(sums[:, LANES:], all_rows)
    exp_scale = jnp.where(target_scale > 0.0, 1.0 / unpack_lanes(sums[:, :LANES], all_rows), 0.0)

    grad = exps_ref[...] * exp_scale - targets_ref[...] * target_scale
    pushed = jnp.dot(grad.astype(jnp.bfloat16), rows_ref[...], preferred_element_type=jnp.float32)
    unit = unit_ref[...]
    along = jnp.sum(unit * pushed, axis=1, keepdims=True)
    proto_out_ref[0] = (pushed - unit * along) * twice(scale_ref[...])

    row = lax.broadcasted_iota(jnp.int32, (rows, LANES), 0) + block_of(place_ref[1]) * rows
    here = lax.broadcasted_iota(jnp.int32, (rows, LANES), 1) == row
    target_column, exp_column = [
        jnp.sum(jnp.where(here, scale[:, :LANES], 0.0), axis=1, keepdims=True) * (1 / student_temp)
        for scale in (target_scale, exp_scale)
    ]
    target_pull, exp_pull = [
        mine_ref[k * rows : (k + 1) * rows, :] + other_ref[k * rows : (k + 1) * rows, :]
        for k in range(2)
    ]
    pulled = exp_pull * exp_column - target_pull * target_column
    unit, scale = quick_unit(feat_ref[...])
    student_out_ref[...] = (
        pulled - unit * jnp.sum(unit * pulled, axis=1, keepdims=True)
    ) * scale


def call(kernel, out_shape, operands, smem=0, scratch=(), work=0):
    vmem = pl.BlockSpec(memory_space=pltpu.VMEM)
    return pl.pallas_call(
        kernel,
        out_shape=out_shape,
        in_specs=[pl.BlockSpec(memory_space=pltpu.SMEM)] * smem + [vmem] * (len(operands) - smem),
        out_specs=jax.tree.map(lambda _: vmem, out_shape),
        scratch_shapes=scratch,
        compiler_params=pltpu.CompilerParams(vmem_limit_bytes=24 * 2**20),
        cost_estimate=pl.CostEstimate(
            flops=512 * work, bytes_accessed=4 * work, transcendentals=work
        ),
    )(*operands)


def swap(values, axis, distance):
    others = [(k, k ^ distance) for k in range(lax.axis_size(axis))]
    return lax.ppermute(values, axis, others)


def swap_dp(values, t):
    n_dp, n_proto = lax.axis_size("dp"), lax.axis_size("proto")
    others = [
        (d * n_proto + p, (d ^ t) * n_proto + (p ^ CORE)) for d in range(n_dp) for p in range(n_proto)
    ]
    return lax.ppermute(values, ("dp", "proto"), others)


def on_device_all_rows(student_feat, teacher_feat, prototypes, teacher_prototypes, live_count):
    n_dp, n_proto = lax.axis_size("dp"), lax.axis_size("proto")
    rows, width = student_feat.shape
    protos = prototypes.shape[0]
    own = protos // n_dp
    all_rows = n_dp * n_proto * rows
    half = all_rows // 2
    first = 4 * rows
    held = 2 * protos
    f32 = functools.partial(jax.ShapeDtypeStruct, dtype=jnp.float32)
    bf16 = functools.partial(jax.ShapeDtypeStruct, dtype=jnp.bfloat16)
    place = jnp.stack([lax.axis_index("dp"), lax.axis_index("proto")]).astype(jnp.int32)
    place = jnp.concatenate([place, live_count])
    tile = f32((8, LANES))
    message = f32((4 * rows + 8, width))
    row_scratch = pltpu.VMEM((half, width), jnp.float32)
    column = pltpu.VMEM((all_rows, LANES), jnp.float32)
    scale_row = pltpu.VMEM((8, held), jnp.float32)
    sweep_scratch = [column, pltpu.VMEM((8, 2 * held), jnp.float32), column]

    both = lax.optimization_barrier(jnp.concatenate([teacher_feat, student_feat], axis=0))
    across_x = swap(both, "proto", X_CROSS)
    across_x, own_protos, place = lax.optimization_barrier((across_x, teacher_prototypes, place))
    across_protos = swap(own_protos, "proto", X_CROSS)
    student_protos = (prototypes, swap(prototypes, "proto", CORE))
    near = jnp.stack([both, across_x])
    teacher_units = call(units_kernel, bf16((protos, width)), (own_protos,), work=protos * width)
    teacher_units = (teacher_units, swap(teacher_units, "proto", CORE))
    near = jnp.stack([near] + [swap_dp(near, t) for t in dp_order(n_dp)[1:]])
    near = jnp.stack([near, swap(near, "proto", Y_CROSS)])
    far = swap(near, "proto", CORE)

    near_weights, near_sums, near_rows, near_live = call(
        functools.partial(near_kernel, own),
        (f32((half, held)), f32((8, held)), bf16((half, width)), f32((half, LANES))),
        (place, near, *teacher_units),
        smem=1,
        scratch=[row_scratch],
        work=held * half,
    )
    far_weights, far_rows, far_live, sums = call(
        functools.partial(far_kernel, own),
        (f32((half, held)), bf16((half, width)), f32((half, LANES)), tile),
        (place, far, near_rows, near_weights, near_sums, *teacher_units),
        smem=1,
        scratch=[row_scratch, scale_row, column],
        work=held * half,
    )
    sums = sums + swap(sums, "proto", Y_CROSS)
    sums, across_protos = lax.optimization_barrier((sums, across_protos))
    parts = (sums, swap(sums, "proto", X_CROSS))
    across_weights, student_rows = call(
        functools.partial(across_kernel, own),
        (f32((all_rows, held)), bf16((all_rows, width))),
        (
            place,
            near,
            far,
            near_rows,
            far_rows,
            near_live,
            far_live,
            across_protos,
            swap(across_protos, "proto", CORE),
        ),
        smem=1,
        scratch=[row_scratch],
        work=held * all_rows,
    )
    weights = (near_weights, far_weights, across_weights)
    for _ in range(ITERS - 2):
        sums = call(
            step_kernel,
            tile,
            (*parts, *weights),
            scratch=sweep_scratch,
            work=held * all_rows,
        )
        sums, student_rows, *student_protos = lax.optimization_barrier(
            (sums, student_rows, *student_protos)
        )
        parts = (sums, swap(sums, "proto", Y_CROSS))
    student_units, exp_pull, exp_sums = call(
        functools.partial(exps_kernel, own),
        (bf16((held, width)), f32((first, width)), tile),
        (student_rows, *student_protos),
        scratch=[pltpu.VMEM((all_rows, own), jnp.float32)],
        work=held * all_rows,
    )
    scales, keep, send = call(
        functools.partial(last_kernel, own, rows),
        (f32((8, 2 * held)), message, message),
        (place, *parts, *weights, student_units, exp_pull, exp_sums),
        smem=1,
        scratch=[column, pltpu.VMEM((2, 4, 16, width), jnp.float32)],
        work=held * all_rows,
    )
    last_sums = call(
        last_sums_kernel,
        f32((8, width)),
        (*weights, scales),
        scratch=[column],
        work=held * all_rows,
    )
    *parts, send = lax.optimization_barrier((*parts, send))
    targets, exps, own_units, own_scales = call(
        own_kernel,
        (f32((own, all_rows)), f32((own, all_rows)), f32((own, width)), f32((own, LANES))),
        (place, *parts, near_rows, far_rows, student_rows, teacher_prototypes, prototypes),
        smem=1,
        work=own * all_rows,
    )
    total = keep + swap(send, "proto", X_CROSS)
    last_sums = total[4 * rows :] + last_sums
    return call(
        grads_kernel,
        (f32((rows, width)), f32((1, own, width))),
        (
            place,
            total,
            last_sums,
            swap(jnp.concatenate([total[2 * rows : 4 * rows], last_sums]), "proto", Y_CROSS),
            targets,
            exps,
            own_units,
            own_scales,
            student_rows,
            student_feat,
        ),
        smem=1,
        work=own * all_rows,
    )


def sample_totals(values):
    return lax.psum(values, "proto")


def proto_totals(values):
    return lax.psum(values, "dp")


def on_device_group_rows(student_feat, teacher_feat, prototypes, teacher_prototypes, live_count):
    student_unit, student_length = unit_rows(student_feat)
    teacher_unit, teacher_length = unit_rows(teacher_feat)
    proto_unit, proto_length = unit_rows(prototypes)
    teacher_proto, teacher_proto_length = unit_rows(teacher_prototypes)
    proto_bf = proto_unit.astype(jnp.bfloat16)
    teacher_proto_bf = teacher_proto.astype(jnp.bfloat16)
    student_rows, teacher_rows = (
        lax.all_gather(student_unit.astype(jnp.bfloat16), "proto", axis=0, tiled=True),
        lax.all_gather(teacher_unit.astype(jnp.bfloat16), "proto", axis=0, tiled=True),
    )
    group_size = student_rows.shape[0]
    live_rows = live_count[lax.axis_index("dp")]
    live_mask = jnp.arange(group_size, dtype=jnp.int32) < live_rows
    live_column = live_mask[:, None]
    contract_last = (((1,), (1,)), ((), ()))
    logits = (
        lax.dot_general(student_rows, proto_bf, contract_last, preferred_element_type=jnp.float32)
        / student_temp
    )
    teacher_scores = (
        lax.dot_general(
            teacher_rows, teacher_proto_bf, contract_last, preferred_element_type=jnp.float32
        )
        / teacher_temp
    )
    weights = jnp.where(live_column, jnp.exp(teacher_scores), 0.0)
    partition = sample_totals(jnp.sum(jnp.exp(logits), axis=1))
    targets = weights
    for iteration in range(ITERS):
        targets = targets / proto_totals(jnp.sum(targets, axis=0))[None, :]
        row_sums = sample_totals(jnp.sum(targets, axis=1))
        targets = targets / jnp.where(live_mask, row_sums, 1.0)[:, None]
    student_probs = jnp.exp(logits - jnp.log(partition)[:, None])
    grad_block = jnp.where(live_column, (student_probs - targets) / student_temp, 0.0).astype(
        jnp.bfloat16
    )
    pulled = lax.psum_scatter(
        jnp.dot(grad_block, proto_bf, preferred_element_type=jnp.float32),
        "proto",
        scatter_dimension=0,
        tiled=True,
    )
    student_grad = (
        pulled - student_unit * jnp.sum(student_unit * pulled, axis=1, keepdims=True)
    ) / student_length
    own_protos = prototypes.shape[0] // lax.axis_size("dp")
    contract_first = (((0,), (0,)), ((), ()))
    pushed = lax.psum_scatter(
        lax.dot_general(
            grad_block, student_rows, contract_first, preferred_element_type=jnp.float32
        ),
        "dp",
        scatter_dimension=0,
        tiled=True,
    )
    first_proto = lax.axis_index("dp") * own_protos
    own_units = lax.dynamic_slice_in_dim(proto_unit, first_proto, own_protos, 0)
    own_lengths = lax.dynamic_slice_in_dim(proto_length, first_proto, own_protos, 0)
    proto_grad = (
        pushed - own_units * jnp.sum(own_units * pushed, axis=1, keepdims=True)
    ) / own_lengths
    return (student_grad, proto_grad[None])


def on_device(student_feat, teacher_feat, prototypes, teacher_prototypes, live_count):
    n_dp, n_proto = lax.axis_size("dp"), lax.axis_size("proto")
    rows, width = student_feat.shape
    protos = prototypes.shape[0]
    lanes = n_dp * n_proto * rows
    fits = (
        n_proto == 2 * Y
        and n_dp & (n_dp - 1) == 0
        and rows % 4 == 0
        and rows <= 16
        and lanes % LANES == 0
        and lanes <= 8 * LANES
        and width == 2 * LANES
        and protos == n_dp * 2 * LANES
        and 4 * protos * lanes * 4 <= BLOCK_BYTES
    )
    plan = on_device_all_rows if fits else on_device_group_rows
    return plan(student_feat, teacher_feat, prototypes, teacher_prototypes, live_count)


def solution(mesh):
    return jax.shard_map(
        on_device,
        mesh=mesh,
        in_specs=(
            P(("dp", "proto"), None),
            P(("dp", "proto"), None),
            P("proto", None),
            P("proto", None),
            P(),
        ),
        out_specs=(P(("dp", "proto"), None), P("proto", "dp", None)),
        check_vma=False,
    )
```

```python
import functools

import jax
import jax.numpy as jnp
from jax import lax
from jax.experimental import pallas as pl
from jax.experimental.pallas import tpu as pltpu
from jax.sharding import PartitionSpec as P

ITERS = 3

student_temp = 0.1
teacher_temp = 0.07
eps_norm = 1e-06

LANES = 128
BLOCK_BYTES = 8 * 2**20


def unit_rows(values):
    widened = values.astype(jnp.float32)
    length = jnp.sqrt(jnp.sum(widened * widened, axis=1, keepdims=True) + eps_norm)
    return (widened / length, length)


CORE, X, Y = 1, 2, 4
X_CROSS, Y_CROSS = X | CORE, Y | CORE


def block_of(proto):
    return (proto & X) + ((proto >> 2) & 1)


def quick_unit(values):
    widened = values.astype(jnp.float32)
    squares = jnp.sum(widened * widened, axis=1, keepdims=True) + eps_norm
    scale = lax.rsqrt(squares)
    return widened * scale, scale


def dp_order(n_dp):
    return [0, *reversed(range(1, n_dp))]


def live_lanes(place_ref, half, lanes, n_dp, rows):
    mine = place_ref[1]
    parity = (mine ^ (mine >> 1) ^ (mine >> 2)) & 1
    lane = lax.broadcasted_iota(jnp.int32, (1, lanes), 1)
    live = jnp.zeros((1, lanes), jnp.float32)
    start = 0
    for t in dp_order(n_dp):
        count = place_ref[2 + (place_ref[0] ^ t)]
        for x in range(2):
            for y in range(2):
                core = parity ^ x ^ y ^ half ^ (1 if t else 0)
                proto = core + X * x + Y * y
                end = start + jnp.clip(count - proto * rows, 0, rows)
                live = jnp.where((lane >= start) & (lane < end), 1.0, live)
                start += rows
    return live


def pack_lanes(values):
    pieces = [values[:, k : k + LANES] for k in range(0, values.shape[1], LANES)]
    return jnp.concatenate(pieces + [jnp.zeros((8 - len(pieces), LANES), jnp.float32)], axis=0)


def unpack_lanes(tile, lanes):
    return jnp.concatenate([tile[k : k + 1, :] for k in range(lanes // LANES)], axis=1)


def as_column(values):
    return jnp.broadcast_to(values, (LANES, values.shape[1])).T


def as_tile(partial):
    return pack_lanes(jnp.sum(partial.T, axis=0, keepdims=True))


def inverse_rows(tile, rows):
    total = unpack_lanes(tile, rows)
    live = total > 0.0
    return jnp.where(live, 1.0 / jnp.where(live, total, 1.0), 0.0)


def place_rows(place_ref, ref, which, rows, scratch):
    mine_x, mine_y = (place_ref[1] >> 1) & 1, (place_ref[1] >> 2) & 1
    start = 0
    for t in range(ref.shape[1]):
        for x in range(2):
            for y in range(2):
                block = ref[mine_y ^ y, t, mine_x ^ x].astype(jnp.float32)
                scratch[start : start + rows, :] = block[which * rows : (which + 1) * rows]
                start += rows
    unit, _ = quick_unit(scratch[...])
    return unit.astype(jnp.bfloat16)


def scores_of(rows_all, units):
    return lax.dot_general(
        rows_all, units, (((1,), (1,)), ((), ())), preferred_element_type=jnp.float32
    )


def twice(column):
    return jnp.concatenate([column, column], axis=1)


def weighted_rows(panels, left, scale_ref, part_ref, add=False):
    tiles = panels[0].shape[1] // LANES
    scales = [scale_ref[:, left + k * LANES : left + (k + 1) * LANES] for k in range(tiles)]
    top = 0
    for ref in panels:

        def body(i, _, ref=ref, top=top):
            at = pl.ds(pl.multiple_of(i * 8, 8), 8)
            to = pl.ds(pl.multiple_of(i * 8 + top, 8), 8)
            sums = [None] * 4
            for k in range(tiles):
                term = ref[at, k * LANES : (k + 1) * LANES] * scales[k]
                sums[k % 4] = term if sums[k % 4] is None else sums[k % 4] + term
            total = (sums[0] + sums[1]) + (sums[2] + sums[3])
            part_ref[to, :] = part_ref[to, :] + total if add else total
            return 0

        lax.fori_loop(0, ref.shape[0] // 8, body, 0, unroll=8)
        top += ref.shape[0]


def column_scales(panels, left, row_ref, scale_ref):
    tiles = panels[0].shape[1] // LANES
    sums = [jnp.zeros((8, LANES), jnp.float32)] * tiles
    top = 0
    for ref in panels:

        def body(i, sums, ref=ref, top=top):
            at = pl.ds(pl.multiple_of(i * 8, 8), 8)
            row = row_ref[pl.ds(pl.multiple_of(i * 8 + top, 8), 8), :]
            return [
                total + ref[at, k * LANES : (k + 1) * LANES] * row for k, total in enumerate(sums)
            ]

        sums = lax.fori_loop(0, ref.shape[0] // 8, body, sums, unroll=8)
        top += ref.shape[0]
    for k, total in enumerate(sums):
        inverse = 1.0 / jnp.sum(total, axis=0, keepdims=True)
        at = slice(left + k * LANES, left + (k + 1) * LANES)
        scale_ref[:, at] = jnp.broadcast_to(inverse, (8, LANES))


def weights_of(rows, units, live):
    weights = jnp.exp(scores_of(rows, units) * (1 / teacher_temp)) * live
    return weights, fold(weights)


def fold(values):
    return jnp.sum(values.reshape(values.shape[0] // 8, 8, values.shape[1]), axis=0)


def units_kernel(n_dp, rows, place_ref, proto_ref, units_ref, *live_refs):
    units_ref[...] = quick_unit(proto_ref[...])[0].astype(jnp.bfloat16)
    for k, live_ref in enumerate(live_refs):
        live_ref[...] = as_column(live_lanes(place_ref, k, live_ref.shape[0], n_dp, rows))


def near_kernel(chunk, place_ref, near_ref, live_ref, own_units_ref, proto_ref, *refs):
    weights_ref, sums_ref, rows_ref, units_ref, scratch = refs
    rows = near_ref.shape[3] // 2
    rows_near = place_rows(place_ref, near_ref, 0, rows, scratch)
    rows_ref[...] = rows_near
    live = twice(live_ref[...])
    protos = own_units_ref.shape[0]
    for start in range(0, 2 * protos, chunk):
        at = slice(start, start + chunk)
        if start < protos:
            units = own_units_ref[at, :]
        else:
            here = slice(start - protos, start - protos + chunk)
            units = quick_unit(proto_ref[here, :])[0].astype(jnp.bfloat16)
            units_ref[here, :] = units
        weights_ref[:, at], sums_ref[:, at] = weights_of(rows_near, units, live)


def far_kernel(chunk, place_ref, far_ref, live_ref, near_weights_ref, near_sums_ref, *refs):
    *unit_refs, weights_ref, rows_ref, sums_ref, scratch, scale_ref, part_ref = refs
    rows = far_ref.shape[3] // 2
    rows_far = place_rows(place_ref, far_ref, 0, rows, scratch)
    rows_ref[...] = rows_far
    live = twice(live_ref[...])
    protos = unit_refs[0].shape[0]
    for k, unit_ref in enumerate(unit_refs):
        for start in range(0, protos, chunk):
            at = slice(k * protos + start, k * protos + start + chunk)
            weights, sums = weights_of(rows_far, unit_ref[start : start + chunk, :], live)
            weights_ref[:, at] = weights
            inverse = 1.0 / jnp.sum(near_sums_ref[:, at] + sums, axis=0, keepdims=True)
            scale_ref[:, at] = jnp.broadcast_to(inverse, (8, chunk))
    weighted_rows([near_weights_ref, weights_ref], 0, scale_ref, part_ref)
    sums_ref[...] = as_tile(part_ref[...])


def across_kernel(chunk, place_ref, near_ref, far_ref, *refs):
    near_rows_ref, far_rows_ref, near_live_ref, far_live_ref, *refs = refs
    *proto_refs, weights_ref, student_ref, scratch = refs
    protos = proto_refs[0].shape[0]
    rows_all = jnp.concatenate([near_rows_ref[...], far_rows_ref[...]], axis=0)
    live = twice(jnp.concatenate([near_live_ref[...], far_live_ref[...]], axis=0))
    for k, proto_ref in enumerate(proto_refs):
        for start in range(0, protos, chunk):
            units = quick_unit(proto_ref[start : start + chunk, :])[0].astype(jnp.bfloat16)
            at = slice(k * protos + start, k * protos + start + chunk)
            weights_ref[:, at], _ = weights_of(rows_all, units, live)
    half = student_ref.shape[0] // 2
    for k, ref in enumerate((near_ref, far_ref)):
        rows_half = place_rows(place_ref, ref, 1, ref.shape[3] // 2, scratch)
        student_ref[k * half : (k + 1) * half, :] = rows_half


def scale_columns(sums, near_ref, far_ref, across_ref, row_ref, scale_ref):
    row_ref[...] = as_column(inverse_rows(sums, row_ref.shape[0]))
    column_scales([near_ref, far_ref], 0, row_ref, scale_ref)
    column_scales([across_ref], near_ref.shape[1], row_ref, scale_ref)


def next_sums(near_ref, far_ref, across_ref, scale_ref, part_ref):
    weighted_rows([near_ref, far_ref], 0, scale_ref, part_ref)
    weighted_rows([across_ref], near_ref.shape[1], scale_ref, part_ref, add=True)
    return as_tile(part_ref[...])


def step_kernel(mine_ref, other_ref, near_ref, far_ref, across_ref, sums_ref, *scratch):
    row_ref, scale_ref, part_ref = scratch
    sums = mine_ref[...] + other_ref[...]
    scale_columns(sums, near_ref, far_ref, across_ref, row_ref, scale_ref)
    sums_ref[...] = next_sums(near_ref, far_ref, across_ref, scale_ref, part_ref)


def split(values):
    high = values.astype(jnp.bfloat16)
    low = (values - high.astype(jnp.float32)).astype(jnp.bfloat16)
    return jnp.concatenate([high, low], axis=0)


def exps_kernel(chunk, rows_ref, *refs):
    *proto_refs, units_ref, pull_ref, sums_ref, exps_ref = refs
    all_rows = rows_ref.shape[0]
    protos = proto_refs[0].shape[0]
    first = pull_ref.shape[0]
    rows_all = rows_ref[...]
    part = jnp.zeros((all_rows, LANES), jnp.float32)
    pull = jnp.zeros((2 * first, pull_ref.shape[1]), jnp.float32)
    for k, proto_ref in enumerate(proto_refs):
        for start in range(0, protos, chunk):
            units = quick_unit(proto_ref[start : start + chunk, :])[0].astype(jnp.bfloat16)
            units_ref[k * protos + start : k * protos + start + chunk, :] = units
            exps_ref[...] = jnp.exp(scores_of(rows_all, units) * (1 / student_temp))
            for at in range(0, chunk, LANES):
                part = part + exps_ref[:, at : at + LANES]
            exps = split(exps_ref[:first, :])
            pull = pull + jnp.dot(exps, units, preferred_element_type=jnp.float32)
    pull_ref[...] = pull[:first] + pull[first:]
    sums_ref[...] = as_tile(part)


def last_kernel(chunk, rows, place_ref, mine_ref, other_ref, near_ref, far_ref, across_ref, *refs):
    units_ref, exp_pull_ref, exp_sums_ref, scale_ref, keep_ref, send_ref, row_ref, blocks_ref = refs
    first = exp_pull_ref.shape[0]
    sums = mine_ref[...] + other_ref[...]
    scale_columns(sums, near_ref, far_ref, across_ref, row_ref, scale_ref)
    pull = jnp.zeros((2 * first, exp_pull_ref.shape[1]), jnp.float32)
    for start in range(0, units_ref.shape[0], chunk):
        at = slice(start, start + chunk)
        scaled = split(near_ref[:first, at] * scale_ref[:1, at])
        pull = pull + jnp.dot(scaled, units_ref[at, :], preferred_element_type=jnp.float32)
    pulls = (pull[:first] + pull[first:], exp_pull_ref[...])
    for k, pull in enumerate(pulls):
        for block in range(4):
            blocks_ref[k, block, :rows, :] = pull[block * rows : (block + 1) * rows]
    mine = place_ref[1]
    for ref, proto in ((keep_ref, mine), (send_ref, mine ^ X)):
        for j, owner in enumerate((proto, proto ^ Y)):
            for k in range(2):
                start = (2 * j + k) * rows
                ref[start : start + rows, :] = blocks_ref[k, block_of(owner), :rows, :]
        ref[4 * rows :, :LANES] = exp_sums_ref[...]
        ref[4 * rows :, LANES:] = jnp.zeros_like(exp_sums_ref)


def last_sums_kernel(near_ref, far_ref, across_ref, scale_ref, sums_ref, part_ref):
    sums_ref[:, :LANES] = jnp.zeros_like(sums_ref[:, :LANES])
    sums_ref[:, LANES:] = next_sums(near_ref, far_ref, across_ref, scale_ref, part_ref)


def own_kernel(place_ref, mine_ref, other_ref, near_rows_ref, far_rows_ref, *refs):
    student_rows_ref, teacher_proto_ref, proto_ref, *refs = refs
    targets_ref, exps_ref, unit_ref, scale_ref = refs
    teacher_rows = jnp.concatenate([near_rows_ref[...], far_rows_ref[...]], axis=0)
    own, all_rows = targets_ref.shape
    row_scale = inverse_rows(mine_ref[...] + other_ref[...], all_rows)
    live = jnp.where(row_scale > 0.0, 1.0, 0.0)
    first = pl.ds(pl.multiple_of(place_ref[0] * own, own), own)
    units = quick_unit(teacher_proto_ref[first, :])[0].astype(jnp.bfloat16)
    weights = jnp.exp(scores_of(units, teacher_rows) * (1 / teacher_temp)) * live
    inverse = 1.0 / jnp.sum(weights * row_scale, axis=1, keepdims=True)
    targets_ref[...] = weights * (inverse * (1 / student_temp))
    unit, scale = quick_unit(proto_ref[first, :])
    unit_ref[...] = unit
    scale_ref[...] = jnp.broadcast_to(scale, scale_ref.shape)
    units = unit.astype(jnp.bfloat16)
    exps = jnp.exp(scores_of(units, student_rows_ref[...]) * (1 / student_temp))
    exps_ref[...] = exps * (1 / student_temp)


def grads_kernel(place_ref, mine_ref, sums_ref, other_ref, targets_ref, exps_ref, *refs):
    unit_ref, scale_ref, rows_ref, feat_ref, student_out_ref, proto_out_ref = refs
    all_rows = targets_ref.shape[1]
    rows = feat_ref.shape[0]
    sums = sums_ref[...] + other_ref[2 * rows :, :]
    target_scale = inverse_rows(sums[:, LANES:], all_rows)
    exp_scale = jnp.where(target_scale > 0.0, 1.0 / unpack_lanes(sums[:, :LANES], all_rows), 0.0)

    grad = exps_ref[...] * exp_scale - targets_ref[...] * target_scale
    pushed = jnp.dot(grad.astype(jnp.bfloat16), rows_ref[...], preferred_element_type=jnp.float32)
    unit = unit_ref[...]
    along = jnp.sum(unit * pushed, axis=1, keepdims=True)
    proto_out_ref[0] = (pushed - unit * along) * twice(scale_ref[...])

    row = lax.broadcasted_iota(jnp.int32, (rows, LANES), 0) + block_of(place_ref[1]) * rows
    here = lax.broadcasted_iota(jnp.int32, (rows, LANES), 1) == row
    target_column, exp_column = [
        jnp.sum(jnp.where(here, scale[:, :LANES], 0.0), axis=1, keepdims=True) * (1 / student_temp)
        for scale in (target_scale, exp_scale)
    ]
    target_pull, exp_pull = [
        mine_ref[k * rows : (k + 1) * rows, :] + other_ref[k * rows : (k + 1) * rows, :]
        for k in range(2)
    ]
    pulled = exp_pull * exp_column - target_pull * target_column
    unit, scale = quick_unit(feat_ref[...])
    student_out_ref[...] = (
        pulled - unit * jnp.sum(unit * pulled, axis=1, keepdims=True)
    ) * scale


def call(kernel, out_shape, operands, smem=0, scratch=(), work=0):
    vmem = pl.BlockSpec(memory_space=pltpu.VMEM)
    return pl.pallas_call(
        kernel,
        out_shape=out_shape,
        in_specs=[pl.BlockSpec(memory_space=pltpu.SMEM)] * smem + [vmem] * (len(operands) - smem),
        out_specs=jax.tree.map(lambda _: vmem, out_shape),
        scratch_shapes=scratch,
        compiler_params=pltpu.CompilerParams(vmem_limit_bytes=24 * 2**20),
        cost_estimate=pl.CostEstimate(
            flops=512 * work, bytes_accessed=4 * work, transcendentals=work
        ),
    )(*operands)


def swap(values, axis, distance):
    others = [(k, k ^ distance) for k in range(lax.axis_size(axis))]
    return lax.ppermute(values, axis, others)


def swap_dp(values, t):
    n_dp, n_proto = lax.axis_size("dp"), lax.axis_size("proto")
    others = [
        (d * n_proto + p, (d ^ t) * n_proto + (p ^ CORE)) for d in range(n_dp) for p in range(n_proto)
    ]
    return lax.ppermute(values, ("dp", "proto"), others)


def on_device_all_rows(student_feat, teacher_feat, prototypes, teacher_prototypes, live_count):
    n_dp, n_proto = lax.axis_size("dp"), lax.axis_size("proto")
    rows, width = student_feat.shape
    protos = prototypes.shape[0]
    own = protos // n_dp
    all_rows = n_dp * n_proto * rows
    half = all_rows // 2
    first = 4 * rows
    held = 2 * protos
    f32 = functools.partial(jax.ShapeDtypeStruct, dtype=jnp.float32)
    bf16 = functools.partial(jax.ShapeDtypeStruct, dtype=jnp.bfloat16)
    place = jnp.stack([lax.axis_index("dp"), lax.axis_index("proto")]).astype(jnp.int32)
    place = jnp.concatenate([place, live_count])
    tile = f32((8, LANES))
    message = f32((4 * rows + 8, width))
    row_scratch = pltpu.VMEM((half, width), jnp.float32)
    column = pltpu.VMEM((all_rows, LANES), jnp.float32)
    scale_row = pltpu.VMEM((8, held), jnp.float32)
    sweep_scratch = [column, pltpu.VMEM((8, 2 * held), jnp.float32), column]

    both = lax.optimization_barrier(jnp.concatenate([teacher_feat, student_feat], axis=0))
    across_x = swap(both, "proto", X_CROSS)
    across_x, late_protos, place = lax.optimization_barrier((across_x, teacher_prototypes, place))
    across_protos = swap(late_protos, "proto", X_CROSS)
    student_protos = (prototypes, swap(prototypes, "proto", CORE))
    teacher_protos = swap(late_protos, "proto", CORE)
    near = jnp.stack([both, across_x])
    near = jnp.stack([near] + [swap_dp(near, t) for t in dp_order(n_dp)[1:]])
    near, own_protos = lax.optimization_barrier((near, teacher_prototypes))
    live = f32((half, LANES))
    teacher_units, near_live, far_live = call(
        functools.partial(units_kernel, n_dp, rows),
        (bf16((protos, width)), live, live),
        (place, own_protos),
        smem=1,
        work=protos * width,
    )
    near = jnp.stack([near, swap(near, "proto", Y_CROSS)])
    near, teacher_units = lax.optimization_barrier((near, teacher_units))
    far = swap(near, "proto", CORE)

    near_weights, near_sums, near_rows, other_units = call(
        functools.partial(near_kernel, own),
        (
            f32((half, held)),
            f32((8, held)),
            bf16((half, width)),
            bf16((protos, width)),
        ),
        (place, near, near_live, teacher_units, teacher_protos),
        smem=1,
        scratch=[row_scratch],
        work=held * half,
    )
    far_weights, far_rows, sums = call(
        functools.partial(far_kernel, own),
        (f32((half, held)), bf16((half, width)), tile),
        (place, far, far_live, near_weights, near_sums, teacher_units, other_units),
        smem=1,
        scratch=[row_scratch, scale_row, column],
        work=held * half,
    )
    sums = sums + swap(sums, "proto", Y_CROSS)
    sums, across_protos = lax.optimization_barrier((sums, across_protos))
    parts = (sums, swap(sums, "proto", X_CROSS))
    across_weights, student_rows = call(
        functools.partial(across_kernel, own),
        (f32((all_rows, held)), bf16((all_rows, width))),
        (
            place,
            near,
            far,
            near_rows,
            far_rows,
            near_live,
            far_live,
            across_protos,
            swap(across_protos, "proto", CORE),
        ),
        smem=1,
        scratch=[row_scratch],
        work=held * all_rows,
    )
    weights = (near_weights, far_weights, across_weights)
    for _ in range(ITERS - 2):
        sums = call(
            step_kernel,
            tile,
            (*parts, *weights),
            scratch=sweep_scratch,
            work=held * all_rows,
        )
        sums, student_rows, *student_protos = lax.optimization_barrier(
            (sums, student_rows, *student_protos)
        )
        parts = (sums, swap(sums, "proto", Y_CROSS))
    student_units, exp_pull, exp_sums = call(
        functools.partial(exps_kernel, own),
        (bf16((held, width)), f32((first, width)), tile),
        (student_rows, *student_protos),
        scratch=[pltpu.VMEM((all_rows, own), jnp.float32)],
        work=held * all_rows,
    )
    scales, keep, send = call(
        functools.partial(last_kernel, own, rows),
        (f32((8, 2 * held)), message, message),
        (place, *parts, *weights, student_units, exp_pull, exp_sums),
        smem=1,
        scratch=[column, pltpu.VMEM((2, 4, 16, width), jnp.float32)],
        work=held * all_rows,
    )
    last_sums = call(
        last_sums_kernel,
        f32((8, width)),
        (*weights, scales),
        scratch=[column],
        work=held * all_rows,
    )
    *parts, send = lax.optimization_barrier((*parts, send))
    targets, exps, own_units, own_scales = call(
        own_kernel,
        (f32((own, all_rows)), f32((own, all_rows)), f32((own, width)), f32((own, LANES))),
        (place, *parts, near_rows, far_rows, student_rows, teacher_prototypes, prototypes),
        smem=1,
        work=own * all_rows,
    )
    total = keep + swap(send, "proto", X_CROSS)
    last_sums = total[4 * rows :] + last_sums
    return call(
        grads_kernel,
        (f32((rows, width)), f32((1, own, width))),
        (
            place,
            total,
            last_sums,
            swap(jnp.concatenate([total[2 * rows : 4 * rows], last_sums]), "proto", Y_CROSS),
            targets,
            exps,
            own_units,
            own_scales,
            student_rows,
            student_feat,
        ),
        smem=1,
        work=own * all_rows,
    )


def sample_totals(values):
    return lax.psum(values, "proto")


def proto_totals(values):
    return lax.psum(values, "dp")


def on_device_group_rows(student_feat, teacher_feat, prototypes, teacher_prototypes, live_count):
    student_unit, student_length = unit_rows(student_feat)
    teacher_unit, teacher_length = unit_rows(teacher_feat)
    proto_unit, proto_length = unit_rows(prototypes)
    teacher_proto, teacher_proto_length = unit_rows(teacher_prototypes)
    proto_bf = proto_unit.astype(jnp.bfloat16)
    teacher_proto_bf = teacher_proto.astype(jnp.bfloat16)
    student_rows, teacher_rows = (
        lax.all_gather(student_unit.astype(jnp.bfloat16), "proto", axis=0, tiled=True),
        lax.all_gather(teacher_unit.astype(jnp.bfloat16), "proto", axis=0, tiled=True),
    )
    group_size = student_rows.shape[0]
    live_rows = live_count[lax.axis_index("dp")]
    live_mask = jnp.arange(group_size, dtype=jnp.int32) < live_rows
    live_column = live_mask[:, None]
    contract_last = (((1,), (1,)), ((), ()))
    logits = (
        lax.dot_general(student_rows, proto_bf, contract_last, preferred_element_type=jnp.float32)
        / student_temp
    )
    teacher_scores = (
        lax.dot_general(
            teacher_rows, teacher_proto_bf, contract_last, preferred_element_type=jnp.float32
        )
        / teacher_temp
    )
    weights = jnp.where(live_column, jnp.exp(teacher_scores), 0.0)
    partition = sample_totals(jnp.sum(jnp.exp(logits), axis=1))
    targets = weights
    for iteration in range(ITERS):
        targets = targets / proto_totals(jnp.sum(targets, axis=0))[None, :]
        row_sums = sample_totals(jnp.sum(targets, axis=1))
        targets = targets / jnp.where(live_mask, row_sums, 1.0)[:, None]
    student_probs = jnp.exp(logits - jnp.log(partition)[:, None])
    grad_block = jnp.where(live_column, (student_probs - targets) / student_temp, 0.0).astype(
        jnp.bfloat16
    )
    pulled = lax.psum_scatter(
        jnp.dot(grad_block, proto_bf, preferred_element_type=jnp.float32),
        "proto",
        scatter_dimension=0,
        tiled=True,
    )
    student_grad = (
        pulled - student_unit * jnp.sum(student_unit * pulled, axis=1, keepdims=True)
    ) / student_length
    own_protos = prototypes.shape[0] // lax.axis_size("dp")
    contract_first = (((0,), (0,)), ((), ()))
    pushed = lax.psum_scatter(
        lax.dot_general(
            grad_block, student_rows, contract_first, preferred_element_type=jnp.float32
        ),
        "dp",
        scatter_dimension=0,
        tiled=True,
    )
    first_proto = lax.axis_index("dp") * own_protos
    own_units = lax.dynamic_slice_in_dim(proto_unit, first_proto, own_protos, 0)
    own_lengths = lax.dynamic_slice_in_dim(proto_length, first_proto, own_protos, 0)
    proto_grad = (
        pushed - own_units * jnp.sum(own_units * pushed, axis=1, keepdims=True)
    ) / own_lengths
    return (student_grad, proto_grad[None])


def on_device(student_feat, teacher_feat, prototypes, teacher_prototypes, live_count):
    n_dp, n_proto = lax.axis_size("dp"), lax.axis_size("proto")
    rows, width = student_feat.shape
    protos = prototypes.shape[0]
    lanes = n_dp * n_proto * rows
    fits = (
        n_proto == 2 * Y
        and n_dp & (n_dp - 1) == 0
        and rows % 4 == 0
        and rows <= 16
        and lanes % LANES == 0
        and lanes <= 8 * LANES
        and width == 2 * LANES
        and protos == n_dp * 2 * LANES
        and 4 * protos * lanes * 4 <= BLOCK_BYTES
    )
    plan = on_device_all_rows if fits else on_device_group_rows
    return plan(student_feat, teacher_feat, prototypes, teacher_prototypes, live_count)


def solution(mesh):
    return jax.shard_map(
        on_device,
        mesh=mesh,
        in_specs=(
            P(("dp", "proto"), None),
            P(("dp", "proto"), None),
            P("proto", None),
            P("proto", None),
            P(),
        ),
        out_specs=(P(("dp", "proto"), None), P("proto", "dp", None)),
        check_vma=False,
    )
```

```python
import functools

import jax
import jax.numpy as jnp
from jax import lax
from jax.experimental import pallas as pl
from jax.experimental.pallas import tpu as pltpu
from jax.sharding import PartitionSpec as P

ITERS = 3

student_temp = 0.1
teacher_temp = 0.07
eps_norm = 1e-06

LANES = 128
BLOCK_BYTES = 8 * 2**20


def unit_rows(values):
    widened = values.astype(jnp.float32)
    length = jnp.sqrt(jnp.sum(widened * widened, axis=1, keepdims=True) + eps_norm)
    return (widened / length, length)


CORE, X, Y = 1, 2, 4
X_CROSS, Y_CROSS = X | CORE, Y | CORE


def block_of(proto):
    return (proto & X) + ((proto >> 2) & 1)


def quick_unit(values):
    widened = values.astype(jnp.float32)
    squares = jnp.sum(widened * widened, axis=1, keepdims=True) + eps_norm
    scale = lax.rsqrt(squares)
    return widened * scale, scale


def dp_order(n_dp):
    return [0, *reversed(range(1, n_dp))]


def live_lanes(place_ref, half, lanes, n_dp, rows):
    mine = place_ref[1]
    parity = (mine ^ (mine >> 1) ^ (mine >> 2)) & 1
    lane = lax.broadcasted_iota(jnp.int32, (1, lanes), 1)
    live = jnp.zeros((1, lanes), jnp.float32)
    start = 0
    for t in dp_order(n_dp):
        count = place_ref[2 + (place_ref[0] ^ t)]
        for x in range(2):
            for y in range(2):
                core = parity ^ x ^ y ^ half ^ (1 if t else 0)
                proto = core + X * x + Y * y
                end = start + jnp.clip(count - proto * rows, 0, rows)
                live = jnp.where((lane >= start) & (lane < end), 1.0, live)
                start += rows
    return live


def pack_lanes(values):
    pieces = [values[:, k : k + LANES] for k in range(0, values.shape[1], LANES)]
    return jnp.concatenate(pieces + [jnp.zeros((8 - len(pieces), LANES), jnp.float32)], axis=0)


def unpack_lanes(tile, lanes):
    return jnp.concatenate([tile[k : k + 1, :] for k in range(lanes // LANES)], axis=1)


def as_column(values):
    return jnp.broadcast_to(values, (LANES, values.shape[1])).T


def as_tile(partial):
    return pack_lanes(jnp.sum(partial.T, axis=0, keepdims=True))


def inverse_rows(tile, rows):
    total = unpack_lanes(tile, rows)
    live = total > 0.0
    return jnp.where(live, 1.0 / jnp.where(live, total, 1.0), 0.0)


def place_rows(place_ref, ref, which, rows, scratch):
    mine_x, mine_y = (place_ref[1] >> 1) & 1, (place_ref[1] >> 2) & 1
    start = 0
    for t in range(ref.shape[1]):
        for x in range(2):
            for y in range(2):
                block = ref[mine_y ^ y, t, mine_x ^ x].astype(jnp.float32)
                scratch[start : start + rows, :] = block[which * rows : (which + 1) * rows]
                start += rows
    unit, _ = quick_unit(scratch[...])
    return unit.astype(jnp.bfloat16)


def scores_of(rows_all, units):
    return lax.dot_general(
        rows_all, units, (((1,), (1,)), ((), ())), preferred_element_type=jnp.float32
    )


def twice(column):
    return jnp.concatenate([column, column], axis=1)


def spread(column, lanes):
    return jnp.concatenate([column] * (lanes // LANES), axis=1)


def weighted_rows(panels, left, scale_ref, part_ref, add=False):
    tiles = panels[0].shape[1] // LANES
    scales = [scale_ref[:, left + k * LANES : left + (k + 1) * LANES] for k in range(tiles)]
    top = 0
    for ref in panels:

        def body(i, _, ref=ref, top=top):
            at = pl.ds(pl.multiple_of(i * 8, 8), 8)
            to = pl.ds(pl.multiple_of(i * 8 + top, 8), 8)
            sums = [None] * 4
            for k in range(tiles):
                term = ref[at, k * LANES : (k + 1) * LANES] * scales[k]
                sums[k % 4] = term if sums[k % 4] is None else sums[k % 4] + term
            total = (sums[0] + sums[1]) + (sums[2] + sums[3])
            part_ref[to, :] = part_ref[to, :] + total if add else total
            return 0

        lax.fori_loop(0, ref.shape[0] // 8, body, 0, unroll=8)
        top += ref.shape[0]


def column_scales(panels, left, row_ref, scale_ref):
    tiles = panels[0].shape[1] // LANES
    sums = [jnp.zeros((8, LANES), jnp.float32)] * tiles
    top = 0
    for ref in panels:

        def body(i, sums, ref=ref, top=top):
            at = pl.ds(pl.multiple_of(i * 8, 8), 8)
            row = row_ref[pl.ds(pl.multiple_of(i * 8 + top, 8), 8), :]
            return [
                total + ref[at, k * LANES : (k + 1) * LANES] * row for k, total in enumerate(sums)
            ]

        sums = lax.fori_loop(0, ref.shape[0] // 8, body, sums, unroll=8)
        top += ref.shape[0]
    for k, total in enumerate(sums):
        inverse = 1.0 / jnp.sum(total, axis=0, keepdims=True)
        at = slice(left + k * LANES, left + (k + 1) * LANES)
        scale_ref[:, at] = jnp.broadcast_to(inverse, (8, LANES))


def weights_of(rows, units, live):
    weights = jnp.exp(scores_of(rows, units) * (1 / teacher_temp)) * live
    return weights, fold(weights)


def fold(values):
    return jnp.sum(values.reshape(values.shape[0] // 8, 8, values.shape[1]), axis=0)


def units_kernel(n_dp, rows, place_ref, proto_ref, units_ref, *live_refs):
    units_ref[...] = quick_unit(proto_ref[...])[0].astype(jnp.bfloat16)
    for k, live_ref in enumerate(live_refs):
        live_ref[...] = as_column(live_lanes(place_ref, k, live_ref.shape[0], n_dp, rows))


def near_kernel(chunk, place_ref, near_ref, live_ref, own_units_ref, proto_ref, *refs):
    weights_ref, sums_ref, rows_ref, units_ref, scratch = refs
    rows = near_ref.shape[3] // 2
    rows_near = place_rows(place_ref, near_ref, 0, rows, scratch)
    rows_ref[...] = rows_near
    live = spread(live_ref[...], chunk)
    protos = own_units_ref.shape[0]
    for start in range(0, 2 * protos, chunk):
        at = slice(start, start + chunk)
        if start < protos:
            units = own_units_ref[at, :]
        else:
            here = slice(start - protos, start - protos + chunk)
            units = quick_unit(proto_ref[here, :])[0].astype(jnp.bfloat16)
            units_ref[here, :] = units
        weights_ref[:, at], sums_ref[:, at] = weights_of(rows_near, units, live)


def far_kernel(chunk, place_ref, far_ref, live_ref, near_weights_ref, near_sums_ref, *refs):
    *unit_refs, weights_ref, rows_ref, sums_ref, scratch, scale_ref, part_ref = refs
    rows = far_ref.shape[3] // 2
    rows_far = place_rows(place_ref, far_ref, 0, rows, scratch)
    rows_ref[...] = rows_far
    live = spread(live_ref[...], chunk)
    protos = unit_refs[0].shape[0]
    for k, unit_ref in enumerate(unit_refs):
        for start in range(0, protos, chunk):
            at = slice(k * protos + start, k * protos + start + chunk)
            weights, sums = weights_of(rows_far, unit_ref[start : start + chunk, :], live)
            weights_ref[:, at] = weights
            inverse = 1.0 / jnp.sum(near_sums_ref[:, at] + sums, axis=0, keepdims=True)
            scale_ref[:, at] = jnp.broadcast_to(inverse, (8, chunk))
    weighted_rows([near_weights_ref, weights_ref], 0, scale_ref, part_ref)
    sums_ref[...] = as_tile(part_ref[...])


def across_kernel(chunk, place_ref, near_ref, far_ref, *refs):
    near_rows_ref, far_rows_ref, near_live_ref, far_live_ref, *refs = refs
    *proto_refs, weights_ref, student_ref, scratch = refs
    protos = proto_refs[0].shape[0]
    rows_all = jnp.concatenate([near_rows_ref[...], far_rows_ref[...]], axis=0)
    live = spread(jnp.concatenate([near_live_ref[...], far_live_ref[...]], axis=0), chunk)
    for k, proto_ref in enumerate(proto_refs):
        for start in range(0, protos, chunk):
            units = quick_unit(proto_ref[start : start + chunk, :])[0].astype(jnp.bfloat16)
            at = slice(k * protos + start, k * protos + start + chunk)
            weights_ref[:, at], _ = weights_of(rows_all, units, live)
    half = student_ref.shape[0] // 2
    for k, ref in enumerate((near_ref, far_ref)):
        rows_half = place_rows(place_ref, ref, 1, ref.shape[3] // 2, scratch)
        student_ref[k * half : (k + 1) * half, :] = rows_half


def scale_columns(sums, near_ref, far_ref, across_ref, row_ref, scale_ref):
    row_ref[...] = as_column(inverse_rows(sums, row_ref.shape[0]))
    column_scales([near_ref, far_ref], 0, row_ref, scale_ref)
    column_scales([across_ref], near_ref.shape[1], row_ref, scale_ref)


def next_sums(near_ref, far_ref, across_ref, scale_ref, part_ref):
    weighted_rows([near_ref, far_ref], 0, scale_ref, part_ref)
    weighted_rows([across_ref], near_ref.shape[1], scale_ref, part_ref, add=True)
    return as_tile(part_ref[...])


def step_kernel(mine_ref, other_ref, near_ref, far_ref, across_ref, sums_ref, *scratch):
    row_ref, scale_ref, part_ref = scratch
    sums = mine_ref[...] + other_ref[...]
    scale_columns(sums, near_ref, far_ref, across_ref, row_ref, scale_ref)
    sums_ref[...] = next_sums(near_ref, far_ref, across_ref, scale_ref, part_ref)


def split(values):
    high = values.astype(jnp.bfloat16)
    low = (values - high.astype(jnp.float32)).astype(jnp.bfloat16)
    return jnp.concatenate([high, low], axis=0)


def exps_kernel(chunk, rows_ref, *refs):
    *proto_refs, units_ref, pull_ref, sums_ref, exps_ref = refs
    all_rows = rows_ref.shape[0]
    protos = proto_refs[0].shape[0]
    first = pull_ref.shape[0]
    rows_all = rows_ref[...]
    part = jnp.zeros((all_rows, LANES), jnp.float32)
    pull = jnp.zeros((2 * first, pull_ref.shape[1]), jnp.float32)
    for k, proto_ref in enumerate(proto_refs):
        for start in range(0, protos, chunk):
            units = quick_unit(proto_ref[start : start + chunk, :])[0].astype(jnp.bfloat16)
            units_ref[k * protos + start : k * protos + start + chunk, :] = units
            exps_ref[...] = jnp.exp(scores_of(rows_all, units) * (1 / student_temp))
            for at in range(0, chunk, LANES):
                part = part + exps_ref[:, at : at + LANES]
            exps = split(exps_ref[:first, :])
            pull = pull + jnp.dot(exps, units, preferred_element_type=jnp.float32)
    pull_ref[...] = pull[:first] + pull[first:]
    sums_ref[...] = as_tile(part)


def last_kernel(chunk, rows, place_ref, mine_ref, other_ref, near_ref, far_ref, across_ref, *refs):
    units_ref, exp_pull_ref, exp_sums_ref, scale_ref, keep_ref, send_ref, row_ref, blocks_ref = refs
    first = exp_pull_ref.shape[0]
    sums = mine_ref[...] + other_ref[...]
    scale_columns(sums, near_ref, far_ref, across_ref, row_ref, scale_ref)
    pull = jnp.zeros((2 * first, exp_pull_ref.shape[1]), jnp.float32)
    for start in range(0, units_ref.shape[0], chunk):
        at = slice(start, start + chunk)
        scaled = split(near_ref[:first, at] * scale_ref[:1, at])
        pull = pull + jnp.dot(scaled, units_ref[at, :], preferred_element_type=jnp.float32)
    pulls = (pull[:first] + pull[first:], exp_pull_ref[...])
    for k, pull in enumerate(pulls):
        for block in range(4):
            blocks_ref[k, block, :rows, :] = pull[block * rows : (block + 1) * rows]
    mine = place_ref[1]
    for ref, proto in ((keep_ref, mine), (send_ref, mine ^ X)):
        for j, owner in enumerate((proto, proto ^ Y)):
            for k in range(2):
                start = (2 * j + k) * rows
                ref[start : start + rows, :] = blocks_ref[k, block_of(owner), :rows, :]
        ref[4 * rows :, :LANES] = exp_sums_ref[...]
        ref[4 * rows :, LANES:] = jnp.zeros_like(exp_sums_ref)


def last_sums_kernel(near_ref, far_ref, across_ref, scale_ref, sums_ref, part_ref):
    sums_ref[:, :LANES] = jnp.zeros_like(sums_ref[:, :LANES])
    sums_ref[:, LANES:] = next_sums(near_ref, far_ref, across_ref, scale_ref, part_ref)


def own_kernel(place_ref, mine_ref, other_ref, near_rows_ref, far_rows_ref, *refs):
    student_rows_ref, teacher_proto_ref, proto_ref, *refs = refs
    targets_ref, exps_ref, unit_ref, scale_ref = refs
    teacher_rows = jnp.concatenate([near_rows_ref[...], far_rows_ref[...]], axis=0)
    own, all_rows = targets_ref.shape
    row_scale = inverse_rows(mine_ref[...] + other_ref[...], all_rows)
    live = jnp.where(row_scale > 0.0, 1.0, 0.0)
    first = pl.ds(pl.multiple_of(place_ref[0] * own, own), own)
    units = quick_unit(teacher_proto_ref[first, :])[0].astype(jnp.bfloat16)
    weights = jnp.exp(scores_of(units, teacher_rows) * (1 / teacher_temp)) * live
    inverse = 1.0 / jnp.sum(weights * row_scale, axis=1, keepdims=True)
    targets_ref[...] = weights * (inverse * (1 / student_temp))
    unit, scale = quick_unit(proto_ref[first, :])
    unit_ref[...] = unit
    scale_ref[...] = jnp.broadcast_to(scale, scale_ref.shape)
    units = unit.astype(jnp.bfloat16)
    exps = jnp.exp(scores_of(units, student_rows_ref[...]) * (1 / student_temp))
    exps_ref[...] = exps * (1 / student_temp)


def grads_kernel(place_ref, mine_ref, sums_ref, other_ref, targets_ref, exps_ref, *refs):
    unit_ref, scale_ref, rows_ref, feat_ref, student_out_ref, proto_out_ref = refs
    all_rows = targets_ref.shape[1]
    rows = feat_ref.shape[0]
    sums = sums_ref[...] + other_ref[2 * rows :, :]
    target_scale = inverse_rows(sums[:, LANES:], all_rows)
    exp_scale = jnp.where(target_scale > 0.0, 1.0 / unpack_lanes(sums[:, :LANES], all_rows), 0.0)

    grad = exps_ref[...] * exp_scale - targets_ref[...] * target_scale
    pushed = jnp.dot(grad.astype(jnp.bfloat16), rows_ref[...], preferred_element_type=jnp.float32)
    unit = unit_ref[...]
    along = jnp.sum(unit * pushed, axis=1, keepdims=True)
    proto_out_ref[0] = (pushed - unit * along) * twice(scale_ref[...])

    row = lax.broadcasted_iota(jnp.int32, (rows, LANES), 0) + block_of(place_ref[1]) * rows
    here = lax.broadcasted_iota(jnp.int32, (rows, LANES), 1) == row
    target_column, exp_column = [
        jnp.sum(jnp.where(here, scale[:, :LANES], 0.0), axis=1, keepdims=True) * (1 / student_temp)
        for scale in (target_scale, exp_scale)
    ]
    target_pull, exp_pull = [
        mine_ref[k * rows : (k + 1) * rows, :] + other_ref[k * rows : (k + 1) * rows, :]
        for k in range(2)
    ]
    pulled = exp_pull * exp_column - target_pull * target_column
    unit, scale = quick_unit(feat_ref[...])
    student_out_ref[...] = (
        pulled - unit * jnp.sum(unit * pulled, axis=1, keepdims=True)
    ) * scale


def call(kernel, out_shape, operands, smem=0, scratch=(), work=0):
    vmem = pl.BlockSpec(memory_space=pltpu.VMEM)
    return pl.pallas_call(
        kernel,
        out_shape=out_shape,
        in_specs=[pl.BlockSpec(memory_space=pltpu.SMEM)] * smem + [vmem] * (len(operands) - smem),
        out_specs=jax.tree.map(lambda _: vmem, out_shape),
        scratch_shapes=scratch,
        compiler_params=pltpu.CompilerParams(vmem_limit_bytes=24 * 2**20),
        cost_estimate=pl.CostEstimate(
            flops=512 * work, bytes_accessed=4 * work, transcendentals=work
        ),
    )(*operands)


def swap(values, axis, distance):
    others = [(k, k ^ distance) for k in range(lax.axis_size(axis))]
    return lax.ppermute(values, axis, others)


def swap_dp(values, t):
    n_dp, n_proto = lax.axis_size("dp"), lax.axis_size("proto")
    others = [
        (d * n_proto + p, (d ^ t) * n_proto + (p ^ CORE)) for d in range(n_dp) for p in range(n_proto)
    ]
    return lax.ppermute(values, ("dp", "proto"), others)


def on_device_all_rows(student_feat, teacher_feat, prototypes, teacher_prototypes, live_count):
    n_dp, n_proto = lax.axis_size("dp"), lax.axis_size("proto")
    rows, width = student_feat.shape
    protos = prototypes.shape[0]
    own = protos // n_dp
    piece = 2 * own
    all_rows = n_dp * n_proto * rows
    half = all_rows // 2
    first = 4 * rows
    held = 2 * protos
    f32 = functools.partial(jax.ShapeDtypeStruct, dtype=jnp.float32)
    bf16 = functools.partial(jax.ShapeDtypeStruct, dtype=jnp.bfloat16)
    place = jnp.stack([lax.axis_index("dp"), lax.axis_index("proto")]).astype(jnp.int32)
    place = jnp.concatenate([place, live_count])
    tile = f32((8, LANES))
    message = f32((4 * rows + 8, width))
    row_scratch = pltpu.VMEM((half, width), jnp.float32)
    column = pltpu.VMEM((all_rows, LANES), jnp.float32)
    scale_row = pltpu.VMEM((8, held), jnp.float32)
    sweep_scratch = [column, pltpu.VMEM((8, 2 * held), jnp.float32), column]

    both = lax.optimization_barrier(jnp.concatenate([teacher_feat, student_feat], axis=0))
    across_x = swap(both, "proto", X_CROSS)
    across_x, late_protos, place = lax.optimization_barrier((across_x, teacher_prototypes, place))
    across_protos = swap(late_protos, "proto", X_CROSS)
    student_protos = (prototypes, swap(prototypes, "proto", CORE))
    teacher_protos = swap(late_protos, "proto", CORE)
    near = jnp.stack([both, across_x])
    near = jnp.stack([near] + [swap_dp(near, t) for t in dp_order(n_dp)[1:]])
    near, own_protos = lax.optimization_barrier((near, teacher_prototypes))
    live = f32((half, LANES))
    teacher_units, near_live, far_live = call(
        functools.partial(units_kernel, n_dp, rows),
        (bf16((protos, width)), live, live),
        (place, own_protos),
        smem=1,
        work=protos * width,
    )
    near = jnp.stack([near, swap(near, "proto", Y_CROSS)])
    near, teacher_units = lax.optimization_barrier((near, teacher_units))
    far = swap(near, "proto", CORE)

    near_weights, near_sums, near_rows, other_units = call(
        functools.partial(near_kernel, piece),
        (
            f32((half, held)),
            f32((8, held)),
            bf16((half, width)),
            bf16((protos, width)),
        ),
        (place, near, near_live, teacher_units, teacher_protos),
        smem=1,
        scratch=[row_scratch],
        work=held * half,
    )
    far_weights, far_rows, sums = call(
        functools.partial(far_kernel, piece),
        (f32((half, held)), bf16((half, width)), tile),
        (place, far, far_live, near_weights, near_sums, teacher_units, other_units),
        smem=1,
        scratch=[row_scratch, scale_row, column],
        work=held * half,
    )
    sums = sums + swap(sums, "proto", Y_CROSS)
    sums, across_protos = lax.optimization_barrier((sums, across_protos))
    parts = (sums, swap(sums, "proto", X_CROSS))
    across_weights, student_rows = call(
        functools.partial(across_kernel, piece),
        (f32((all_rows, held)), bf16((all_rows, width))),
        (
            place,
            near,
            far,
            near_rows,
            far_rows,
            near_live,
            far_live,
            across_protos,
            swap(across_protos, "proto", CORE),
        ),
        smem=1,
        scratch=[row_scratch],
        work=held * all_rows,
    )
    weights = (near_weights, far_weights, across_weights)
    for _ in range(ITERS - 2):
        sums = call(
            step_kernel,
            tile,
            (*parts, *weights),
            scratch=sweep_scratch,
            work=held * all_rows,
        )
        sums, student_rows, *student_protos = lax.optimization_barrier(
            (sums, student_rows, *student_protos)
        )
        parts = (sums, swap(sums, "proto", Y_CROSS))
    student_units, exp_pull, exp_sums = call(
        functools.partial(exps_kernel, piece),
        (bf16((held, width)), f32((first, width)), tile),
        (student_rows, *student_protos),
        scratch=[pltpu.VMEM((all_rows, piece), jnp.float32)],
        work=held * all_rows,
    )
    scales, keep, send = call(
        functools.partial(last_kernel, own, rows),
        (f32((8, 2 * held)), message, message),
        (place, *parts, *weights, student_units, exp_pull, exp_sums),
        smem=1,
        scratch=[column, pltpu.VMEM((2, 4, 16, width), jnp.float32)],
        work=held * all_rows,
    )
    last_sums = call(
        last_sums_kernel,
        f32((8, width)),
        (*weights, scales),
        scratch=[column],
        work=held * all_rows,
    )
    *parts, send = lax.optimization_barrier((*parts, send))
    targets, exps, own_units, own_scales = call(
        own_kernel,
        (f32((own, all_rows)), f32((own, all_rows)), f32((own, width)), f32((own, LANES))),
        (place, *parts, near_rows, far_rows, student_rows, teacher_prototypes, prototypes),
        smem=1,
        work=own * all_rows,
    )
    total = keep + swap(send, "proto", X_CROSS)
    last_sums = total[4 * rows :] + last_sums
    return call(
        grads_kernel,
        (f32((rows, width)), f32((1, own, width))),
        (
            place,
            total,
            last_sums,
            swap(jnp.concatenate([total[2 * rows : 4 * rows], last_sums]), "proto", Y_CROSS),
            targets,
            exps,
            own_units,
            own_scales,
            student_rows,
            student_feat,
        ),
        smem=1,
        work=own * all_rows,
    )


def sample_totals(values):
    return lax.psum(values, "proto")


def proto_totals(values):
    return lax.psum(values, "dp")


def on_device_group_rows(student_feat, teacher_feat, prototypes, teacher_prototypes, live_count):
    student_unit, student_length = unit_rows(student_feat)
    teacher_unit, teacher_length = unit_rows(teacher_feat)
    proto_unit, proto_length = unit_rows(prototypes)
    teacher_proto, teacher_proto_length = unit_rows(teacher_prototypes)
    proto_bf = proto_unit.astype(jnp.bfloat16)
    teacher_proto_bf = teacher_proto.astype(jnp.bfloat16)
    student_rows, teacher_rows = (
        lax.all_gather(student_unit.astype(jnp.bfloat16), "proto", axis=0, tiled=True),
        lax.all_gather(teacher_unit.astype(jnp.bfloat16), "proto", axis=0, tiled=True),
    )
    group_size = student_rows.shape[0]
    live_rows = live_count[lax.axis_index("dp")]
    live_mask = jnp.arange(group_size, dtype=jnp.int32) < live_rows
    live_column = live_mask[:, None]
    contract_last = (((1,), (1,)), ((), ()))
    logits = (
        lax.dot_general(student_rows, proto_bf, contract_last, preferred_element_type=jnp.float32)
        / student_temp
    )
    teacher_scores = (
        lax.dot_general(
            teacher_rows, teacher_proto_bf, contract_last, preferred_element_type=jnp.float32
        )
        / teacher_temp
    )
    weights = jnp.where(live_column, jnp.exp(teacher_scores), 0.0)
    partition = sample_totals(jnp.sum(jnp.exp(logits), axis=1))
    targets = weights
    for iteration in range(ITERS):
        targets = targets / proto_totals(jnp.sum(targets, axis=0))[None, :]
        row_sums = sample_totals(jnp.sum(targets, axis=1))
        targets = targets / jnp.where(live_mask, row_sums, 1.0)[:, None]
    student_probs = jnp.exp(logits - jnp.log(partition)[:, None])
    grad_block = jnp.where(live_column, (student_probs - targets) / student_temp, 0.0).astype(
        jnp.bfloat16
    )
    pulled = lax.psum_scatter(
        jnp.dot(grad_block, proto_bf, preferred_element_type=jnp.float32),
        "proto",
        scatter_dimension=0,
        tiled=True,
    )
    student_grad = (
        pulled - student_unit * jnp.sum(student_unit * pulled, axis=1, keepdims=True)
    ) / student_length
    own_protos = prototypes.shape[0] // lax.axis_size("dp")
    contract_first = (((0,), (0,)), ((), ()))
    pushed = lax.psum_scatter(
        lax.dot_general(
            grad_block, student_rows, contract_first, preferred_element_type=jnp.float32
        ),
        "dp",
        scatter_dimension=0,
        tiled=True,
    )
    first_proto = lax.axis_index("dp") * own_protos
    own_units = lax.dynamic_slice_in_dim(proto_unit, first_proto, own_protos, 0)
    own_lengths = lax.dynamic_slice_in_dim(proto_length, first_proto, own_protos, 0)
    proto_grad = (
        pushed - own_units * jnp.sum(own_units * pushed, axis=1, keepdims=True)
    ) / own_lengths
    return (student_grad, proto_grad[None])


def on_device(student_feat, teacher_feat, prototypes, teacher_prototypes, live_count):
    n_dp, n_proto = lax.axis_size("dp"), lax.axis_size("proto")
    rows, width = student_feat.shape
    protos = prototypes.shape[0]
    lanes = n_dp * n_proto * rows
    fits = (
        n_proto == 2 * Y
        and n_dp & (n_dp - 1) == 0
        and rows % 4 == 0
        and rows <= 16
        and lanes % LANES == 0
        and lanes <= 8 * LANES
        and width == 2 * LANES
        and protos == n_dp * 2 * LANES
        and 4 * protos * lanes * 4 <= BLOCK_BYTES
    )
    plan = on_device_all_rows if fits else on_device_group_rows
    return plan(student_feat, teacher_feat, prototypes, teacher_prototypes, live_count)


def solution(mesh):
    return jax.shard_map(
        on_device,
        mesh=mesh,
        in_specs=(
            P(("dp", "proto"), None),
            P(("dp", "proto"), None),
            P("proto", None),
            P("proto", None),
            P(),
        ),
        out_specs=(P(("dp", "proto"), None), P("proto", "dp", None)),
        check_vma=False,
    )
```

```python
import functools

import jax
import jax.numpy as jnp
from jax import lax
from jax.experimental import pallas as pl
from jax.experimental.pallas import tpu as pltpu
from jax.sharding import PartitionSpec as P

ITERS = 3

student_temp = 0.1
teacher_temp = 0.07
eps_norm = 1e-06

LANES = 128
BLOCK_BYTES = 8 * 2**20


def unit_rows(values):
    widened = values.astype(jnp.float32)
    length = jnp.sqrt(jnp.sum(widened * widened, axis=1, keepdims=True) + eps_norm)
    return (widened / length, length)


CORE, X, Y = 1, 2, 4
X_CROSS, Y_CROSS = X | CORE, Y | CORE


def block_of(proto):
    return 2 * ((proto >> 2) & 1) + ((proto >> 1) & 1)


def quick_unit(values):
    widened = values.astype(jnp.float32)
    squares = jnp.sum(widened * widened, axis=1, keepdims=True) + eps_norm
    scale = lax.rsqrt(squares)
    return widened * scale, scale


def dp_order(n_dp):
    return [0, *reversed(range(1, n_dp))]


def live_lanes(place_ref, half, lanes, n_dp, rows):
    mine = place_ref[1]
    parity = (mine ^ (mine >> 1) ^ (mine >> 2)) & 1
    lane = lax.broadcasted_iota(jnp.int32, (1, lanes), 1)
    live = jnp.zeros((1, lanes), jnp.float32)
    start = 0
    for t in dp_order(n_dp):
        count = place_ref[2 + (place_ref[0] ^ t)]
        for y in range(2):
            for x in range(2):
                core = parity ^ x ^ y ^ half ^ (1 if t else 0)
                proto = core + X * x + Y * y
                end = start + jnp.clip(count - proto * rows, 0, rows)
                live = jnp.where((lane >= start) & (lane < end), 1.0, live)
                start += rows
    return live


def pack_lanes(values):
    pieces = [values[:, k : k + LANES] for k in range(0, values.shape[1], LANES)]
    return jnp.concatenate(pieces + [jnp.zeros((8 - len(pieces), LANES), jnp.float32)], axis=0)


def unpack_lanes(tile, lanes):
    return jnp.concatenate([tile[k : k + 1, :] for k in range(lanes // LANES)], axis=1)


def as_column(values):
    return jnp.broadcast_to(values, (LANES, values.shape[1])).T


def as_tile(partial):
    return pack_lanes(jnp.sum(partial.T, axis=0, keepdims=True))


def inverse_rows(tile, rows):
    total = unpack_lanes(tile, rows)
    live = total > 0.0
    return jnp.where(live, 1.0 / jnp.where(live, total, 1.0), 0.0)


def pair_kernel(place_ref, mine_ref, other_ref, out_ref, scratch):
    rows = mine_ref.shape[0] // 2
    swapped = (place_ref[1] & X) > 0
    mine, other = [quick_unit(ref[...])[0] for ref in (mine_ref, other_ref)]
    pair = (jnp.where(swapped, other, mine), jnp.where(swapped, mine, other))
    for which in range(2):
        for x in range(2):
            start = (2 * which + x) * rows
            scratch[start : start + rows, :] = pair[x][which * rows : (which + 1) * rows]
    out_ref[...] = scratch[...].astype(jnp.bfloat16)


def place_rows(place_ref, ref, which):
    mine_y = (place_ref[1] >> 2) & 1
    pair = ref.shape[2] // 2
    blocks = [
        ref[mine_y ^ y, t].astype(jnp.float32)[which * pair : (which + 1) * pair]
        for t in range(ref.shape[1])
        for y in range(2)
    ]
    return jnp.concatenate(blocks, axis=0).astype(jnp.bfloat16)


def scores_of(rows_all, units):
    return lax.dot_general(
        rows_all, units, (((1,), (1,)), ((), ())), preferred_element_type=jnp.float32
    )


def twice(column):
    return jnp.concatenate([column, column], axis=1)


def spread(column, lanes):
    return jnp.concatenate([column] * (lanes // LANES), axis=1)


def weighted_rows(panels, left, scale_ref, part_ref, add=False):
    tiles = panels[0].shape[1] // LANES
    scales = [scale_ref[:, left + k * LANES : left + (k + 1) * LANES] for k in range(tiles)]
    top = 0
    for ref in panels:

        def body(i, _, ref=ref, top=top):
            at = pl.ds(pl.multiple_of(i * 8, 8), 8)
            to = pl.ds(pl.multiple_of(i * 8 + top, 8), 8)
            sums = [None] * 4
            for k in range(tiles):
                term = ref[at, k * LANES : (k + 1) * LANES] * scales[k]
                sums[k % 4] = term if sums[k % 4] is None else sums[k % 4] + term
            total = (sums[0] + sums[1]) + (sums[2] + sums[3])
            part_ref[to, :] = part_ref[to, :] + total if add else total
            return 0

        lax.fori_loop(0, ref.shape[0] // 8, body, 0, unroll=8)
        top += ref.shape[0]


def column_scales(panels, left, row_ref, scale_ref):
    tiles = panels[0].shape[1] // LANES
    sums = [jnp.zeros((8, LANES), jnp.float32)] * tiles
    top = 0
    for ref in panels:

        def body(i, sums, ref=ref, top=top):
            at = pl.ds(pl.multiple_of(i * 8, 8), 8)
            row = row_ref[pl.ds(pl.multiple_of(i * 8 + top, 8), 8), :]
            return [
                total + ref[at, k * LANES : (k + 1) * LANES] * row for k, total in enumerate(sums)
            ]

        sums = lax.fori_loop(0, ref.shape[0] // 8, body, sums, unroll=8)
        top += ref.shape[0]
    for k, total in enumerate(sums):
        inverse = 1.0 / jnp.sum(total, axis=0, keepdims=True)
        at = slice(left + k * LANES, left + (k + 1) * LANES)
        scale_ref[:, at] = jnp.broadcast_to(inverse, (8, LANES))


def weights_of(rows, units, live):
    weights = jnp.exp(scores_of(rows, units) * (1 / teacher_temp)) * live
    return weights, fold(weights)


def fold(values):
    return jnp.sum(values.reshape(values.shape[0] // 8, 8, values.shape[1]), axis=0)


def units_kernel(n_dp, rows, place_ref, proto_ref, units_ref, *live_refs):
    units_ref[...] = quick_unit(proto_ref[...])[0].astype(jnp.bfloat16)
    for k, live_ref in enumerate(live_refs):
        live_ref[...] = as_column(live_lanes(place_ref, k, live_ref.shape[0], n_dp, rows))


def near_kernel(chunk, place_ref, near_ref, live_ref, own_units_ref, proto_ref, *refs):
    weights_ref, sums_ref, rows_ref, units_ref = refs
    rows_near = place_rows(place_ref, near_ref, 0)
    rows_ref[...] = rows_near
    live = spread(live_ref[...], chunk)
    protos = own_units_ref.shape[0]
    for start in range(0, 2 * protos, chunk):
        at = slice(start, start + chunk)
        if start < protos:
            units = own_units_ref[at, :]
        else:
            here = slice(start - protos, start - protos + chunk)
            units = quick_unit(proto_ref[here, :])[0].astype(jnp.bfloat16)
            units_ref[here, :] = units
        weights_ref[:, at], sums_ref[:, at] = weights_of(rows_near, units, live)


def far_kernel(chunk, place_ref, far_ref, live_ref, near_weights_ref, near_sums_ref, *refs):
    *unit_refs, weights_ref, rows_ref, sums_ref, scale_ref, part_ref = refs
    rows_far = place_rows(place_ref, far_ref, 0)
    rows_ref[...] = rows_far
    live = spread(live_ref[...], chunk)
    protos = unit_refs[0].shape[0]
    for k, unit_ref in enumerate(unit_refs):
        for start in range(0, protos, chunk):
            at = slice(k * protos + start, k * protos + start + chunk)
            weights, sums = weights_of(rows_far, unit_ref[start : start + chunk, :], live)
            weights_ref[:, at] = weights
            inverse = 1.0 / jnp.sum(near_sums_ref[:, at] + sums, axis=0, keepdims=True)
            scale_ref[:, at] = jnp.broadcast_to(inverse, (8, chunk))
    weighted_rows([near_weights_ref, weights_ref], 0, scale_ref, part_ref)
    sums_ref[...] = as_tile(part_ref[...])


def across_kernel(chunk, place_ref, near_ref, far_ref, *refs):
    near_rows_ref, far_rows_ref, near_live_ref, far_live_ref, *refs = refs
    *proto_refs, weights_ref, student_ref = refs
    protos = proto_refs[0].shape[0]
    rows_all = jnp.concatenate([near_rows_ref[...], far_rows_ref[...]], axis=0)
    live = spread(jnp.concatenate([near_live_ref[...], far_live_ref[...]], axis=0), chunk)
    for k, proto_ref in enumerate(proto_refs):
        for start in range(0, protos, chunk):
            units = quick_unit(proto_ref[start : start + chunk, :])[0].astype(jnp.bfloat16)
            at = slice(k * protos + start, k * protos + start + chunk)
            weights_ref[:, at], _ = weights_of(rows_all, units, live)
    half = student_ref.shape[0] // 2
    for k, ref in enumerate((near_ref, far_ref)):
        student_ref[k * half : (k + 1) * half, :] = place_rows(place_ref, ref, 1)


def scale_columns(sums, near_ref, far_ref, across_ref, row_ref, scale_ref):
    row_ref[...] = as_column(inverse_rows(sums, row_ref.shape[0]))
    column_scales([near_ref, far_ref], 0, row_ref, scale_ref)
    column_scales([across_ref], near_ref.shape[1], row_ref, scale_ref)


def next_sums(near_ref, far_ref, across_ref, scale_ref, part_ref):
    weighted_rows([near_ref, far_ref], 0, scale_ref, part_ref)
    weighted_rows([across_ref], near_ref.shape[1], scale_ref, part_ref, add=True)
    return as_tile(part_ref[...])


def step_kernel(mine_ref, other_ref, near_ref, far_ref, across_ref, sums_ref, *scratch):
    row_ref, scale_ref, part_ref = scratch
    sums = mine_ref[...] + other_ref[...]
    scale_columns(sums, near_ref, far_ref, across_ref, row_ref, scale_ref)
    sums_ref[...] = next_sums(near_ref, far_ref, across_ref, scale_ref, part_ref)


def split(values):
    high = values.astype(jnp.bfloat16)
    low = (values - high.astype(jnp.float32)).astype(jnp.bfloat16)
    return jnp.concatenate([high, low], axis=0)


def exps_kernel(chunk, rows_ref, *refs):
    *proto_refs, units_ref, pull_ref, sums_ref, exps_ref = refs
    all_rows = rows_ref.shape[0]
    protos = proto_refs[0].shape[0]
    first = pull_ref.shape[0]
    rows_all = rows_ref[...]
    part = jnp.zeros((all_rows, LANES), jnp.float32)
    pull = jnp.zeros((2 * first, pull_ref.shape[1]), jnp.float32)
    for k, proto_ref in enumerate(proto_refs):
        for start in range(0, protos, chunk):
            units = quick_unit(proto_ref[start : start + chunk, :])[0].astype(jnp.bfloat16)
            units_ref[k * protos + start : k * protos + start + chunk, :] = units
            exps_ref[...] = jnp.exp(scores_of(rows_all, units) * (1 / student_temp))
            for at in range(0, chunk, LANES):
                part = part + exps_ref[:, at : at + LANES]
            exps = split(exps_ref[:first, :])
            pull = pull + jnp.dot(exps, units, preferred_element_type=jnp.float32)
    pull_ref[...] = pull[:first] + pull[first:]
    sums_ref[...] = as_tile(part)


def last_kernel(chunk, rows, place_ref, mine_ref, other_ref, near_ref, far_ref, across_ref, *refs):
    units_ref, exp_pull_ref, exp_sums_ref, scale_ref, keep_ref, send_ref, row_ref, blocks_ref = refs
    first = exp_pull_ref.shape[0]
    sums = mine_ref[...] + other_ref[...]
    scale_columns(sums, near_ref, far_ref, across_ref, row_ref, scale_ref)
    pull = jnp.zeros((2 * first, exp_pull_ref.shape[1]), jnp.float32)
    for start in range(0, units_ref.shape[0], chunk):
        at = slice(start, start + chunk)
        scaled = split(near_ref[:first, at] * scale_ref[:1, at])
        pull = pull + jnp.dot(scaled, units_ref[at, :], preferred_element_type=jnp.float32)
    pulls = (pull[:first] + pull[first:], exp_pull_ref[...])
    for k, pull in enumerate(pulls):
        for block in range(4):
            blocks_ref[k, block, :rows, :] = pull[block * rows : (block + 1) * rows]
    mine = place_ref[1]
    for ref, proto in ((keep_ref, mine), (send_ref, mine ^ X)):
        for j, owner in enumerate((proto, proto ^ Y)):
            for k in range(2):
                start = (2 * j + k) * rows
                ref[start : start + rows, :] = blocks_ref[k, block_of(owner), :rows, :]
        ref[4 * rows :, :LANES] = exp_sums_ref[...]
        ref[4 * rows :, LANES:] = jnp.zeros_like(exp_sums_ref)


def last_sums_kernel(near_ref, far_ref, across_ref, scale_ref, sums_ref, part_ref):
    sums_ref[:, :LANES] = jnp.zeros_like(sums_ref[:, :LANES])
    sums_ref[:, LANES:] = next_sums(near_ref, far_ref, across_ref, scale_ref, part_ref)


def own_kernel(place_ref, mine_ref, other_ref, near_rows_ref, far_rows_ref, *refs):
    student_rows_ref, teacher_proto_ref, proto_ref, *refs = refs
    targets_ref, exps_ref, unit_ref, scale_ref = refs
    teacher_rows = jnp.concatenate([near_rows_ref[...], far_rows_ref[...]], axis=0)
    own, all_rows = targets_ref.shape
    row_scale = inverse_rows(mine_ref[...] + other_ref[...], all_rows)
    live = jnp.where(row_scale > 0.0, 1.0, 0.0)
    first = pl.ds(pl.multiple_of(place_ref[0] * own, own), own)
    units = quick_unit(teacher_proto_ref[first, :])[0].astype(jnp.bfloat16)
    weights = jnp.exp(scores_of(units, teacher_rows) * (1 / teacher_temp)) * live
    inverse = 1.0 / jnp.sum(weights * row_scale, axis=1, keepdims=True)
    targets_ref[...] = weights * (inverse * (1 / student_temp))
    unit, scale = quick_unit(proto_ref[first, :])
    unit_ref[...] = unit
    scale_ref[...] = jnp.broadcast_to(scale, scale_ref.shape)
    units = unit.astype(jnp.bfloat16)
    exps = jnp.exp(scores_of(units, student_rows_ref[...]) * (1 / student_temp))
    exps_ref[...] = exps * (1 / student_temp)


def grads_kernel(place_ref, mine_ref, sums_ref, other_ref, targets_ref, exps_ref, *refs):
    unit_ref, scale_ref, rows_ref, feat_ref, student_out_ref, proto_out_ref = refs
    all_rows = targets_ref.shape[1]
    rows = feat_ref.shape[0]
    sums = sums_ref[...] + other_ref[2 * rows :, :]
    target_scale = inverse_rows(sums[:, LANES:], all_rows)
    exp_scale = jnp.where(target_scale > 0.0, 1.0 / unpack_lanes(sums[:, :LANES], all_rows), 0.0)

    grad = exps_ref[...] * exp_scale - targets_ref[...] * target_scale
    pushed = jnp.dot(grad.astype(jnp.bfloat16), rows_ref[...], preferred_element_type=jnp.float32)
    unit = unit_ref[...]
    along = jnp.sum(unit * pushed, axis=1, keepdims=True)
    proto_out_ref[0] = (pushed - unit * along) * twice(scale_ref[...])

    row = lax.broadcasted_iota(jnp.int32, (rows, LANES), 0) + block_of(place_ref[1]) * rows
    here = lax.broadcasted_iota(jnp.int32, (rows, LANES), 1) == row
    target_column, exp_column = [
        jnp.sum(jnp.where(here, scale[:, :LANES], 0.0), axis=1, keepdims=True) * (1 / student_temp)
        for scale in (target_scale, exp_scale)
    ]
    target_pull, exp_pull = [
        mine_ref[k * rows : (k + 1) * rows, :] + other_ref[k * rows : (k + 1) * rows, :]
        for k in range(2)
    ]
    pulled = exp_pull * exp_column - target_pull * target_column
    unit, scale = quick_unit(feat_ref[...])
    student_out_ref[...] = (
        pulled - unit * jnp.sum(unit * pulled, axis=1, keepdims=True)
    ) * scale


def call(kernel, out_shape, operands, smem=0, scratch=(), work=0):
    vmem = pl.BlockSpec(memory_space=pltpu.VMEM)
    return pl.pallas_call(
        kernel,
        out_shape=out_shape,
        in_specs=[pl.BlockSpec(memory_space=pltpu.SMEM)] * smem + [vmem] * (len(operands) - smem),
        out_specs=jax.tree.map(lambda _: vmem, out_shape),
        scratch_shapes=scratch,
        compiler_params=pltpu.CompilerParams(vmem_limit_bytes=24 * 2**20),
        cost_estimate=pl.CostEstimate(
            flops=512 * work, bytes_accessed=4 * work, transcendentals=work
        ),
    )(*operands)


def swap(values, axis, distance):
    others = [(k, k ^ distance) for k in range(lax.axis_size(axis))]
    return lax.ppermute(values, axis, others)


def swap_dp(values, t):
    n_dp, n_proto = lax.axis_size("dp"), lax.axis_size("proto")
    others = [
        (d * n_proto + p, (d ^ t) * n_proto + (p ^ CORE)) for d in range(n_dp) for p in range(n_proto)
    ]
    return lax.ppermute(values, ("dp", "proto"), others)


def on_device_all_rows(student_feat, teacher_feat, prototypes, teacher_prototypes, live_count):
    n_dp, n_proto = lax.axis_size("dp"), lax.axis_size("proto")
    rows, width = student_feat.shape
    protos = prototypes.shape[0]
    own = protos // n_dp
    piece = 2 * own
    all_rows = n_dp * n_proto * rows
    half = all_rows // 2
    first = 4 * rows
    held = 2 * protos
    f32 = functools.partial(jax.ShapeDtypeStruct, dtype=jnp.float32)
    bf16 = functools.partial(jax.ShapeDtypeStruct, dtype=jnp.bfloat16)
    place = jnp.stack([lax.axis_index("dp"), lax.axis_index("proto")]).astype(jnp.int32)
    place = jnp.concatenate([place, live_count])
    tile = f32((8, LANES))
    message = f32((4 * rows + 8, width))
    column = pltpu.VMEM((all_rows, LANES), jnp.float32)
    scale_row = pltpu.VMEM((8, held), jnp.float32)
    sweep_scratch = [column, pltpu.VMEM((8, 2 * held), jnp.float32), column]

    both = lax.optimization_barrier(jnp.concatenate([teacher_feat, student_feat], axis=0))
    across_x = swap(both, "proto", X_CROSS)
    across_x, late_protos, place = lax.optimization_barrier((across_x, teacher_prototypes, place))
    across_protos = swap(late_protos, "proto", X_CROSS)
    student_protos = (prototypes, swap(prototypes, "proto", CORE))
    teacher_protos = swap(late_protos, "proto", CORE)
    near = call(
        pair_kernel,
        bf16((4 * rows, width)),
        (place, both, across_x),
        smem=1,
        scratch=[pltpu.VMEM((4 * rows, width), jnp.float32)],
    )
    near = jnp.stack([near] + [swap_dp(near, t) for t in dp_order(n_dp)[1:]])
    near, own_protos = lax.optimization_barrier((near, teacher_prototypes))
    live = f32((half, LANES))
    teacher_units, near_live, far_live = call(
        functools.partial(units_kernel, n_dp, rows),
        (bf16((protos, width)), live, live),
        (place, own_protos),
        smem=1,
        work=protos * width,
    )
    near = jnp.stack([near, swap(near, "proto", Y_CROSS)])
    near, teacher_units = lax.optimization_barrier((near, teacher_units))
    far = swap(near, "proto", CORE)

    near_weights, near_sums, near_rows, other_units = call(
        functools.partial(near_kernel, piece),
        (
            f32((half, held)),
            f32((8, held)),
            bf16((half, width)),
            bf16((protos, width)),
        ),
        (place, near, near_live, teacher_units, teacher_protos),
        smem=1,
        work=held * half,
    )
    far_weights, far_rows, sums = call(
        functools.partial(far_kernel, piece),
        (f32((half, held)), bf16((half, width)), tile),
        (place, far, far_live, near_weights, near_sums, teacher_units, other_units),
        smem=1,
        scratch=[scale_row, column],
        work=held * half,
    )
    sums = sums + swap(sums, "proto", Y_CROSS)
    sums, across_protos = lax.optimization_barrier((sums, across_protos))
    parts = (sums, swap(sums, "proto", X_CROSS))
    across_weights, student_rows = call(
        functools.partial(across_kernel, piece),
        (f32((all_rows, held)), bf16((all_rows, width))),
        (
            place,
            near,
            far,
            near_rows,
            far_rows,
            near_live,
            far_live,
            across_protos,
            swap(across_protos, "proto", CORE),
        ),
        smem=1,
        work=held * all_rows,
    )
    weights = (near_weights, far_weights, across_weights)
    for _ in range(ITERS - 2):
        sums = call(
            step_kernel,
            tile,
            (*parts, *weights),
            scratch=sweep_scratch,
            work=held * all_rows,
        )
        sums, student_rows, *student_protos = lax.optimization_barrier(
            (sums, student_rows, *student_protos)
        )
        parts = (sums, swap(sums, "proto", Y_CROSS))
    student_units, exp_pull, exp_sums = call(
        functools.partial(exps_kernel, piece),
        (bf16((held, width)), f32((first, width)), tile),
        (student_rows, *student_protos),
        scratch=[pltpu.VMEM((all_rows, piece), jnp.float32)],
        work=held * all_rows,
    )
    scales, keep, send = call(
        functools.partial(last_kernel, own, rows),
        (f32((8, 2 * held)), message, message),
        (place, *parts, *weights, student_units, exp_pull, exp_sums),
        smem=1,
        scratch=[column, pltpu.VMEM((2, 4, 16, width), jnp.float32)],
        work=held * all_rows,
    )
    last_sums = call(
        last_sums_kernel,
        f32((8, width)),
        (*weights, scales),
        scratch=[column],
        work=held * all_rows,
    )
    *parts, send = lax.optimization_barrier((*parts, send))
    targets, exps, own_units, own_scales = call(
        own_kernel,
        (f32((own, all_rows)), f32((own, all_rows)), f32((own, width)), f32((own, LANES))),
        (place, *parts, near_rows, far_rows, student_rows, teacher_prototypes, prototypes),
        smem=1,
        work=own * all_rows,
    )
    total = keep + swap(send, "proto", X_CROSS)
    last_sums = total[4 * rows :] + last_sums
    return call(
        grads_kernel,
        (f32((rows, width)), f32((1, own, width))),
        (
            place,
            total,
            last_sums,
            swap(jnp.concatenate([total[2 * rows : 4 * rows], last_sums]), "proto", Y_CROSS),
            targets,
            exps,
            own_units,
            own_scales,
            student_rows,
            student_feat,
        ),
        smem=1,
        work=own * all_rows,
    )


def sample_totals(values):
    return lax.psum(values, "proto")


def proto_totals(values):
    return lax.psum(values, "dp")


def on_device_group_rows(student_feat, teacher_feat, prototypes, teacher_prototypes, live_count):
    student_unit, student_length = unit_rows(student_feat)
    teacher_unit, teacher_length = unit_rows(teacher_feat)
    proto_unit, proto_length = unit_rows(prototypes)
    teacher_proto, teacher_proto_length = unit_rows(teacher_prototypes)
    proto_bf = proto_unit.astype(jnp.bfloat16)
    teacher_proto_bf = teacher_proto.astype(jnp.bfloat16)
    student_rows, teacher_rows = (
        lax.all_gather(student_unit.astype(jnp.bfloat16), "proto", axis=0, tiled=True),
        lax.all_gather(teacher_unit.astype(jnp.bfloat16), "proto", axis=0, tiled=True),
    )
    group_size = student_rows.shape[0]
    live_rows = live_count[lax.axis_index("dp")]
    live_mask = jnp.arange(group_size, dtype=jnp.int32) < live_rows
    live_column = live_mask[:, None]
    contract_last = (((1,), (1,)), ((), ()))
    logits = (
        lax.dot_general(student_rows, proto_bf, contract_last, preferred_element_type=jnp.float32)
        / student_temp
    )
    teacher_scores = (
        lax.dot_general(
            teacher_rows, teacher_proto_bf, contract_last, preferred_element_type=jnp.float32
        )
        / teacher_temp
    )
    weights = jnp.where(live_column, jnp.exp(teacher_scores), 0.0)
    partition = sample_totals(jnp.sum(jnp.exp(logits), axis=1))
    targets = weights
    for iteration in range(ITERS):
        targets = targets / proto_totals(jnp.sum(targets, axis=0))[None, :]
        row_sums = sample_totals(jnp.sum(targets, axis=1))
        targets = targets / jnp.where(live_mask, row_sums, 1.0)[:, None]
    student_probs = jnp.exp(logits - jnp.log(partition)[:, None])
    grad_block = jnp.where(live_column, (student_probs - targets) / student_temp, 0.0).astype(
        jnp.bfloat16
    )
    pulled = lax.psum_scatter(
        jnp.dot(grad_block, proto_bf, preferred_element_type=jnp.float32),
        "proto",
        scatter_dimension=0,
        tiled=True,
    )
    student_grad = (
        pulled - student_unit * jnp.sum(student_unit * pulled, axis=1, keepdims=True)
    ) / student_length
    own_protos = prototypes.shape[0] // lax.axis_size("dp")
    contract_first = (((0,), (0,)), ((), ()))
    pushed = lax.psum_scatter(
        lax.dot_general(
            grad_block, student_rows, contract_first, preferred_element_type=jnp.float32
        ),
        "dp",
        scatter_dimension=0,
        tiled=True,
    )
    first_proto = lax.axis_index("dp") * own_protos
    own_units = lax.dynamic_slice_in_dim(proto_unit, first_proto, own_protos, 0)
    own_lengths = lax.dynamic_slice_in_dim(proto_length, first_proto, own_protos, 0)
    proto_grad = (
        pushed - own_units * jnp.sum(own_units * pushed, axis=1, keepdims=True)
    ) / own_lengths
    return (student_grad, proto_grad[None])


def on_device(student_feat, teacher_feat, prototypes, teacher_prototypes, live_count):
    n_dp, n_proto = lax.axis_size("dp"), lax.axis_size("proto")
    rows, width = student_feat.shape
    protos = prototypes.shape[0]
    lanes = n_dp * n_proto * rows
    fits = (
        n_proto == 2 * Y
        and n_dp & (n_dp - 1) == 0
        and rows % 4 == 0
        and rows <= 16
        and lanes % LANES == 0
        and lanes <= 8 * LANES
        and width == 2 * LANES
        and protos == n_dp * 2 * LANES
        and 4 * protos * lanes * 4 <= BLOCK_BYTES
    )
    plan = on_device_all_rows if fits else on_device_group_rows
    return plan(student_feat, teacher_feat, prototypes, teacher_prototypes, live_count)


def solution(mesh):
    return jax.shard_map(
        on_device,
        mesh=mesh,
        in_specs=(
            P(("dp", "proto"), None),
            P(("dp", "proto"), None),
            P("proto", None),
            P("proto", None),
            P(),
        ),
        out_specs=(P(("dp", "proto"), None), P("proto", "dp", None)),
        check_vma=False,
    )
```

```python
import functools

import jax
import jax.numpy as jnp
from jax import lax
from jax.experimental import pallas as pl
from jax.experimental.pallas import tpu as pltpu
from jax.sharding import PartitionSpec as P

ITERS = 3

student_temp = 0.1
teacher_temp = 0.07
eps_norm = 1e-06

LANES = 128
BLOCK_BYTES = 8 * 2**20


def unit_rows(values):
    widened = values.astype(jnp.float32)
    length = jnp.sqrt(jnp.sum(widened * widened, axis=1, keepdims=True) + eps_norm)
    return (widened / length, length)


CORE, X, Y = 1, 2, 4
X_CROSS, Y_CROSS = X | CORE, Y | CORE


def block_of(proto):
    return (proto & X) + ((proto >> 2) & 1)


def own_place():
    return lax.axis_index("dp"), lax.axis_index("proto")


def quick_unit(values):
    widened = values.astype(jnp.float32)
    squares = jnp.sum(widened * widened, axis=1, keepdims=True) + eps_norm
    scale = lax.rsqrt(squares)
    return widened * scale, scale


def dp_order(n_dp):
    return [0, *reversed(range(1, n_dp))]


def live_lanes(place_ref, half, lanes, n_dp, rows):
    mine = place_ref[1]
    parity = (mine ^ (mine >> 1) ^ (mine >> 2)) & 1
    lane = lax.broadcasted_iota(jnp.int32, (1, lanes), 1)
    live = jnp.zeros((1, lanes), jnp.float32)
    start = 0
    for t in dp_order(n_dp):
        count = place_ref[2 + (place_ref[0] ^ t)]
        for x in range(2):
            for y in range(2):
                core = parity ^ x ^ y ^ half ^ (1 if t else 0)
                proto = core + X * x + Y * y
                end = start + jnp.clip(count - proto * rows, 0, rows)
                live = jnp.where((lane >= start) & (lane < end), 1.0, live)
                start += rows
    return live


def pack_lanes(values):
    pieces = [values[:, k : k + LANES] for k in range(0, values.shape[1], LANES)]
    return jnp.concatenate(pieces + [jnp.zeros((8 - len(pieces), LANES), jnp.float32)], axis=0)


def unpack_lanes(tile, lanes):
    return jnp.concatenate([tile[k : k + 1, :] for k in range(lanes // LANES)], axis=1)


def as_column(values):
    return jnp.broadcast_to(values, (LANES, values.shape[1])).T


def as_tile(partial):
    return pack_lanes(jnp.sum(partial.T, axis=0, keepdims=True))


def inverse_rows(tile, rows):
    total = unpack_lanes(tile, rows)
    live = total > 0.0
    return jnp.where(live, 1.0 / jnp.where(live, total, 1.0), 0.0)


def place_rows(place, ref, which, rows, scratch):
    mine_x, mine_y = (place[1] >> 1) & 1, (place[1] >> 2) & 1
    start = 0
    for t in range(ref.shape[1]):
        for x in range(2):
            for y in range(2):
                block = ref[mine_y ^ y, t, mine_x ^ x].astype(jnp.float32)
                scratch[start : start + rows, :] = block[which * rows : (which + 1) * rows]
                start += rows
    unit, _ = quick_unit(scratch[...])
    return unit.astype(jnp.bfloat16)


def scores_of(rows_all, units):
    return lax.dot_general(
        rows_all, units, (((1,), (1,)), ((), ())), preferred_element_type=jnp.float32
    )


def twice(column):
    return jnp.concatenate([column, column], axis=1)


def spread(column, lanes):
    return jnp.concatenate([column] * (lanes // LANES), axis=1)


def weighted_rows(panels, left, scale_ref, part_ref, add=False):
    tiles = panels[0].shape[1] // LANES
    scales = [scale_ref[:, left + k * LANES : left + (k + 1) * LANES] for k in range(tiles)]
    top = 0
    for ref in panels:

        def body(i, _, ref=ref, top=top):
            at = pl.ds(pl.multiple_of(i * 8, 8), 8)
            to = pl.ds(pl.multiple_of(i * 8 + top, 8), 8)
            sums = [None] * 4
            for k in range(tiles):
                term = ref[at, k * LANES : (k + 1) * LANES] * scales[k]
                sums[k % 4] = term if sums[k % 4] is None else sums[k % 4] + term
            total = (sums[0] + sums[1]) + (sums[2] + sums[3])
            part_ref[to, :] = part_ref[to, :] + total if add else total
            return 0

        lax.fori_loop(0, ref.shape[0] // 8, body, 0, unroll=8)
        top += ref.shape[0]


def column_scales(panels, left, row_ref, scale_ref):
    tiles = panels[0].shape[1] // LANES
    sums = [jnp.zeros((8, LANES), jnp.float32)] * tiles
    top = 0
    for ref in panels:

        def body(i, sums, ref=ref, top=top):
            at = pl.ds(pl.multiple_of(i * 8, 8), 8)
            row = row_ref[pl.ds(pl.multiple_of(i * 8 + top, 8), 8), :]
            return [
                total + ref[at, k * LANES : (k + 1) * LANES] * row for k, total in enumerate(sums)
            ]

        sums = lax.fori_loop(0, ref.shape[0] // 8, body, sums, unroll=8)
        top += ref.shape[0]
    for k, total in enumerate(sums):
        inverse = 1.0 / jnp.sum(total, axis=0, keepdims=True)
        at = slice(left + k * LANES, left + (k + 1) * LANES)
        scale_ref[:, at] = jnp.broadcast_to(inverse, (8, LANES))


def weights_of(rows, units, live):
    weights = jnp.exp(scores_of(rows, units) * (1 / teacher_temp)) * live
    return weights, fold(weights)


def fold(values):
    return jnp.sum(values.reshape(values.shape[0] // 8, 8, values.shape[1]), axis=0)


def units_kernel(n_dp, rows, place_ref, proto_ref, units_ref, *live_refs):
    units_ref[...] = quick_unit(proto_ref[...])[0].astype(jnp.bfloat16)
    for k, live_ref in enumerate(live_refs):
        live_ref[...] = as_column(live_lanes(place_ref, k, live_ref.shape[0], n_dp, rows))


def near_kernel(chunk, near_ref, live_ref, own_units_ref, proto_ref, *refs):
    weights_ref, sums_ref, rows_ref, units_ref, scratch = refs
    rows = near_ref.shape[3] // 2
    rows_near = place_rows(own_place(), near_ref, 0, rows, scratch)
    rows_ref[...] = rows_near
    live = spread(live_ref[...], chunk)
    protos = own_units_ref.shape[0]
    for start in range(0, 2 * protos, chunk):
        at = slice(start, start + chunk)
        if start < protos:
            units = own_units_ref[at, :]
        else:
            here = slice(start - protos, start - protos + chunk)
            units = quick_unit(proto_ref[here, :])[0].astype(jnp.bfloat16)
            units_ref[here, :] = units
        weights_ref[:, at], sums_ref[:, at] = weights_of(rows_near, units, live)


def far_kernel(chunk, far_ref, live_ref, near_weights_ref, near_sums_ref, *refs):
    *unit_refs, weights_ref, rows_ref, sums_ref, scratch, scale_ref, part_ref = refs
    rows = far_ref.shape[3] // 2
    rows_far = place_rows(own_place(), far_ref, 0, rows, scratch)
    rows_ref[...] = rows_far
    live = spread(live_ref[...], chunk)
    protos = unit_refs[0].shape[0]
    for k, unit_ref in enumerate(unit_refs):
        for start in range(0, protos, chunk):
            at = slice(k * protos + start, k * protos + start + chunk)
            weights, sums = weights_of(rows_far, unit_ref[start : start + chunk, :], live)
            weights_ref[:, at] = weights
            inverse = 1.0 / jnp.sum(near_sums_ref[:, at] + sums, axis=0, keepdims=True)
            scale_ref[:, at] = jnp.broadcast_to(inverse, (8, chunk))
    weighted_rows([near_weights_ref, weights_ref], 0, scale_ref, part_ref)
    sums_ref[...] = as_tile(part_ref[...])


def across_kernel(chunk, near_ref, far_ref, *refs):
    near_rows_ref, far_rows_ref, near_live_ref, far_live_ref, *refs = refs
    *proto_refs, weights_ref, student_ref, scratch = refs
    protos = proto_refs[0].shape[0]
    rows_all = jnp.concatenate([near_rows_ref[...], far_rows_ref[...]], axis=0)
    live = spread(jnp.concatenate([near_live_ref[...], far_live_ref[...]], axis=0), chunk)
    for k, proto_ref in enumerate(proto_refs):
        for start in range(0, protos, chunk):
            units = quick_unit(proto_ref[start : start + chunk, :])[0].astype(jnp.bfloat16)
            at = slice(k * protos + start, k * protos + start + chunk)
            weights_ref[:, at], _ = weights_of(rows_all, units, live)
    half = student_ref.shape[0] // 2
    for k, ref in enumerate((near_ref, far_ref)):
        rows_half = place_rows(own_place(), ref, 1, ref.shape[3] // 2, scratch)
        student_ref[k * half : (k + 1) * half, :] = rows_half


def scale_columns(sums, near_ref, far_ref, across_ref, row_ref, scale_ref):
    row_ref[...] = as_column(inverse_rows(sums, row_ref.shape[0]))
    column_scales([near_ref, far_ref], 0, row_ref, scale_ref)
    column_scales([across_ref], near_ref.shape[1], row_ref, scale_ref)


def next_sums(near_ref, far_ref, across_ref, scale_ref, part_ref):
    weighted_rows([near_ref, far_ref], 0, scale_ref, part_ref)
    weighted_rows([across_ref], near_ref.shape[1], scale_ref, part_ref, add=True)
    return as_tile(part_ref[...])


def step_kernel(mine_ref, other_ref, near_ref, far_ref, across_ref, sums_ref, *scratch):
    row_ref, scale_ref, part_ref = scratch
    sums = mine_ref[...] + other_ref[...]
    scale_columns(sums, near_ref, far_ref, across_ref, row_ref, scale_ref)
    sums_ref[...] = next_sums(near_ref, far_ref, across_ref, scale_ref, part_ref)


def split(values):
    high = values.astype(jnp.bfloat16)
    low = (values - high.astype(jnp.float32)).astype(jnp.bfloat16)
    return jnp.concatenate([high, low], axis=0)


def exps_kernel(chunk, rows_ref, *refs):
    *proto_refs, units_ref, pull_ref, sums_ref, exps_ref = refs
    all_rows = rows_ref.shape[0]
    protos = proto_refs[0].shape[0]
    first = pull_ref.shape[0]
    rows_all = rows_ref[...]
    part = jnp.zeros((all_rows, LANES), jnp.float32)
    pull = jnp.zeros((2 * first, pull_ref.shape[1]), jnp.float32)
    for k, proto_ref in enumerate(proto_refs):
        for start in range(0, protos, chunk):
            units = quick_unit(proto_ref[start : start + chunk, :])[0].astype(jnp.bfloat16)
            units_ref[k * protos + start : k * protos + start + chunk, :] = units
            exps_ref[...] = jnp.exp(scores_of(rows_all, units) * (1 / student_temp))
            for at in range(0, chunk, LANES):
                part = part + exps_ref[:, at : at + LANES]
            exps = split(exps_ref[:first, :])
            pull = pull + jnp.dot(exps, units, preferred_element_type=jnp.float32)
    pull_ref[...] = pull[:first] + pull[first:]
    sums_ref[...] = as_tile(part)


def last_kernel(chunk, rows, mine_ref, other_ref, near_ref, far_ref, across_ref, *refs):
    units_ref, exp_pull_ref, exp_sums_ref, scale_ref, keep_ref, send_ref, row_ref, blocks_ref = refs
    first = exp_pull_ref.shape[0]
    sums = mine_ref[...] + other_ref[...]
    scale_columns(sums, near_ref, far_ref, across_ref, row_ref, scale_ref)
    pull = jnp.zeros((2 * first, exp_pull_ref.shape[1]), jnp.float32)
    for start in range(0, units_ref.shape[0], chunk):
        at = slice(start, start + chunk)
        scaled = split(near_ref[:first, at] * scale_ref[:1, at])
        pull = pull + jnp.dot(scaled, units_ref[at, :], preferred_element_type=jnp.float32)
    pulls = (pull[:first] + pull[first:], exp_pull_ref[...])
    for k, pull in enumerate(pulls):
        for block in range(4):
            blocks_ref[k, block, :rows, :] = pull[block * rows : (block + 1) * rows]
    _, mine = own_place()
    for ref, proto in ((keep_ref, mine), (send_ref, mine ^ X)):
        for j, owner in enumerate((proto, proto ^ Y)):
            for k in range(2):
                start = (2 * j + k) * rows
                ref[start : start + rows, :] = blocks_ref[k, block_of(owner), :rows, :]
        ref[4 * rows :, :LANES] = exp_sums_ref[...]
        ref[4 * rows :, LANES:] = jnp.zeros_like(exp_sums_ref)


def last_sums_kernel(near_ref, far_ref, across_ref, scale_ref, sums_ref, part_ref):
    sums_ref[:, :LANES] = jnp.zeros_like(sums_ref[:, :LANES])
    sums_ref[:, LANES:] = next_sums(near_ref, far_ref, across_ref, scale_ref, part_ref)


def own_kernel(mine_ref, other_ref, near_rows_ref, far_rows_ref, *refs):
    student_rows_ref, teacher_proto_ref, proto_ref, *refs = refs
    targets_ref, exps_ref, unit_ref, scale_ref = refs
    teacher_rows = jnp.concatenate([near_rows_ref[...], far_rows_ref[...]], axis=0)
    own, all_rows = targets_ref.shape
    row_scale = inverse_rows(mine_ref[...] + other_ref[...], all_rows)
    live = jnp.where(row_scale > 0.0, 1.0, 0.0)
    first = pl.ds(pl.multiple_of(own_place()[0] * own, own), own)
    units = quick_unit(teacher_proto_ref[first, :])[0].astype(jnp.bfloat16)
    weights = jnp.exp(scores_of(units, teacher_rows) * (1 / teacher_temp)) * live
    inverse = 1.0 / jnp.sum(weights * row_scale, axis=1, keepdims=True)
    targets_ref[...] = weights * (inverse * (1 / student_temp))
    unit, scale = quick_unit(proto_ref[first, :])
    unit_ref[...] = unit
    scale_ref[...] = jnp.broadcast_to(scale, scale_ref.shape)
    units = unit.astype(jnp.bfloat16)
    exps = jnp.exp(scores_of(units, student_rows_ref[...]) * (1 / student_temp))
    exps_ref[...] = exps * (1 / student_temp)


def grads_kernel(mine_ref, sums_ref, other_ref, targets_ref, exps_ref, *refs):
    unit_ref, scale_ref, rows_ref, feat_ref, student_out_ref, proto_out_ref = refs
    all_rows = targets_ref.shape[1]
    rows = feat_ref.shape[0]
    sums = sums_ref[...] + other_ref[2 * rows :, :]
    target_scale = inverse_rows(sums[:, LANES:], all_rows)
    exp_scale = jnp.where(target_scale > 0.0, 1.0 / unpack_lanes(sums[:, :LANES], all_rows), 0.0)

    grad = exps_ref[...] * exp_scale - targets_ref[...] * target_scale
    pushed = jnp.dot(grad.astype(jnp.bfloat16), rows_ref[...], preferred_element_type=jnp.float32)
    unit = unit_ref[...]
    along = jnp.sum(unit * pushed, axis=1, keepdims=True)
    proto_out_ref[0] = (pushed - unit * along) * twice(scale_ref[...])

    row = lax.broadcasted_iota(jnp.int32, (rows, LANES), 0) + block_of(own_place()[1]) * rows
    here = lax.broadcasted_iota(jnp.int32, (rows, LANES), 1) == row
    target_column, exp_column = [
        jnp.sum(jnp.where(here, scale[:, :LANES], 0.0), axis=1, keepdims=True) * (1 / student_temp)
        for scale in (target_scale, exp_scale)
    ]
    target_pull, exp_pull = [
        mine_ref[k * rows : (k + 1) * rows, :] + other_ref[k * rows : (k + 1) * rows, :]
        for k in range(2)
    ]
    pulled = exp_pull * exp_column - target_pull * target_column
    unit, scale = quick_unit(feat_ref[...])
    student_out_ref[...] = (
        pulled - unit * jnp.sum(unit * pulled, axis=1, keepdims=True)
    ) * scale


def call(kernel, out_shape, operands, smem=0, scratch=(), work=0):
    vmem = pl.BlockSpec(memory_space=pltpu.VMEM)
    return pl.pallas_call(
        kernel,
        out_shape=out_shape,
        in_specs=[pl.BlockSpec(memory_space=pltpu.SMEM)] * smem + [vmem] * (len(operands) - smem),
        out_specs=jax.tree.map(lambda _: vmem, out_shape),
        scratch_shapes=scratch,
        compiler_params=pltpu.CompilerParams(vmem_limit_bytes=24 * 2**20),
        cost_estimate=pl.CostEstimate(
            flops=512 * work, bytes_accessed=4 * work, transcendentals=work
        ),
    )(*operands)


def swap(values, axis, distance):
    others = [(k, k ^ distance) for k in range(lax.axis_size(axis))]
    return lax.ppermute(values, axis, others)


def swap_dp(values, t):
    n_dp, n_proto = lax.axis_size("dp"), lax.axis_size("proto")
    others = [
        (d * n_proto + p, (d ^ t) * n_proto + (p ^ CORE)) for d in range(n_dp) for p in range(n_proto)
    ]
    return lax.ppermute(values, ("dp", "proto"), others)


def on_device_all_rows(student_feat, teacher_feat, prototypes, teacher_prototypes, live_count):
    n_dp, n_proto = lax.axis_size("dp"), lax.axis_size("proto")
    rows, width = student_feat.shape
    protos = prototypes.shape[0]
    own = protos // n_dp
    piece = 2 * own
    all_rows = n_dp * n_proto * rows
    half = all_rows // 2
    first = 4 * rows
    held = 2 * protos
    f32 = functools.partial(jax.ShapeDtypeStruct, dtype=jnp.float32)
    bf16 = functools.partial(jax.ShapeDtypeStruct, dtype=jnp.bfloat16)
    place = jnp.stack([lax.axis_index("dp"), lax.axis_index("proto")]).astype(jnp.int32)
    place = jnp.concatenate([place, live_count])
    tile = f32((8, LANES))
    message = f32((4 * rows + 8, width))
    row_scratch = pltpu.VMEM((half, width), jnp.float32)
    column = pltpu.VMEM((all_rows, LANES), jnp.float32)
    scale_row = pltpu.VMEM((8, held), jnp.float32)
    sweep_scratch = [column, pltpu.VMEM((8, 2 * held), jnp.float32), column]

    both = lax.optimization_barrier(jnp.concatenate([teacher_feat, student_feat], axis=0))
    across_x = swap(both, "proto", X_CROSS)
    across_x, late_protos, place = lax.optimization_barrier((across_x, teacher_prototypes, place))
    across_protos = swap(late_protos, "proto", X_CROSS)
    student_protos = (prototypes, swap(prototypes, "proto", CORE))
    teacher_protos = swap(late_protos, "proto", CORE)
    near = jnp.stack([both, across_x])
    near = jnp.stack([near] + [swap_dp(near, t) for t in dp_order(n_dp)[1:]])
    near, own_protos = lax.optimization_barrier((near, teacher_prototypes))
    live = f32((half, LANES))
    teacher_units, near_live, far_live = call(
        functools.partial(units_kernel, n_dp, rows),
        (bf16((protos, width)), live, live),
        (place, own_protos),
        smem=1,
        work=protos * width,
    )
    near = jnp.stack([near, swap(near, "proto", Y_CROSS)])
    near, teacher_units = lax.optimization_barrier((near, teacher_units))
    far = swap(near, "proto", CORE)

    near_weights, near_sums, near_rows, other_units = call(
        functools.partial(near_kernel, piece),
        (
            f32((half, held)),
            f32((8, held)),
            bf16((half, width)),
            bf16((protos, width)),
        ),
        (near, near_live, teacher_units, teacher_protos),
        scratch=[row_scratch],
        work=held * half,
    )
    far_weights, far_rows, sums = call(
        functools.partial(far_kernel, piece),
        (f32((half, held)), bf16((half, width)), tile),
        (far, far_live, near_weights, near_sums, teacher_units, other_units),
        scratch=[row_scratch, scale_row, column],
        work=held * half,
    )
    sums = sums + swap(sums, "proto", Y_CROSS)
    sums, across_protos = lax.optimization_barrier((sums, across_protos))
    parts = (sums, swap(sums, "proto", X_CROSS))
    across_weights, student_rows = call(
        functools.partial(across_kernel, piece),
        (f32((all_rows, held)), bf16((all_rows, width))),
        (
            near,
            far,
            near_rows,
            far_rows,
            near_live,
            far_live,
            across_protos,
            swap(across_protos, "proto", CORE),
        ),
        scratch=[row_scratch],
        work=held * all_rows,
    )
    weights = (near_weights, far_weights, across_weights)
    for _ in range(ITERS - 2):
        sums = call(
            step_kernel,
            tile,
            (*parts, *weights),
            scratch=sweep_scratch,
            work=held * all_rows,
        )
        sums, student_rows, *student_protos = lax.optimization_barrier(
            (sums, student_rows, *student_protos)
        )
        parts = (sums, swap(sums, "proto", Y_CROSS))
    student_units, exp_pull, exp_sums = call(
        functools.partial(exps_kernel, piece),
        (bf16((held, width)), f32((first, width)), tile),
        (student_rows, *student_protos),
        scratch=[pltpu.VMEM((all_rows, piece), jnp.float32)],
        work=held * all_rows,
    )
    scales, keep, send = call(
        functools.partial(last_kernel, own, rows),
        (f32((8, 2 * held)), message, message),
        (*parts, *weights, student_units, exp_pull, exp_sums),
        scratch=[column, pltpu.VMEM((2, 4, 16, width), jnp.float32)],
        work=held * all_rows,
    )
    last_sums = call(
        last_sums_kernel,
        f32((8, width)),
        (*weights, scales),
        scratch=[column],
        work=held * all_rows,
    )
    *parts, send = lax.optimization_barrier((*parts, send))
    targets, exps, own_units, own_scales = call(
        own_kernel,
        (f32((own, all_rows)), f32((own, all_rows)), f32((own, width)), f32((own, LANES))),
        (*parts, near_rows, far_rows, student_rows, teacher_prototypes, prototypes),
        work=own * all_rows,
    )
    total = keep + swap(send, "proto", X_CROSS)
    last_sums = total[4 * rows :] + last_sums
    return call(
        grads_kernel,
        (f32((rows, width)), f32((1, own, width))),
        (
            total,
            last_sums,
            swap(jnp.concatenate([total[2 * rows : 4 * rows], last_sums]), "proto", Y_CROSS),
            targets,
            exps,
            own_units,
            own_scales,
            student_rows,
            student_feat,
        ),
        work=own * all_rows,
    )


def sample_totals(values):
    return lax.psum(values, "proto")


def proto_totals(values):
    return lax.psum(values, "dp")


def on_device_group_rows(student_feat, teacher_feat, prototypes, teacher_prototypes, live_count):
    student_unit, student_length = unit_rows(student_feat)
    teacher_unit, teacher_length = unit_rows(teacher_feat)
    proto_unit, proto_length = unit_rows(prototypes)
    teacher_proto, teacher_proto_length = unit_rows(teacher_prototypes)
    proto_bf = proto_unit.astype(jnp.bfloat16)
    teacher_proto_bf = teacher_proto.astype(jnp.bfloat16)
    student_rows, teacher_rows = (
        lax.all_gather(student_unit.astype(jnp.bfloat16), "proto", axis=0, tiled=True),
        lax.all_gather(teacher_unit.astype(jnp.bfloat16), "proto", axis=0, tiled=True),
    )
    group_size = student_rows.shape[0]
    live_rows = live_count[lax.axis_index("dp")]
    live_mask = jnp.arange(group_size, dtype=jnp.int32) < live_rows
    live_column = live_mask[:, None]
    contract_last = (((1,), (1,)), ((), ()))
    logits = (
        lax.dot_general(student_rows, proto_bf, contract_last, preferred_element_type=jnp.float32)
        / student_temp
    )
    teacher_scores = (
        lax.dot_general(
            teacher_rows, teacher_proto_bf, contract_last, preferred_element_type=jnp.float32
        )
        / teacher_temp
    )
    weights = jnp.where(live_column, jnp.exp(teacher_scores), 0.0)
    partition = sample_totals(jnp.sum(jnp.exp(logits), axis=1))
    targets = weights
    for iteration in range(ITERS):
        targets = targets / proto_totals(jnp.sum(targets, axis=0))[None, :]
        row_sums = sample_totals(jnp.sum(targets, axis=1))
        targets = targets / jnp.where(live_mask, row_sums, 1.0)[:, None]
    student_probs = jnp.exp(logits - jnp.log(partition)[:, None])
    grad_block = jnp.where(live_column, (student_probs - targets) / student_temp, 0.0).astype(
        jnp.bfloat16
    )
    pulled = lax.psum_scatter(
        jnp.dot(grad_block, proto_bf, preferred_element_type=jnp.float32),
        "proto",
        scatter_dimension=0,
        tiled=True,
    )
    student_grad = (
        pulled - student_unit * jnp.sum(student_unit * pulled, axis=1, keepdims=True)
    ) / student_length
    own_protos = prototypes.shape[0] // lax.axis_size("dp")
    contract_first = (((0,), (0,)), ((), ()))
    pushed = lax.psum_scatter(
        lax.dot_general(
            grad_block, student_rows, contract_first, preferred_element_type=jnp.float32
        ),
        "dp",
        scatter_dimension=0,
        tiled=True,
    )
    first_proto = lax.axis_index("dp") * own_protos
    own_units = lax.dynamic_slice_in_dim(proto_unit, first_proto, own_protos, 0)
    own_lengths = lax.dynamic_slice_in_dim(proto_length, first_proto, own_protos, 0)
    proto_grad = (
        pushed - own_units * jnp.sum(own_units * pushed, axis=1, keepdims=True)
    ) / own_lengths
    return (student_grad, proto_grad[None])


def on_device(student_feat, teacher_feat, prototypes, teacher_prototypes, live_count):
    n_dp, n_proto = lax.axis_size("dp"), lax.axis_size("proto")
    rows, width = student_feat.shape
    protos = prototypes.shape[0]
    lanes = n_dp * n_proto * rows
    fits = (
        n_proto == 2 * Y
        and n_dp & (n_dp - 1) == 0
        and rows % 4 == 0
        and rows <= 16
        and lanes % LANES == 0
        and lanes <= 8 * LANES
        and width == 2 * LANES
        and protos == n_dp * 2 * LANES
        and 4 * protos * lanes * 4 <= BLOCK_BYTES
    )
    plan = on_device_all_rows if fits else on_device_group_rows
    return plan(student_feat, teacher_feat, prototypes, teacher_prototypes, live_count)


def solution(mesh):
    return jax.shard_map(
        on_device,
        mesh=mesh,
        in_specs=(
            P(("dp", "proto"), None),
            P(("dp", "proto"), None),
            P("proto", None),
            P("proto", None),
            P(),
        ),
        out_specs=(P(("dp", "proto"), None), P("proto", "dp", None)),
        check_vma=False,
    )
```

```python
import functools

import jax
import jax.numpy as jnp
from jax import lax
from jax.experimental import pallas as pl
from jax.experimental.pallas import tpu as pltpu
from jax.sharding import PartitionSpec as P

ITERS = 3

student_temp = 0.1
teacher_temp = 0.07
eps_norm = 1e-06

LANES = 128
BLOCK_BYTES = 8 * 2**20


def unit_rows(values):
    widened = values.astype(jnp.float32)
    length = jnp.sqrt(jnp.sum(widened * widened, axis=1, keepdims=True) + eps_norm)
    return (widened / length, length)


CORE, X, Y = 1, 2, 4
X_CROSS, Y_CROSS = X | CORE, Y | CORE


def block_of(proto):
    return (proto & X) + ((proto >> 2) & 1)


def own_place():
    return lax.axis_index("dp"), lax.axis_index("proto")


def quick_unit(values):
    widened = values.astype(jnp.float32)
    squares = jnp.sum(widened * widened, axis=1, keepdims=True) + eps_norm
    scale = lax.rsqrt(squares)
    return widened * scale, scale


def dp_order(n_dp):
    return [0, *reversed(range(1, n_dp))]


def live_lanes(place_ref, half, lanes, n_dp, rows):
    mine = place_ref[1]
    parity = (mine ^ (mine >> 1) ^ (mine >> 2)) & 1
    lane = lax.broadcasted_iota(jnp.int32, (1, lanes), 1)
    live = jnp.zeros((1, lanes), jnp.float32)
    start = 0
    for t in dp_order(n_dp):
        count = place_ref[2 + (place_ref[0] ^ t)]
        for x in range(2):
            for y in range(2):
                core = parity ^ x ^ y ^ half ^ (1 if t else 0)
                proto = core + X * x + Y * y
                end = start + jnp.clip(count - proto * rows, 0, rows)
                live = jnp.where((lane >= start) & (lane < end), 1.0, live)
                start += rows
    return live


def pack_lanes(values):
    pieces = [values[:, k : k + LANES] for k in range(0, values.shape[1], LANES)]
    return jnp.concatenate(pieces + [jnp.zeros((8 - len(pieces), LANES), jnp.float32)], axis=0)


def unpack_lanes(tile, lanes):
    return jnp.concatenate([tile[k : k + 1, :] for k in range(lanes // LANES)], axis=1)


def as_column(values):
    return jnp.broadcast_to(values, (LANES, values.shape[1])).T


def as_tile(partial):
    return pack_lanes(jnp.sum(partial.T, axis=0, keepdims=True))


def inverse_rows(tile, rows):
    total = unpack_lanes(tile, rows)
    live = total > 0.0
    return jnp.where(live, 1.0 / jnp.where(live, total, 1.0), 0.0)


def place_rows(place, ref, which, rows, scratch):
    mine_x, mine_y = (place[1] >> 1) & 1, (place[1] >> 2) & 1
    start = 0
    for t in range(ref.shape[1]):
        for x in range(2):
            for y in range(2):
                block = ref[mine_y ^ y, t, mine_x ^ x].astype(jnp.float32)
                scratch[start : start + rows, :] = block[which * rows : (which + 1) * rows]
                start += rows
    unit, _ = quick_unit(scratch[...])
    return unit.astype(jnp.bfloat16)


def scores_of(rows_all, units):
    return lax.dot_general(
        rows_all, units, (((1,), (1,)), ((), ())), preferred_element_type=jnp.float32
    )


def twice(column):
    return jnp.concatenate([column, column], axis=1)


def spread(column, lanes):
    return jnp.concatenate([column] * (lanes // LANES), axis=1)


def weighted_rows(panels, left, scale_ref, part_ref, add=False):
    tiles = panels[0].shape[1] // LANES
    scales = [scale_ref[:, left + k * LANES : left + (k + 1) * LANES] for k in range(tiles)]
    top = 0
    for ref in panels:

        def body(i, _, ref=ref, top=top):
            at = pl.ds(pl.multiple_of(i * 8, 8), 8)
            to = pl.ds(pl.multiple_of(i * 8 + top, 8), 8)
            sums = [None] * 4
            for k in range(tiles):
                term = ref[at, k * LANES : (k + 1) * LANES] * scales[k]
                sums[k % 4] = term if sums[k % 4] is None else sums[k % 4] + term
            total = (sums[0] + sums[1]) + (sums[2] + sums[3])
            part_ref[to, :] = part_ref[to, :] + total if add else total
            return 0

        lax.fori_loop(0, ref.shape[0] // 8, body, 0, unroll=24)
        top += ref.shape[0]


def column_scales(panels, left, row_ref, scale_ref):
    tiles = panels[0].shape[1] // LANES
    sums = [jnp.zeros((8, LANES), jnp.float32)] * tiles
    top = 0
    for ref in panels:

        def body(i, sums, ref=ref, top=top):
            at = pl.ds(pl.multiple_of(i * 8, 8), 8)
            row = row_ref[pl.ds(pl.multiple_of(i * 8 + top, 8), 8), :]
            return [
                total + ref[at, k * LANES : (k + 1) * LANES] * row for k, total in enumerate(sums)
            ]

        sums = lax.fori_loop(0, ref.shape[0] // 8, body, sums, unroll=24)
        top += ref.shape[0]
    for k, total in enumerate(sums):
        inverse = 1.0 / jnp.sum(total, axis=0, keepdims=True)
        at = slice(left + k * LANES, left + (k + 1) * LANES)
        scale_ref[:, at] = jnp.broadcast_to(inverse, (8, LANES))


def weights_of(rows, units, live):
    weights = jnp.exp(scores_of(rows, units) * (1 / teacher_temp)) * live
    return weights, fold(weights)


def fold(values):
    return jnp.sum(values.reshape(values.shape[0] // 8, 8, values.shape[1]), axis=0)


def units_kernel(n_dp, rows, place_ref, proto_ref, units_ref, *live_refs):
    units_ref[...] = quick_unit(proto_ref[...])[0].astype(jnp.bfloat16)
    for k, live_ref in enumerate(live_refs):
        live_ref[...] = as_column(live_lanes(place_ref, k, live_ref.shape[0], n_dp, rows))


def near_kernel(chunk, near_ref, live_ref, own_units_ref, proto_ref, *refs):
    weights_ref, sums_ref, rows_ref, units_ref, scratch = refs
    rows = near_ref.shape[3] // 2
    rows_near = place_rows(own_place(), near_ref, 0, rows, scratch)
    rows_ref[...] = rows_near
    live = spread(live_ref[...], chunk)
    protos = own_units_ref.shape[0]
    for start in range(0, 2 * protos, chunk):
        at = slice(start, start + chunk)
        if start < protos:
            units = own_units_ref[at, :]
        else:
            here = slice(start - protos, start - protos + chunk)
            units = quick_unit(proto_ref[here, :])[0].astype(jnp.bfloat16)
            units_ref[here, :] = units
        weights_ref[:, at], sums_ref[:, at] = weights_of(rows_near, units, live)


def far_kernel(chunk, far_ref, live_ref, near_weights_ref, near_sums_ref, *refs):
    *unit_refs, weights_ref, rows_ref, sums_ref, scratch, scale_ref, part_ref = refs
    rows = far_ref.shape[3] // 2
    rows_far = place_rows(own_place(), far_ref, 0, rows, scratch)
    rows_ref[...] = rows_far
    live = spread(live_ref[...], chunk)
    protos = unit_refs[0].shape[0]
    for k, unit_ref in enumerate(unit_refs):
        for start in range(0, protos, chunk):
            at = slice(k * protos + start, k * protos + start + chunk)
            weights, sums = weights_of(rows_far, unit_ref[start : start + chunk, :], live)
            weights_ref[:, at] = weights
            inverse = 1.0 / jnp.sum(near_sums_ref[:, at] + sums, axis=0, keepdims=True)
            scale_ref[:, at] = jnp.broadcast_to(inverse, (8, chunk))
    weighted_rows([near_weights_ref, weights_ref], 0, scale_ref, part_ref)
    sums_ref[...] = as_tile(part_ref[...])


def across_kernel(chunk, near_ref, far_ref, *refs):
    near_rows_ref, far_rows_ref, near_live_ref, far_live_ref, *refs = refs
    *proto_refs, weights_ref, student_ref, scratch = refs
    protos = proto_refs[0].shape[0]
    rows_all = jnp.concatenate([near_rows_ref[...], far_rows_ref[...]], axis=0)
    live = spread(jnp.concatenate([near_live_ref[...], far_live_ref[...]], axis=0), chunk)
    for k, proto_ref in enumerate(proto_refs):
        for start in range(0, protos, chunk):
            units = quick_unit(proto_ref[start : start + chunk, :])[0].astype(jnp.bfloat16)
            at = slice(k * protos + start, k * protos + start + chunk)
            weights_ref[:, at], _ = weights_of(rows_all, units, live)
    half = student_ref.shape[0] // 2
    for k, ref in enumerate((near_ref, far_ref)):
        rows_half = place_rows(own_place(), ref, 1, ref.shape[3] // 2, scratch)
        student_ref[k * half : (k + 1) * half, :] = rows_half


def scale_columns(sums, near_ref, far_ref, across_ref, row_ref, scale_ref):
    row_ref[...] = as_column(inverse_rows(sums, row_ref.shape[0]))
    column_scales([near_ref, far_ref], 0, row_ref, scale_ref)
    column_scales([across_ref], near_ref.shape[1], row_ref, scale_ref)


def next_sums(near_ref, far_ref, across_ref, scale_ref, part_ref):
    weighted_rows([near_ref, far_ref], 0, scale_ref, part_ref)
    weighted_rows([across_ref], near_ref.shape[1], scale_ref, part_ref, add=True)
    return as_tile(part_ref[...])


def step_kernel(mine_ref, other_ref, near_ref, far_ref, across_ref, sums_ref, *scratch):
    row_ref, scale_ref, part_ref = scratch
    sums = mine_ref[...] + other_ref[...]
    scale_columns(sums, near_ref, far_ref, across_ref, row_ref, scale_ref)
    sums_ref[...] = next_sums(near_ref, far_ref, across_ref, scale_ref, part_ref)


def split(values):
    high = values.astype(jnp.bfloat16)
    low = (values - high.astype(jnp.float32)).astype(jnp.bfloat16)
    return jnp.concatenate([high, low], axis=0)


def exps_kernel(chunk, rows_ref, *refs):
    *proto_refs, units_ref, pull_ref, sums_ref, exps_ref = refs
    all_rows = rows_ref.shape[0]
    protos = proto_refs[0].shape[0]
    first = pull_ref.shape[0]
    rows_all = rows_ref[...]
    part = jnp.zeros((all_rows, LANES), jnp.float32)
    pull = jnp.zeros((2 * first, pull_ref.shape[1]), jnp.float32)
    for k, proto_ref in enumerate(proto_refs):
        for start in range(0, protos, chunk):
            units = quick_unit(proto_ref[start : start + chunk, :])[0].astype(jnp.bfloat16)
            units_ref[k * protos + start : k * protos + start + chunk, :] = units
            exps_ref[...] = jnp.exp(scores_of(rows_all, units) * (1 / student_temp))
            for at in range(0, chunk, LANES):
                part = part + exps_ref[:, at : at + LANES]
            exps = split(exps_ref[:first, :])
            pull = pull + jnp.dot(exps, units, preferred_element_type=jnp.float32)
    pull_ref[...] = pull[:first] + pull[first:]
    sums_ref[...] = as_tile(part)


def last_kernel(chunk, rows, mine_ref, other_ref, near_ref, far_ref, across_ref, *refs):
    units_ref, exp_pull_ref, exp_sums_ref, scale_ref, keep_ref, send_ref, row_ref, blocks_ref = refs
    first = exp_pull_ref.shape[0]
    sums = mine_ref[...] + other_ref[...]
    scale_columns(sums, near_ref, far_ref, across_ref, row_ref, scale_ref)
    pull = jnp.zeros((2 * first, exp_pull_ref.shape[1]), jnp.float32)
    for start in range(0, units_ref.shape[0], chunk):
        at = slice(start, start + chunk)
        scaled = split(near_ref[:first, at] * scale_ref[:1, at])
        pull = pull + jnp.dot(scaled, units_ref[at, :], preferred_element_type=jnp.float32)
    pulls = (pull[:first] + pull[first:], exp_pull_ref[...])
    for k, pull in enumerate(pulls):
        for block in range(4):
            blocks_ref[k, block, :rows, :] = pull[block * rows : (block + 1) * rows]
    _, mine = own_place()
    for ref, proto in ((keep_ref, mine), (send_ref, mine ^ X)):
        for j, owner in enumerate((proto, proto ^ Y)):
            for k in range(2):
                start = (2 * j + k) * rows
                ref[start : start + rows, :] = blocks_ref[k, block_of(owner), :rows, :]
        ref[4 * rows :, :LANES] = exp_sums_ref[...]
        ref[4 * rows :, LANES:] = jnp.zeros_like(exp_sums_ref)


def last_sums_kernel(near_ref, far_ref, across_ref, scale_ref, sums_ref, part_ref):
    sums_ref[:, :LANES] = jnp.zeros_like(sums_ref[:, :LANES])
    sums_ref[:, LANES:] = next_sums(near_ref, far_ref, across_ref, scale_ref, part_ref)


def own_kernel(mine_ref, other_ref, near_rows_ref, far_rows_ref, *refs):
    student_rows_ref, teacher_proto_ref, proto_ref, *refs = refs
    targets_ref, exps_ref, unit_ref, scale_ref = refs
    teacher_rows = jnp.concatenate([near_rows_ref[...], far_rows_ref[...]], axis=0)
    own, all_rows = targets_ref.shape
    row_scale = inverse_rows(mine_ref[...] + other_ref[...], all_rows)
    live = jnp.where(row_scale > 0.0, 1.0, 0.0)
    first = pl.ds(pl.multiple_of(own_place()[0] * own, own), own)
    units = quick_unit(teacher_proto_ref[first, :])[0].astype(jnp.bfloat16)
    weights = jnp.exp(scores_of(units, teacher_rows) * (1 / teacher_temp)) * live
    inverse = 1.0 / jnp.sum(weights * row_scale, axis=1, keepdims=True)
    targets_ref[...] = weights * (inverse * (1 / student_temp))
    unit, scale = quick_unit(proto_ref[first, :])
    unit_ref[...] = unit
    scale_ref[...] = jnp.broadcast_to(scale, scale_ref.shape)
    units = unit.astype(jnp.bfloat16)
    exps = jnp.exp(scores_of(units, student_rows_ref[...]) * (1 / student_temp))
    exps_ref[...] = exps * (1 / student_temp)


def grads_kernel(mine_ref, sums_ref, other_ref, targets_ref, exps_ref, *refs):
    unit_ref, scale_ref, rows_ref, feat_ref, student_out_ref, proto_out_ref = refs
    all_rows = targets_ref.shape[1]
    rows = feat_ref.shape[0]
    sums = sums_ref[...] + other_ref[2 * rows :, :]
    target_scale = inverse_rows(sums[:, LANES:], all_rows)
    exp_scale = jnp.where(target_scale > 0.0, 1.0 / unpack_lanes(sums[:, :LANES], all_rows), 0.0)

    grad = exps_ref[...] * exp_scale - targets_ref[...] * target_scale
    pushed = jnp.dot(grad.astype(jnp.bfloat16), rows_ref[...], preferred_element_type=jnp.float32)
    unit = unit_ref[...]
    along = jnp.sum(unit * pushed, axis=1, keepdims=True)
    proto_out_ref[0] = (pushed - unit * along) * twice(scale_ref[...])

    row = lax.broadcasted_iota(jnp.int32, (rows, LANES), 0) + block_of(own_place()[1]) * rows
    here = lax.broadcasted_iota(jnp.int32, (rows, LANES), 1) == row
    target_column, exp_column = [
        jnp.sum(jnp.where(here, scale[:, :LANES], 0.0), axis=1, keepdims=True) * (1 / student_temp)
        for scale in (target_scale, exp_scale)
    ]
    target_pull, exp_pull = [
        mine_ref[k * rows : (k + 1) * rows, :] + other_ref[k * rows : (k + 1) * rows, :]
        for k in range(2)
    ]
    pulled = exp_pull * exp_column - target_pull * target_column
    unit, scale = quick_unit(feat_ref[...])
    student_out_ref[...] = (
        pulled - unit * jnp.sum(unit * pulled, axis=1, keepdims=True)
    ) * scale


def call(kernel, out_shape, operands, smem=0, scratch=(), work=0):
    vmem = pl.BlockSpec(memory_space=pltpu.VMEM)
    return pl.pallas_call(
        kernel,
        out_shape=out_shape,
        in_specs=[pl.BlockSpec(memory_space=pltpu.SMEM)] * smem + [vmem] * (len(operands) - smem),
        out_specs=jax.tree.map(lambda _: vmem, out_shape),
        scratch_shapes=scratch,
        compiler_params=pltpu.CompilerParams(vmem_limit_bytes=24 * 2**20),
        cost_estimate=pl.CostEstimate(
            flops=512 * work, bytes_accessed=4 * work, transcendentals=work
        ),
    )(*operands)


def swap(values, axis, distance):
    others = [(k, k ^ distance) for k in range(lax.axis_size(axis))]
    return lax.ppermute(values, axis, others)


def swap_dp(values, t):
    n_dp, n_proto = lax.axis_size("dp"), lax.axis_size("proto")
    others = [
        (d * n_proto + p, (d ^ t) * n_proto + (p ^ CORE)) for d in range(n_dp) for p in range(n_proto)
    ]
    return lax.ppermute(values, ("dp", "proto"), others)


def on_device_all_rows(student_feat, teacher_feat, prototypes, teacher_prototypes, live_count):
    n_dp, n_proto = lax.axis_size("dp"), lax.axis_size("proto")
    rows, width = student_feat.shape
    protos = prototypes.shape[0]
    own = protos // n_dp
    piece = 2 * own
    all_rows = n_dp * n_proto * rows
    half = all_rows // 2
    first = 4 * rows
    held = 2 * protos
    f32 = functools.partial(jax.ShapeDtypeStruct, dtype=jnp.float32)
    bf16 = functools.partial(jax.ShapeDtypeStruct, dtype=jnp.bfloat16)
    place = jnp.stack([lax.axis_index("dp"), lax.axis_index("proto")]).astype(jnp.int32)
    place = jnp.concatenate([place, live_count])
    tile = f32((8, LANES))
    message = f32((4 * rows + 8, width))
    row_scratch = pltpu.VMEM((half, width), jnp.float32)
    column = pltpu.VMEM((all_rows, LANES), jnp.float32)
    scale_row = pltpu.VMEM((8, held), jnp.float32)
    sweep_scratch = [column, pltpu.VMEM((8, 2 * held), jnp.float32), column]

    both = lax.optimization_barrier(jnp.concatenate([teacher_feat, student_feat], axis=0))
    across_x = swap(both, "proto", X_CROSS)
    across_x, late_protos, place = lax.optimization_barrier((across_x, teacher_prototypes, place))
    across_protos = swap(late_protos, "proto", X_CROSS)
    student_protos = (prototypes, swap(prototypes, "proto", CORE))
    teacher_protos = swap(late_protos, "proto", CORE)
    near = jnp.stack([both, across_x])
    near = jnp.stack([near] + [swap_dp(near, t) for t in dp_order(n_dp)[1:]])
    near, own_protos = lax.optimization_barrier((near, teacher_prototypes))
    live = f32((half, LANES))
    teacher_units, near_live, far_live = call(
        functools.partial(units_kernel, n_dp, rows),
        (bf16((protos, width)), live, live),
        (place, own_protos),
        smem=1,
        work=protos * width,
    )
    near = jnp.stack([near, swap(near, "proto", Y_CROSS)])
    near, teacher_units = lax.optimization_barrier((near, teacher_units))
    far = swap(near, "proto", CORE)

    near_weights, near_sums, near_rows, other_units = call(
        functools.partial(near_kernel, piece),
        (
            f32((half, held)),
            f32((8, held)),
            bf16((half, width)),
            bf16((protos, width)),
        ),
        (near, near_live, teacher_units, teacher_protos),
        scratch=[row_scratch],
        work=held * half,
    )
    far_weights, far_rows, sums = call(
        functools.partial(far_kernel, piece),
        (f32((half, held)), bf16((half, width)), tile),
        (far, far_live, near_weights, near_sums, teacher_units, other_units),
        scratch=[row_scratch, scale_row, column],
        work=held * half,
    )
    sums = sums + swap(sums, "proto", Y_CROSS)
    sums, across_protos = lax.optimization_barrier((sums, across_protos))
    parts = (sums, swap(sums, "proto", X_CROSS))
    across_weights, student_rows = call(
        functools.partial(across_kernel, piece),
        (f32((all_rows, held)), bf16((all_rows, width))),
        (
            near,
            far,
            near_rows,
            far_rows,
            near_live,
            far_live,
            across_protos,
            swap(across_protos, "proto", CORE),
        ),
        scratch=[row_scratch],
        work=held * all_rows,
    )
    weights = (near_weights, far_weights, across_weights)
    for _ in range(ITERS - 2):
        sums = call(
            step_kernel,
            tile,
            (*parts, *weights),
            scratch=sweep_scratch,
            work=held * all_rows,
        )
        sums, student_rows, *student_protos = lax.optimization_barrier(
            (sums, student_rows, *student_protos)
        )
        parts = (sums, swap(sums, "proto", Y_CROSS))
    student_units, exp_pull, exp_sums = call(
        functools.partial(exps_kernel, piece),
        (bf16((held, width)), f32((first, width)), tile),
        (student_rows, *student_protos),
        scratch=[pltpu.VMEM((all_rows, piece), jnp.float32)],
        work=held * all_rows,
    )
    scales, keep, send = call(
        functools.partial(last_kernel, own, rows),
        (f32((8, 2 * held)), message, message),
        (*parts, *weights, student_units, exp_pull, exp_sums),
        scratch=[column, pltpu.VMEM((2, 4, 16, width), jnp.float32)],
        work=held * all_rows,
    )
    last_sums = call(
        last_sums_kernel,
        f32((8, width)),
        (*weights, scales),
        scratch=[column],
        work=held * all_rows,
    )
    *parts, send = lax.optimization_barrier((*parts, send))
    targets, exps, own_units, own_scales = call(
        own_kernel,
        (f32((own, all_rows)), f32((own, all_rows)), f32((own, width)), f32((own, LANES))),
        (*parts, near_rows, far_rows, student_rows, teacher_prototypes, prototypes),
        work=own * all_rows,
    )
    total = keep + swap(send, "proto", X_CROSS)
    last_sums = total[4 * rows :] + last_sums
    return call(
        grads_kernel,
        (f32((rows, width)), f32((1, own, width))),
        (
            total,
            last_sums,
            swap(jnp.concatenate([total[2 * rows : 4 * rows], last_sums]), "proto", Y_CROSS),
            targets,
            exps,
            own_units,
            own_scales,
            student_rows,
            student_feat,
        ),
        work=own * all_rows,
    )


def sample_totals(values):
    return lax.psum(values, "proto")


def proto_totals(values):
    return lax.psum(values, "dp")


def on_device_group_rows(student_feat, teacher_feat, prototypes, teacher_prototypes, live_count):
    student_unit, student_length = unit_rows(student_feat)
    teacher_unit, teacher_length = unit_rows(teacher_feat)
    proto_unit, proto_length = unit_rows(prototypes)
    teacher_proto, teacher_proto_length = unit_rows(teacher_prototypes)
    proto_bf = proto_unit.astype(jnp.bfloat16)
    teacher_proto_bf = teacher_proto.astype(jnp.bfloat16)
    student_rows, teacher_rows = (
        lax.all_gather(student_unit.astype(jnp.bfloat16), "proto", axis=0, tiled=True),
        lax.all_gather(teacher_unit.astype(jnp.bfloat16), "proto", axis=0, tiled=True),
    )
    group_size = student_rows.shape[0]
    live_rows = live_count[lax.axis_index("dp")]
    live_mask = jnp.arange(group_size, dtype=jnp.int32) < live_rows
    live_column = live_mask[:, None]
    contract_last = (((1,), (1,)), ((), ()))
    logits = (
        lax.dot_general(student_rows, proto_bf, contract_last, preferred_element_type=jnp.float32)
        / student_temp
    )
    teacher_scores = (
        lax.dot_general(
            teacher_rows, teacher_proto_bf, contract_last, preferred_element_type=jnp.float32
        )
        / teacher_temp
    )
    weights = jnp.where(live_column, jnp.exp(teacher_scores), 0.0)
    partition = sample_totals(jnp.sum(jnp.exp(logits), axis=1))
    targets = weights
    for iteration in range(ITERS):
        targets = targets / proto_totals(jnp.sum(targets, axis=0))[None, :]
        row_sums = sample_totals(jnp.sum(targets, axis=1))
        targets = targets / jnp.where(live_mask, row_sums, 1.0)[:, None]
    student_probs = jnp.exp(logits - jnp.log(partition)[:, None])
    grad_block = jnp.where(live_column, (student_probs - targets) / student_temp, 0.0).astype(
        jnp.bfloat16
    )
    pulled = lax.psum_scatter(
        jnp.dot(grad_block, proto_bf, preferred_element_type=jnp.float32),
        "proto",
        scatter_dimension=0,
        tiled=True,
    )
    student_grad = (
        pulled - student_unit * jnp.sum(student_unit * pulled, axis=1, keepdims=True)
    ) / student_length
    own_protos = prototypes.shape[0] // lax.axis_size("dp")
    contract_first = (((0,), (0,)), ((), ()))
    pushed = lax.psum_scatter(
        lax.dot_general(
            grad_block, student_rows, contract_first, preferred_element_type=jnp.float32
        ),
        "dp",
        scatter_dimension=0,
        tiled=True,
    )
    first_proto = lax.axis_index("dp") * own_protos
    own_units = lax.dynamic_slice_in_dim(proto_unit, first_proto, own_protos, 0)
    own_lengths = lax.dynamic_slice_in_dim(proto_length, first_proto, own_protos, 0)
    proto_grad = (
        pushed - own_units * jnp.sum(own_units * pushed, axis=1, keepdims=True)
    ) / own_lengths
    return (student_grad, proto_grad[None])


def on_device(student_feat, teacher_feat, prototypes, teacher_prototypes, live_count):
    n_dp, n_proto = lax.axis_size("dp"), lax.axis_size("proto")
    rows, width = student_feat.shape
    protos = prototypes.shape[0]
    lanes = n_dp * n_proto * rows
    fits = (
        n_proto == 2 * Y
        and n_dp & (n_dp - 1) == 0
        and rows % 4 == 0
        and rows <= 16
        and lanes % LANES == 0
        and lanes <= 8 * LANES
        and width == 2 * LANES
        and protos == n_dp * 2 * LANES
        and 4 * protos * lanes * 4 <= BLOCK_BYTES
    )
    plan = on_device_all_rows if fits else on_device_group_rows
    return plan(student_feat, teacher_feat, prototypes, teacher_prototypes, live_count)


def solution(mesh):
    return jax.shard_map(
        on_device,
        mesh=mesh,
        in_specs=(
            P(("dp", "proto"), None),
            P(("dp", "proto"), None),
            P("proto", None),
            P("proto", None),
            P(),
        ),
        out_specs=(P(("dp", "proto"), None), P("proto", "dp", None)),
        check_vma=False,
    )
```

```python
import functools

import jax
import jax.numpy as jnp
from jax import lax
from jax.experimental import pallas as pl
from jax.experimental.pallas import tpu as pltpu
from jax.sharding import PartitionSpec as P

ITERS = 3

student_temp = 0.1
teacher_temp = 0.07
eps_norm = 1e-06

LANES = 128
BLOCK_BYTES = 8 * 2**20


def unit_rows(values):
    widened = values.astype(jnp.float32)
    length = jnp.sqrt(jnp.sum(widened * widened, axis=1, keepdims=True) + eps_norm)
    return (widened / length, length)


CORE, X, Y = 1, 2, 4
X_CROSS, Y_CROSS = X | CORE, Y | CORE


def block_of(proto):
    return (proto & X) + ((proto >> 2) & 1)


def own_place():
    return lax.axis_index("dp"), lax.axis_index("proto")


def quick_unit(values):
    widened = values.astype(jnp.float32)
    squares = jnp.sum(widened * widened, axis=1, keepdims=True) + eps_norm
    scale = lax.rsqrt(squares)
    return widened * scale, scale


def dp_order(n_dp):
    return [0, *reversed(range(1, n_dp))]


def live_lanes(place_ref, half, lanes, n_dp, rows):
    mine = place_ref[1]
    parity = (mine ^ (mine >> 1) ^ (mine >> 2)) & 1
    lane = lax.broadcasted_iota(jnp.int32, (1, lanes), 1)
    live = jnp.zeros((1, lanes), jnp.float32)
    start = 0
    for t in dp_order(n_dp):
        count = place_ref[2 + (place_ref[0] ^ t)]
        for x in range(2):
            for y in range(2):
                core = parity ^ x ^ y ^ half ^ (1 if t else 0)
                proto = core + X * x + Y * y
                end = start + jnp.clip(count - proto * rows, 0, rows)
                live = jnp.where((lane >= start) & (lane < end), 1.0, live)
                start += rows
    return live


def pack_lanes(values):
    pieces = [values[:, k : k + LANES] for k in range(0, values.shape[1], LANES)]
    return jnp.concatenate(pieces + [jnp.zeros((8 - len(pieces), LANES), jnp.float32)], axis=0)


def unpack_lanes(tile, lanes):
    return jnp.concatenate([tile[k : k + 1, :] for k in range(lanes // LANES)], axis=1)


def as_column(values):
    return jnp.broadcast_to(values, (LANES, values.shape[1])).T


def as_tile(partial):
    return pack_lanes(jnp.sum(partial.T, axis=0, keepdims=True))


def inverse_rows(tile, rows):
    total = unpack_lanes(tile, rows)
    live = total > 0.0
    return jnp.where(live, 1.0 / jnp.where(live, total, 1.0), 0.0)


def place_rows(place, ref, which, rows, scratch):
    mine_x, mine_y = (place[1] >> 1) & 1, (place[1] >> 2) & 1
    start = 0
    for t in range(ref.shape[1]):
        for x in range(2):
            for y in range(2):
                block = ref[mine_y ^ y, t, mine_x ^ x].astype(jnp.float32)
                scratch[start : start + rows, :] = block[which * rows : (which + 1) * rows]
                start += rows
    unit, _ = quick_unit(scratch[...])
    return unit.astype(jnp.bfloat16)


def scores_of(rows_all, units):
    return lax.dot_general(
        rows_all, units, (((1,), (1,)), ((), ())), preferred_element_type=jnp.float32
    )


def twice(column):
    return jnp.concatenate([column, column], axis=1)


def spread(column, lanes):
    return jnp.concatenate([column] * (lanes // LANES), axis=1)


def weighted_rows(panels, left, scale_ref, part_ref, add=False):
    tiles = panels[0].shape[1] // LANES
    scales = [scale_ref[:, left + k * LANES : left + (k + 1) * LANES] for k in range(tiles)]
    top = 0
    for ref in panels:

        def body(i, _, ref=ref, top=top):
            at = pl.ds(pl.multiple_of(i * 8, 8), 8)
            to = pl.ds(pl.multiple_of(i * 8 + top, 8), 8)
            sums = [None] * 4
            for k in range(tiles):
                term = ref[at, k * LANES : (k + 1) * LANES] * scales[k]
                sums[k % 4] = term if sums[k % 4] is None else sums[k % 4] + term
            total = (sums[0] + sums[1]) + (sums[2] + sums[3])
            part_ref[to, :] = part_ref[to, :] + total if add else total
            return 0

        lax.fori_loop(0, ref.shape[0] // 8, body, 0, unroll=24)
        top += ref.shape[0]


def column_scales(panels, left, row_ref, scale_ref):
    tiles = panels[0].shape[1] // LANES
    sums = [jnp.zeros((8, LANES), jnp.float32)] * tiles
    top = 0
    for ref in panels:

        def body(i, sums, ref=ref, top=top):
            at = pl.ds(pl.multiple_of(i * 8, 8), 8)
            row = row_ref[pl.ds(pl.multiple_of(i * 8 + top, 8), 8), :]
            return [
                total + ref[at, k * LANES : (k + 1) * LANES] * row for k, total in enumerate(sums)
            ]

        sums = lax.fori_loop(0, ref.shape[0] // 8, body, sums, unroll=24)
        top += ref.shape[0]
    for k, total in enumerate(sums):
        inverse = 1.0 / jnp.sum(total, axis=0, keepdims=True)
        at = slice(left + k * LANES, left + (k + 1) * LANES)
        scale_ref[:, at] = jnp.broadcast_to(inverse, (8, LANES))


def weights_of(rows, units, live):
    weights = jnp.exp(scores_of(rows, units) * (1 / teacher_temp)) * live
    return weights, fold(weights)


def fold(values):
    return jnp.sum(values.reshape(values.shape[0] // 8, 8, values.shape[1]), axis=0)


def units_kernel(n_dp, rows, place_ref, proto_ref, units_ref, *live_refs):
    units_ref[...] = quick_unit(proto_ref[...])[0].astype(jnp.bfloat16)
    for k, live_ref in enumerate(live_refs):
        live_ref[...] = as_column(live_lanes(place_ref, k, live_ref.shape[0], n_dp, rows))


def near_kernel(chunk, near_ref, live_ref, own_units_ref, proto_ref, *refs):
    weights_ref, sums_ref, rows_ref, units_ref, scratch = refs
    rows = near_ref.shape[3] // 2
    rows_near = place_rows(own_place(), near_ref, 0, rows, scratch)
    rows_ref[...] = rows_near
    live = spread(live_ref[...], chunk)
    protos = own_units_ref.shape[0]
    for start in range(0, 2 * protos, chunk):
        at = slice(start, start + chunk)
        if start < protos:
            units = own_units_ref[at, :]
        else:
            here = slice(start - protos, start - protos + chunk)
            units = quick_unit(proto_ref[here, :])[0].astype(jnp.bfloat16)
            units_ref[here, :] = units
        weights_ref[:, at], sums_ref[:, at] = weights_of(rows_near, units, live)


def far_kernel(chunk, far_ref, live_ref, near_weights_ref, near_sums_ref, *refs):
    *unit_refs, weights_ref, rows_ref, sums_ref, scratch, scale_ref, part_ref = refs
    rows = far_ref.shape[3] // 2
    rows_far = place_rows(own_place(), far_ref, 0, rows, scratch)
    rows_ref[...] = rows_far
    live = spread(live_ref[...], chunk)
    protos = unit_refs[0].shape[0]
    for k, unit_ref in enumerate(unit_refs):
        for start in range(0, protos, chunk):
            at = slice(k * protos + start, k * protos + start + chunk)
            weights, sums = weights_of(rows_far, unit_ref[start : start + chunk, :], live)
            weights_ref[:, at] = weights
            inverse = 1.0 / jnp.sum(near_sums_ref[:, at] + sums, axis=0, keepdims=True)
            scale_ref[:, at] = jnp.broadcast_to(inverse, (8, chunk))
    weighted_rows([near_weights_ref, weights_ref], 0, scale_ref, part_ref)
    sums_ref[...] = as_tile(part_ref[...])


def across_kernel(chunk, near_ref, far_ref, *refs):
    near_rows_ref, far_rows_ref, near_live_ref, far_live_ref, *refs = refs
    *proto_refs, weights_ref, student_ref, scratch = refs
    protos = proto_refs[0].shape[0]
    rows_all = jnp.concatenate([near_rows_ref[...], far_rows_ref[...]], axis=0)
    live = spread(jnp.concatenate([near_live_ref[...], far_live_ref[...]], axis=0), chunk)
    for k, proto_ref in enumerate(proto_refs):
        for start in range(0, protos, chunk):
            units = quick_unit(proto_ref[start : start + chunk, :])[0].astype(jnp.bfloat16)
            at = slice(k * protos + start, k * protos + start + chunk)
            weights_ref[:, at], _ = weights_of(rows_all, units, live)
    half = student_ref.shape[0] // 2
    for k, ref in enumerate((near_ref, far_ref)):
        rows_half = place_rows(own_place(), ref, 1, ref.shape[3] // 2, scratch)
        student_ref[k * half : (k + 1) * half, :] = rows_half


def scale_columns(sums, near_ref, far_ref, across_ref, row_ref, scale_ref):
    row_ref[...] = as_column(inverse_rows(sums, row_ref.shape[0]))
    column_scales([near_ref, far_ref], 0, row_ref, scale_ref)
    column_scales([across_ref], near_ref.shape[1], row_ref, scale_ref)


def next_sums(near_ref, far_ref, across_ref, scale_ref, part_ref):
    weighted_rows([near_ref, far_ref], 0, scale_ref, part_ref)
    weighted_rows([across_ref], near_ref.shape[1], scale_ref, part_ref, add=True)
    return as_tile(part_ref[...])


def step_kernel(mine_ref, other_ref, near_ref, far_ref, across_ref, sums_ref, *scratch):
    row_ref, scale_ref, part_ref = scratch
    sums = mine_ref[...] + other_ref[...]
    scale_columns(sums, near_ref, far_ref, across_ref, row_ref, scale_ref)
    sums_ref[...] = next_sums(near_ref, far_ref, across_ref, scale_ref, part_ref)


def split(values):
    high = values.astype(jnp.bfloat16)
    low = (values - high.astype(jnp.float32)).astype(jnp.bfloat16)
    return jnp.concatenate([high, low], axis=0)


def exps_kernel(chunk, rows_ref, *refs):
    *proto_refs, units_ref, pull_ref, sums_ref, exps_ref = refs
    all_rows = rows_ref.shape[0]
    protos = proto_refs[0].shape[0]
    first = pull_ref.shape[0]
    rows_all = rows_ref[...]
    part = jnp.zeros((all_rows, LANES), jnp.float32)
    pull = jnp.zeros((2 * first, pull_ref.shape[1]), jnp.float32)
    for k, proto_ref in enumerate(proto_refs):
        for start in range(0, protos, chunk):
            units = quick_unit(proto_ref[start : start + chunk, :])[0].astype(jnp.bfloat16)
            units_ref[k * protos + start : k * protos + start + chunk, :] = units
            exps_ref[...] = jnp.exp(scores_of(rows_all, units) * (1 / student_temp))
            for at in range(0, chunk, LANES):
                part = part + exps_ref[:, at : at + LANES]
            exps = split(exps_ref[:first, :])
            pull = pull + jnp.dot(exps, units, preferred_element_type=jnp.float32)
    pull_ref[...] = pull[:first] + pull[first:]
    sums_ref[...] = as_tile(part)


def last_kernel(chunk, rows, mine_ref, other_ref, near_ref, far_ref, across_ref, *refs):
    units_ref, exp_pull_ref, exp_sums_ref, scale_ref, keep_ref, send_ref, row_ref, blocks_ref = refs
    first = exp_pull_ref.shape[0]
    sums = mine_ref[...] + other_ref[...]
    scale_columns(sums, near_ref, far_ref, across_ref, row_ref, scale_ref)
    pull = jnp.zeros((2 * first, exp_pull_ref.shape[1]), jnp.float32)
    for start in range(0, units_ref.shape[0], chunk):
        at = slice(start, start + chunk)
        scaled = split(near_ref[:first, at] * scale_ref[:1, at])
        pull = pull + jnp.dot(scaled, units_ref[at, :], preferred_element_type=jnp.float32)
    pulls = (pull[:first] + pull[first:], exp_pull_ref[...])
    for k, pull in enumerate(pulls):
        for block in range(4):
            blocks_ref[k, block, :rows, :] = pull[block * rows : (block + 1) * rows]
    _, mine = own_place()
    for ref, proto in ((keep_ref, mine), (send_ref, mine ^ X)):
        for j, owner in enumerate((proto, proto ^ Y)):
            for k in range(2):
                start = (2 * j + k) * rows
                ref[start : start + rows, :] = blocks_ref[k, block_of(owner), :rows, :]
        ref[4 * rows :, :LANES] = exp_sums_ref[...]
        ref[4 * rows :, LANES:] = jnp.zeros_like(exp_sums_ref)


def last_sums_kernel(near_ref, far_ref, across_ref, scale_ref, sums_ref, part_ref):
    sums_ref[:, :LANES] = jnp.zeros_like(sums_ref[:, :LANES])
    sums_ref[:, LANES:] = next_sums(near_ref, far_ref, across_ref, scale_ref, part_ref)


def own_kernel(mine_ref, other_ref, near_rows_ref, far_rows_ref, *refs):
    student_rows_ref, teacher_proto_ref, proto_ref, feat_ref, *refs = refs
    targets_ref, exps_ref, unit_ref, scale_ref, row_unit_ref, row_scale_ref = refs
    teacher_rows = jnp.concatenate([near_rows_ref[...], far_rows_ref[...]], axis=0)
    own, all_rows = targets_ref.shape
    row_scale = inverse_rows(mine_ref[...] + other_ref[...], all_rows)
    live = jnp.where(row_scale > 0.0, 1.0, 0.0)
    first = pl.ds(pl.multiple_of(own_place()[0] * own, own), own)
    units = quick_unit(teacher_proto_ref[first, :])[0].astype(jnp.bfloat16)
    weights = jnp.exp(scores_of(units, teacher_rows) * (1 / teacher_temp)) * live
    inverse = 1.0 / jnp.sum(weights * row_scale, axis=1, keepdims=True)
    targets_ref[...] = weights * (inverse * (1 / student_temp))
    unit, scale = quick_unit(proto_ref[first, :])
    unit_ref[...] = unit
    scale_ref[...] = jnp.broadcast_to(scale, scale_ref.shape)
    units = unit.astype(jnp.bfloat16)
    exps = jnp.exp(scores_of(units, student_rows_ref[...]) * (1 / student_temp))
    exps_ref[...] = exps * (1 / student_temp)
    unit, scale = quick_unit(feat_ref[...])
    row_unit_ref[...] = unit
    row_scale_ref[...] = jnp.broadcast_to(scale, row_scale_ref.shape)


def grads_kernel(mine_ref, sums_ref, other_ref, targets_ref, exps_ref, *refs):
    unit_ref, scale_ref, rows_ref, row_unit_ref, row_scale_ref, *refs = refs
    student_out_ref, proto_out_ref = refs
    all_rows = targets_ref.shape[1]
    rows = row_unit_ref.shape[0]
    sums = sums_ref[...] + other_ref[2 * rows :, :]
    target_scale = inverse_rows(sums[:, LANES:], all_rows)
    exp_scale = jnp.where(target_scale > 0.0, 1.0 / unpack_lanes(sums[:, :LANES], all_rows), 0.0)

    grad = exps_ref[...] * exp_scale - targets_ref[...] * target_scale
    pushed = jnp.dot(grad.astype(jnp.bfloat16), rows_ref[...], preferred_element_type=jnp.float32)
    unit = unit_ref[...]
    along = jnp.sum(unit * pushed, axis=1, keepdims=True)
    proto_out_ref[0] = (pushed - unit * along) * scale_ref[...]

    row = lax.broadcasted_iota(jnp.int32, (rows, LANES), 0) + block_of(own_place()[1]) * rows
    here = lax.broadcasted_iota(jnp.int32, (rows, LANES), 1) == row
    target_column, exp_column = [
        jnp.sum(jnp.where(here, scale[:, :LANES], 0.0), axis=1, keepdims=True) * (1 / student_temp)
        for scale in (target_scale, exp_scale)
    ]
    target_pull, exp_pull = [
        mine_ref[k * rows : (k + 1) * rows, :] + other_ref[k * rows : (k + 1) * rows, :]
        for k in range(2)
    ]
    pulled = exp_pull * exp_column - target_pull * target_column
    unit = row_unit_ref[...]
    student_out_ref[...] = (
        pulled - unit * jnp.sum(unit * pulled, axis=1, keepdims=True)
    ) * row_scale_ref[...]


def call(kernel, out_shape, operands, smem=0, scratch=(), work=0):
    vmem = pl.BlockSpec(memory_space=pltpu.VMEM)
    return pl.pallas_call(
        kernel,
        out_shape=out_shape,
        in_specs=[pl.BlockSpec(memory_space=pltpu.SMEM)] * smem + [vmem] * (len(operands) - smem),
        out_specs=jax.tree.map(lambda _: vmem, out_shape),
        scratch_shapes=scratch,
        compiler_params=pltpu.CompilerParams(vmem_limit_bytes=24 * 2**20),
        cost_estimate=pl.CostEstimate(
            flops=512 * work, bytes_accessed=4 * work, transcendentals=work
        ),
    )(*operands)


def swap(values, axis, distance):
    others = [(k, k ^ distance) for k in range(lax.axis_size(axis))]
    return lax.ppermute(values, axis, others)


def swap_dp(values, t):
    n_dp, n_proto = lax.axis_size("dp"), lax.axis_size("proto")
    others = [
        (d * n_proto + p, (d ^ t) * n_proto + (p ^ CORE)) for d in range(n_dp) for p in range(n_proto)
    ]
    return lax.ppermute(values, ("dp", "proto"), others)


def on_device_all_rows(student_feat, teacher_feat, prototypes, teacher_prototypes, live_count):
    n_dp, n_proto = lax.axis_size("dp"), lax.axis_size("proto")
    rows, width = student_feat.shape
    protos = prototypes.shape[0]
    own = protos // n_dp
    piece = 2 * own
    all_rows = n_dp * n_proto * rows
    half = all_rows // 2
    first = 4 * rows
    held = 2 * protos
    f32 = functools.partial(jax.ShapeDtypeStruct, dtype=jnp.float32)
    bf16 = functools.partial(jax.ShapeDtypeStruct, dtype=jnp.bfloat16)
    place = jnp.stack([lax.axis_index("dp"), lax.axis_index("proto")]).astype(jnp.int32)
    place = jnp.concatenate([place, live_count])
    tile = f32((8, LANES))
    message = f32((4 * rows + 8, width))
    row_scratch = pltpu.VMEM((half, width), jnp.float32)
    column = pltpu.VMEM((all_rows, LANES), jnp.float32)
    scale_row = pltpu.VMEM((8, held), jnp.float32)
    sweep_scratch = [column, pltpu.VMEM((8, 2 * held), jnp.float32), column]

    both = lax.optimization_barrier(jnp.concatenate([teacher_feat, student_feat], axis=0))
    across_x = swap(both, "proto", X_CROSS)
    across_x, late_protos, place = lax.optimization_barrier((across_x, teacher_prototypes, place))
    across_protos = swap(late_protos, "proto", X_CROSS)
    student_protos = (prototypes, swap(prototypes, "proto", CORE))
    teacher_protos = swap(late_protos, "proto", CORE)
    near = jnp.stack([both, across_x])
    near = jnp.stack([near] + [swap_dp(near, t) for t in dp_order(n_dp)[1:]])
    near, own_protos = lax.optimization_barrier((near, teacher_prototypes))
    live = f32((half, LANES))
    teacher_units, near_live, far_live = call(
        functools.partial(units_kernel, n_dp, rows),
        (bf16((protos, width)), live, live),
        (place, own_protos),
        smem=1,
        work=protos * width,
    )
    near = jnp.stack([near, swap(near, "proto", Y_CROSS)])
    near, teacher_units = lax.optimization_barrier((near, teacher_units))
    far = swap(near, "proto", CORE)

    near_weights, near_sums, near_rows, other_units = call(
        functools.partial(near_kernel, piece),
        (
            f32((half, held)),
            f32((8, held)),
            bf16((half, width)),
            bf16((protos, width)),
        ),
        (near, near_live, teacher_units, teacher_protos),
        scratch=[row_scratch],
        work=held * half,
    )
    far_weights, far_rows, sums = call(
        functools.partial(far_kernel, piece),
        (f32((half, held)), bf16((half, width)), tile),
        (far, far_live, near_weights, near_sums, teacher_units, other_units),
        scratch=[row_scratch, scale_row, column],
        work=held * half,
    )
    sums = sums + swap(sums, "proto", Y_CROSS)
    sums, across_protos = lax.optimization_barrier((sums, across_protos))
    parts = (sums, swap(sums, "proto", X_CROSS))
    across_weights, student_rows = call(
        functools.partial(across_kernel, piece),
        (f32((all_rows, held)), bf16((all_rows, width))),
        (
            near,
            far,
            near_rows,
            far_rows,
            near_live,
            far_live,
            across_protos,
            swap(across_protos, "proto", CORE),
        ),
        scratch=[row_scratch],
        work=held * all_rows,
    )
    weights = (near_weights, far_weights, across_weights)
    for _ in range(ITERS - 2):
        sums = call(
            step_kernel,
            tile,
            (*parts, *weights),
            scratch=sweep_scratch,
            work=held * all_rows,
        )
        sums, student_rows, *student_protos = lax.optimization_barrier(
            (sums, student_rows, *student_protos)
        )
        parts = (sums, swap(sums, "proto", Y_CROSS))
    student_units, exp_pull, exp_sums = call(
        functools.partial(exps_kernel, piece),
        (bf16((held, width)), f32((first, width)), tile),
        (student_rows, *student_protos),
        scratch=[pltpu.VMEM((all_rows, piece), jnp.float32)],
        work=held * all_rows,
    )
    scales, keep, send = call(
        functools.partial(last_kernel, own, rows),
        (f32((8, 2 * held)), message, message),
        (*parts, *weights, student_units, exp_pull, exp_sums),
        scratch=[column, pltpu.VMEM((2, 4, 16, width), jnp.float32)],
        work=held * all_rows,
    )
    last_sums = call(
        last_sums_kernel,
        f32((8, width)),
        (*weights, scales),
        scratch=[column],
        work=held * all_rows,
    )
    *parts, send = lax.optimization_barrier((*parts, send))
    targets, exps, own_units, own_scales, row_units, row_scales = call(
        own_kernel,
        (f32((own, all_rows)), f32((own, all_rows)), *([f32((own, width))] * 2), *([f32((rows, width))] * 2)),
        (*parts, near_rows, far_rows, student_rows, teacher_prototypes, prototypes, student_feat),
        work=own * all_rows,
    )
    total = keep + swap(send, "proto", X_CROSS)
    last_sums = total[4 * rows :] + last_sums
    return call(
        grads_kernel,
        (f32((rows, width)), f32((1, own, width))),
        (
            total,
            last_sums,
            swap(jnp.concatenate([total[2 * rows : 4 * rows], last_sums]), "proto", Y_CROSS),
            targets,
            exps,
            own_units,
            own_scales,
            student_rows,
            row_units,
            row_scales,
        ),
        work=own * all_rows,
    )


def sample_totals(values):
    return lax.psum(values, "proto")


def proto_totals(values):
    return lax.psum(values, "dp")


def on_device_group_rows(student_feat, teacher_feat, prototypes, teacher_prototypes, live_count):
    student_unit, student_length = unit_rows(student_feat)
    teacher_unit, teacher_length = unit_rows(teacher_feat)
    proto_unit, proto_length = unit_rows(prototypes)
    teacher_proto, teacher_proto_length = unit_rows(teacher_prototypes)
    proto_bf = proto_unit.astype(jnp.bfloat16)
    teacher_proto_bf = teacher_proto.astype(jnp.bfloat16)
    student_rows, teacher_rows = (
        lax.all_gather(student_unit.astype(jnp.bfloat16), "proto", axis=0, tiled=True),
        lax.all_gather(teacher_unit.astype(jnp.bfloat16), "proto", axis=0, tiled=True),
    )
    group_size = student_rows.shape[0]
    live_rows = live_count[lax.axis_index("dp")]
    live_mask = jnp.arange(group_size, dtype=jnp.int32) < live_rows
    live_column = live_mask[:, None]
    contract_last = (((1,), (1,)), ((), ()))
    logits = (
        lax.dot_general(student_rows, proto_bf, contract_last, preferred_element_type=jnp.float32)
        / student_temp
    )
    teacher_scores = (
        lax.dot_general(
            teacher_rows, teacher_proto_bf, contract_last, preferred_element_type=jnp.float32
        )
        / teacher_temp
    )
    weights = jnp.where(live_column, jnp.exp(teacher_scores), 0.0)
    partition = sample_totals(jnp.sum(jnp.exp(logits), axis=1))
    targets = weights
    for iteration in range(ITERS):
        targets = targets / proto_totals(jnp.sum(targets, axis=0))[None, :]
        row_sums = sample_totals(jnp.sum(targets, axis=1))
        targets = targets / jnp.where(live_mask, row_sums, 1.0)[:, None]
    student_probs = jnp.exp(logits - jnp.log(partition)[:, None])
    grad_block = jnp.where(live_column, (student_probs - targets) / student_temp, 0.0).astype(
        jnp.bfloat16
    )
    pulled = lax.psum_scatter(
        jnp.dot(grad_block, proto_bf, preferred_element_type=jnp.float32),
        "proto",
        scatter_dimension=0,
        tiled=True,
    )
    student_grad = (
        pulled - student_unit * jnp.sum(student_unit * pulled, axis=1, keepdims=True)
    ) / student_length
    own_protos = prototypes.shape[0] // lax.axis_size("dp")
    contract_first = (((0,), (0,)), ((), ()))
    pushed = lax.psum_scatter(
        lax.dot_general(
            grad_block, student_rows, contract_first, preferred_element_type=jnp.float32
        ),
        "dp",
        scatter_dimension=0,
        tiled=True,
    )
    first_proto = lax.axis_index("dp") * own_protos
    own_units = lax.dynamic_slice_in_dim(proto_unit, first_proto, own_protos, 0)
    own_lengths = lax.dynamic_slice_in_dim(proto_length, first_proto, own_protos, 0)
    proto_grad = (
        pushed - own_units * jnp.sum(own_units * pushed, axis=1, keepdims=True)
    ) / own_lengths
    return (student_grad, proto_grad[None])


def on_device(student_feat, teacher_feat, prototypes, teacher_prototypes, live_count):
    n_dp, n_proto = lax.axis_size("dp"), lax.axis_size("proto")
    rows, width = student_feat.shape
    protos = prototypes.shape[0]
    lanes = n_dp * n_proto * rows
    fits = (
        n_proto == 2 * Y
        and n_dp & (n_dp - 1) == 0
        and rows % 4 == 0
        and rows <= 16
        and lanes % LANES == 0
        and lanes <= 8 * LANES
        and width == 2 * LANES
        and protos == n_dp * 2 * LANES
        and 4 * protos * lanes * 4 <= BLOCK_BYTES
    )
    plan = on_device_all_rows if fits else on_device_group_rows
    return plan(student_feat, teacher_feat, prototypes, teacher_prototypes, live_count)


def solution(mesh):
    return jax.shard_map(
        on_device,
        mesh=mesh,
        in_specs=(
            P(("dp", "proto"), None),
            P(("dp", "proto"), None),
            P("proto", None),
            P("proto", None),
            P(),
        ),
        out_specs=(P(("dp", "proto"), None), P("proto", "dp", None)),
        check_vma=False,
    )
```

```python
import functools

import jax
import jax.numpy as jnp
from jax import lax
from jax.experimental import pallas as pl
from jax.experimental.pallas import tpu as pltpu
from jax.sharding import PartitionSpec as P

ITERS = 3

student_temp = 0.1
teacher_temp = 0.07
eps_norm = 1e-06

LANES = 128
BLOCK_BYTES = 8 * 2**20


def unit_rows(values):
    widened = values.astype(jnp.float32)
    length = jnp.sqrt(jnp.sum(widened * widened, axis=1, keepdims=True) + eps_norm)
    return (widened / length, length)


CORE, X, Y = 1, 2, 4
X_CROSS, Y_CROSS = X | CORE, Y | CORE


def block_of(proto):
    return 2 * ((proto >> 2) & 1) + ((proto >> 1) & 1)


def own_place():
    return lax.axis_index("dp"), lax.axis_index("proto")


def quick_unit(values):
    widened = values.astype(jnp.float32)
    squares = jnp.sum(widened * widened, axis=1, keepdims=True) + eps_norm
    scale = lax.rsqrt(squares)
    return widened * scale, scale


def dp_order(n_dp):
    return [0, *reversed(range(1, n_dp))]


def live_lanes(place_ref, half, lanes, n_dp, rows):
    mine = place_ref[1]
    parity = (mine ^ (mine >> 1) ^ (mine >> 2)) & 1
    lane = lax.broadcasted_iota(jnp.int32, (1, lanes), 1)
    live = jnp.zeros((1, lanes), jnp.float32)
    start = 0
    for t in dp_order(n_dp):
        count = place_ref[2 + (place_ref[0] ^ t)]
        for y in range(2):
            for x in range(2):
                core = parity ^ x ^ y ^ half ^ (1 if t else 0)
                proto = core + X * x + Y * y
                end = start + jnp.clip(count - proto * rows, 0, rows)
                live = jnp.where((lane >= start) & (lane < end), 1.0, live)
                start += rows
    return live


def pack_lanes(values):
    pieces = [values[:, k : k + LANES] for k in range(0, values.shape[1], LANES)]
    return jnp.concatenate(pieces + [jnp.zeros((8 - len(pieces), LANES), jnp.float32)], axis=0)


def unpack_lanes(tile, lanes):
    return jnp.concatenate([tile[k : k + 1, :] for k in range(lanes // LANES)], axis=1)


def as_column(values):
    return jnp.broadcast_to(values, (LANES, values.shape[1])).T


def as_tile(partial):
    return pack_lanes(jnp.sum(partial.T, axis=0, keepdims=True))


def inverse_rows(tile, rows):
    total = unpack_lanes(tile, rows)
    live = total > 0.0
    return jnp.where(live, 1.0 / jnp.where(live, total, 1.0), 0.0)


def pair_kernel(mine_ref, other_ref, out_ref, scratch):
    rows = mine_ref.shape[0] // 2
    swapped = (own_place()[1] & X) > 0
    mine, other = [quick_unit(ref[...])[0] for ref in (mine_ref, other_ref)]
    pair = (jnp.where(swapped, other, mine), jnp.where(swapped, mine, other))
    for which in range(2):
        for x in range(2):
            start = (2 * which + x) * rows
            scratch[start : start + rows, :] = pair[x][which * rows : (which + 1) * rows]
    out_ref[...] = scratch[...].astype(jnp.bfloat16)


def place_rows(place, ref, which):
    mine_y = (place[1] >> 2) & 1
    pair = ref.shape[2] // 2
    blocks = [
        ref[mine_y ^ y, t].astype(jnp.float32)[which * pair : (which + 1) * pair]
        for t in range(ref.shape[1])
        for y in range(2)
    ]
    return jnp.concatenate(blocks, axis=0).astype(jnp.bfloat16)


def scores_of(rows_all, units):
    return lax.dot_general(
        rows_all, units, (((1,), (1,)), ((), ())), preferred_element_type=jnp.float32
    )


def twice(column):
    return jnp.concatenate([column, column], axis=1)


def spread(column, lanes):
    return jnp.concatenate([column] * (lanes // LANES), axis=1)


def weighted_rows(panels, left, scale_ref, part_ref, add=False):
    tiles = panels[0].shape[1] // LANES
    scales = [scale_ref[:, left + k * LANES : left + (k + 1) * LANES] for k in range(tiles)]
    top = 0
    for ref in panels:

        def body(i, _, ref=ref, top=top):
            at = pl.ds(pl.multiple_of(i * 8, 8), 8)
            to = pl.ds(pl.multiple_of(i * 8 + top, 8), 8)
            sums = [None] * 4
            for k in range(tiles):
                term = ref[at, k * LANES : (k + 1) * LANES] * scales[k]
                sums[k % 4] = term if sums[k % 4] is None else sums[k % 4] + term
            total = (sums[0] + sums[1]) + (sums[2] + sums[3])
            part_ref[to, :] = part_ref[to, :] + total if add else total
            return 0

        lax.fori_loop(0, ref.shape[0] // 8, body, 0, unroll=24)
        top += ref.shape[0]


def column_scales(panels, left, row_ref, scale_ref):
    tiles = panels[0].shape[1] // LANES
    sums = [jnp.zeros((8, LANES), jnp.float32)] * tiles
    top = 0
    for ref in panels:

        def body(i, sums, ref=ref, top=top):
            at = pl.ds(pl.multiple_of(i * 8, 8), 8)
            row = row_ref[pl.ds(pl.multiple_of(i * 8 + top, 8), 8), :]
            return [
                total + ref[at, k * LANES : (k + 1) * LANES] * row for k, total in enumerate(sums)
            ]

        sums = lax.fori_loop(0, ref.shape[0] // 8, body, sums, unroll=24)
        top += ref.shape[0]
    for k, total in enumerate(sums):
        inverse = 1.0 / jnp.sum(total, axis=0, keepdims=True)
        at = slice(left + k * LANES, left + (k + 1) * LANES)
        scale_ref[:, at] = jnp.broadcast_to(inverse, (8, LANES))


def weights_of(rows, units, live):
    weights = jnp.exp(scores_of(rows, units) * (1 / teacher_temp)) * live
    return weights, fold(weights)


def fold(values):
    return jnp.sum(values.reshape(values.shape[0] // 8, 8, values.shape[1]), axis=0)


def units_kernel(n_dp, rows, place_ref, proto_ref, units_ref, *live_refs):
    units_ref[...] = quick_unit(proto_ref[...])[0].astype(jnp.bfloat16)
    for k, live_ref in enumerate(live_refs):
        live_ref[...] = as_column(live_lanes(place_ref, k, live_ref.shape[0], n_dp, rows))


def near_kernel(chunk, near_ref, live_ref, own_units_ref, proto_ref, *refs):
    weights_ref, sums_ref, rows_ref, units_ref = refs
    rows_near = place_rows(own_place(), near_ref, 0)
    rows_ref[...] = rows_near
    live = spread(live_ref[...], chunk)
    protos = own_units_ref.shape[0]
    for start in range(0, 2 * protos, chunk):
        at = slice(start, start + chunk)
        if start < protos:
            units = own_units_ref[at, :]
        else:
            here = slice(start - protos, start - protos + chunk)
            units = quick_unit(proto_ref[here, :])[0].astype(jnp.bfloat16)
            units_ref[here, :] = units
        weights_ref[:, at], sums_ref[:, at] = weights_of(rows_near, units, live)


def far_kernel(chunk, far_ref, live_ref, near_weights_ref, near_sums_ref, *refs):
    *unit_refs, weights_ref, rows_ref, sums_ref, scale_ref, part_ref = refs
    rows_far = place_rows(own_place(), far_ref, 0)
    rows_ref[...] = rows_far
    live = spread(live_ref[...], chunk)
    protos = unit_refs[0].shape[0]
    for k, unit_ref in enumerate(unit_refs):
        for start in range(0, protos, chunk):
            at = slice(k * protos + start, k * protos + start + chunk)
            weights, sums = weights_of(rows_far, unit_ref[start : start + chunk, :], live)
            weights_ref[:, at] = weights
            inverse = 1.0 / jnp.sum(near_sums_ref[:, at] + sums, axis=0, keepdims=True)
            scale_ref[:, at] = jnp.broadcast_to(inverse, (8, chunk))
    weighted_rows([near_weights_ref, weights_ref], 0, scale_ref, part_ref)
    sums_ref[...] = as_tile(part_ref[...])


def across_kernel(chunk, near_ref, far_ref, *refs):
    near_rows_ref, far_rows_ref, near_live_ref, far_live_ref, *refs = refs
    *proto_refs, weights_ref, student_ref = refs
    protos = proto_refs[0].shape[0]
    rows_all = jnp.concatenate([near_rows_ref[...], far_rows_ref[...]], axis=0)
    live = spread(jnp.concatenate([near_live_ref[...], far_live_ref[...]], axis=0), chunk)
    for k, proto_ref in enumerate(proto_refs):
        for start in range(0, protos, chunk):
            units = quick_unit(proto_ref[start : start + chunk, :])[0].astype(jnp.bfloat16)
            at = slice(k * protos + start, k * protos + start + chunk)
            weights_ref[:, at], _ = weights_of(rows_all, units, live)
    half = student_ref.shape[0] // 2
    for k, ref in enumerate((near_ref, far_ref)):
        student_ref[k * half : (k + 1) * half, :] = place_rows(own_place(), ref, 1)


def scale_columns(sums, near_ref, far_ref, across_ref, row_ref, scale_ref):
    row_ref[...] = as_column(inverse_rows(sums, row_ref.shape[0]))
    column_scales([near_ref, far_ref], 0, row_ref, scale_ref)
    column_scales([across_ref], near_ref.shape[1], row_ref, scale_ref)


def next_sums(near_ref, far_ref, across_ref, scale_ref, part_ref):
    weighted_rows([near_ref, far_ref], 0, scale_ref, part_ref)
    weighted_rows([across_ref], near_ref.shape[1], scale_ref, part_ref, add=True)
    return as_tile(part_ref[...])


def step_kernel(mine_ref, other_ref, near_ref, far_ref, across_ref, sums_ref, *scratch):
    row_ref, scale_ref, part_ref = scratch
    sums = mine_ref[...] + other_ref[...]
    scale_columns(sums, near_ref, far_ref, across_ref, row_ref, scale_ref)
    sums_ref[...] = next_sums(near_ref, far_ref, across_ref, scale_ref, part_ref)


def split(values):
    high = values.astype(jnp.bfloat16)
    low = (values - high.astype(jnp.float32)).astype(jnp.bfloat16)
    return jnp.concatenate([high, low], axis=0)


def exps_kernel(chunk, rows_ref, *refs):
    *proto_refs, units_ref, pull_ref, sums_ref, exps_ref = refs
    all_rows = rows_ref.shape[0]
    protos = proto_refs[0].shape[0]
    first = pull_ref.shape[0]
    rows_all = rows_ref[...]
    part = jnp.zeros((all_rows, LANES), jnp.float32)
    pull = jnp.zeros((2 * first, pull_ref.shape[1]), jnp.float32)
    for k, proto_ref in enumerate(proto_refs):
        for start in range(0, protos, chunk):
            units = quick_unit(proto_ref[start : start + chunk, :])[0].astype(jnp.bfloat16)
            units_ref[k * protos + start : k * protos + start + chunk, :] = units
            exps_ref[...] = jnp.exp(scores_of(rows_all, units) * (1 / student_temp))
            for at in range(0, chunk, LANES):
                part = part + exps_ref[:, at : at + LANES]
            exps = split(exps_ref[:first, :])
            pull = pull + jnp.dot(exps, units, preferred_element_type=jnp.float32)
    pull_ref[...] = pull[:first] + pull[first:]
    sums_ref[...] = as_tile(part)


def last_kernel(chunk, rows, mine_ref, other_ref, near_ref, far_ref, across_ref, *refs):
    units_ref, exp_pull_ref, exp_sums_ref, scale_ref, keep_ref, send_ref, row_ref, blocks_ref = refs
    first = exp_pull_ref.shape[0]
    sums = mine_ref[...] + other_ref[...]
    scale_columns(sums, near_ref, far_ref, across_ref, row_ref, scale_ref)
    pull = jnp.zeros((2 * first, exp_pull_ref.shape[1]), jnp.float32)
    for start in range(0, units_ref.shape[0], chunk):
        at = slice(start, start + chunk)
        scaled = split(near_ref[:first, at] * scale_ref[:1, at])
        pull = pull + jnp.dot(scaled, units_ref[at, :], preferred_element_type=jnp.float32)
    pulls = (pull[:first] + pull[first:], exp_pull_ref[...])
    for k, pull in enumerate(pulls):
        for block in range(4):
            blocks_ref[k, block, :rows, :] = pull[block * rows : (block + 1) * rows]
    _, mine = own_place()
    for ref, proto in ((keep_ref, mine), (send_ref, mine ^ X)):
        for j, owner in enumerate((proto, proto ^ Y)):
            for k in range(2):
                start = (2 * j + k) * rows
                ref[start : start + rows, :] = blocks_ref[k, block_of(owner), :rows, :]
        ref[4 * rows :, :LANES] = exp_sums_ref[...]
        ref[4 * rows :, LANES:] = jnp.zeros_like(exp_sums_ref)


def last_sums_kernel(near_ref, far_ref, across_ref, scale_ref, sums_ref, part_ref):
    sums_ref[:, :LANES] = jnp.zeros_like(sums_ref[:, :LANES])
    sums_ref[:, LANES:] = next_sums(near_ref, far_ref, across_ref, scale_ref, part_ref)


def own_kernel(mine_ref, other_ref, near_rows_ref, far_rows_ref, *refs):
    student_rows_ref, teacher_proto_ref, proto_ref, feat_ref, *refs = refs
    targets_ref, exps_ref, unit_ref, scale_ref, row_unit_ref, row_scale_ref = refs
    teacher_rows = jnp.concatenate([near_rows_ref[...], far_rows_ref[...]], axis=0)
    own, all_rows = targets_ref.shape
    row_scale = inverse_rows(mine_ref[...] + other_ref[...], all_rows)
    live = jnp.where(row_scale > 0.0, 1.0, 0.0)
    first = pl.ds(pl.multiple_of(own_place()[0] * own, own), own)
    units = quick_unit(teacher_proto_ref[first, :])[0].astype(jnp.bfloat16)
    weights = jnp.exp(scores_of(units, teacher_rows) * (1 / teacher_temp)) * live
    inverse = 1.0 / jnp.sum(weights * row_scale, axis=1, keepdims=True)
    targets_ref[...] = weights * (inverse * (1 / student_temp))
    unit, scale = quick_unit(proto_ref[first, :])
    unit_ref[...] = unit
    scale_ref[...] = jnp.broadcast_to(scale, scale_ref.shape)
    units = unit.astype(jnp.bfloat16)
    exps = jnp.exp(scores_of(units, student_rows_ref[...]) * (1 / student_temp))
    exps_ref[...] = exps * (1 / student_temp)
    unit, scale = quick_unit(feat_ref[...])
    row_unit_ref[...] = unit
    row_scale_ref[...] = jnp.broadcast_to(scale, row_scale_ref.shape)


def grads_kernel(mine_ref, sums_ref, other_ref, targets_ref, exps_ref, *refs):
    unit_ref, scale_ref, rows_ref, row_unit_ref, row_scale_ref, *refs = refs
    student_out_ref, proto_out_ref = refs
    all_rows = targets_ref.shape[1]
    rows = row_unit_ref.shape[0]
    sums = sums_ref[...] + other_ref[2 * rows :, :]
    target_scale = inverse_rows(sums[:, LANES:], all_rows)
    exp_scale = jnp.where(target_scale > 0.0, 1.0 / unpack_lanes(sums[:, :LANES], all_rows), 0.0)

    grad = exps_ref[...] * exp_scale - targets_ref[...] * target_scale
    pushed = jnp.dot(grad.astype(jnp.bfloat16), rows_ref[...], preferred_element_type=jnp.float32)
    unit = unit_ref[...]
    along = jnp.sum(unit * pushed, axis=1, keepdims=True)
    proto_out_ref[0] = (pushed - unit * along) * scale_ref[...]

    row = lax.broadcasted_iota(jnp.int32, (rows, LANES), 0) + block_of(own_place()[1]) * rows
    here = lax.broadcasted_iota(jnp.int32, (rows, LANES), 1) == row
    target_column, exp_column = [
        jnp.sum(jnp.where(here, scale[:, :LANES], 0.0), axis=1, keepdims=True) * (1 / student_temp)
        for scale in (target_scale, exp_scale)
    ]
    target_pull, exp_pull = [
        mine_ref[k * rows : (k + 1) * rows, :] + other_ref[k * rows : (k + 1) * rows, :]
        for k in range(2)
    ]
    pulled = exp_pull * exp_column - target_pull * target_column
    unit = row_unit_ref[...]
    student_out_ref[...] = (
        pulled - unit * jnp.sum(unit * pulled, axis=1, keepdims=True)
    ) * row_scale_ref[...]


def call(kernel, out_shape, operands, smem=0, scratch=(), work=0):
    vmem = pl.BlockSpec(memory_space=pltpu.VMEM)
    return pl.pallas_call(
        kernel,
        out_shape=out_shape,
        in_specs=[pl.BlockSpec(memory_space=pltpu.SMEM)] * smem + [vmem] * (len(operands) - smem),
        out_specs=jax.tree.map(lambda _: vmem, out_shape),
        scratch_shapes=scratch,
        compiler_params=pltpu.CompilerParams(vmem_limit_bytes=24 * 2**20),
        cost_estimate=pl.CostEstimate(
            flops=512 * work, bytes_accessed=4 * work, transcendentals=work
        ),
    )(*operands)


def swap(values, axis, distance):
    others = [(k, k ^ distance) for k in range(lax.axis_size(axis))]
    return lax.ppermute(values, axis, others)


def swap_dp(values, t):
    n_dp, n_proto = lax.axis_size("dp"), lax.axis_size("proto")
    others = [
        (d * n_proto + p, (d ^ t) * n_proto + (p ^ CORE)) for d in range(n_dp) for p in range(n_proto)
    ]
    return lax.ppermute(values, ("dp", "proto"), others)


def on_device_all_rows(student_feat, teacher_feat, prototypes, teacher_prototypes, live_count):
    n_dp, n_proto = lax.axis_size("dp"), lax.axis_size("proto")
    rows, width = student_feat.shape
    protos = prototypes.shape[0]
    own = protos // n_dp
    piece = 2 * own
    all_rows = n_dp * n_proto * rows
    half = all_rows // 2
    first = 4 * rows
    held = 2 * protos
    f32 = functools.partial(jax.ShapeDtypeStruct, dtype=jnp.float32)
    bf16 = functools.partial(jax.ShapeDtypeStruct, dtype=jnp.bfloat16)
    place = jnp.stack([lax.axis_index("dp"), lax.axis_index("proto")]).astype(jnp.int32)
    place = jnp.concatenate([place, live_count])
    tile = f32((8, LANES))
    message = f32((4 * rows + 8, width))
    column = pltpu.VMEM((all_rows, LANES), jnp.float32)
    scale_row = pltpu.VMEM((8, held), jnp.float32)
    sweep_scratch = [column, pltpu.VMEM((8, 2 * held), jnp.float32), column]

    both = lax.optimization_barrier(jnp.concatenate([teacher_feat, student_feat], axis=0))
    across_x = swap(both, "proto", X_CROSS)
    across_x, late_protos, place = lax.optimization_barrier((across_x, teacher_prototypes, place))
    across_protos = swap(late_protos, "proto", X_CROSS)
    student_protos = (prototypes, swap(prototypes, "proto", CORE))
    teacher_protos = swap(late_protos, "proto", CORE)
    near = call(
        pair_kernel,
        bf16((4 * rows, width)),
        (both, across_x),
        scratch=[pltpu.VMEM((4 * rows, width), jnp.float32)],
    )
    near = jnp.stack([near] + [swap_dp(near, t) for t in dp_order(n_dp)[1:]])
    near, own_protos = lax.optimization_barrier((near, teacher_prototypes))
    live = f32((half, LANES))
    teacher_units, near_live, far_live = call(
        functools.partial(units_kernel, n_dp, rows),
        (bf16((protos, width)), live, live),
        (place, own_protos),
        smem=1,
        work=protos * width,
    )
    near = jnp.stack([near, swap(near, "proto", Y_CROSS)])
    near, teacher_units = lax.optimization_barrier((near, teacher_units))
    far = swap(near, "proto", CORE)

    near_weights, near_sums, near_rows, other_units = call(
        functools.partial(near_kernel, piece),
        (
            f32((half, held)),
            f32((8, held)),
            bf16((half, width)),
            bf16((protos, width)),
        ),
        (near, near_live, teacher_units, teacher_protos),
        work=held * half,
    )
    far_weights, far_rows, sums = call(
        functools.partial(far_kernel, piece),
        (f32((half, held)), bf16((half, width)), tile),
        (far, far_live, near_weights, near_sums, teacher_units, other_units),
        scratch=[scale_row, column],
        work=held * half,
    )
    sums = sums + swap(sums, "proto", Y_CROSS)
    sums, across_protos = lax.optimization_barrier((sums, across_protos))
    parts = (sums, swap(sums, "proto", X_CROSS))
    across_weights, student_rows = call(
        functools.partial(across_kernel, piece),
        (f32((all_rows, held)), bf16((all_rows, width))),
        (
            near,
            far,
            near_rows,
            far_rows,
            near_live,
            far_live,
            across_protos,
            swap(across_protos, "proto", CORE),
        ),
        work=held * all_rows,
    )
    weights = (near_weights, far_weights, across_weights)
    for _ in range(ITERS - 2):
        sums = call(
            step_kernel,
            tile,
            (*parts, *weights),
            scratch=sweep_scratch,
            work=held * all_rows,
        )
        sums, student_rows, *student_protos = lax.optimization_barrier(
            (sums, student_rows, *student_protos)
        )
        parts = (sums, swap(sums, "proto", Y_CROSS))
    student_units, exp_pull, exp_sums = call(
        functools.partial(exps_kernel, piece),
        (bf16((held, width)), f32((first, width)), tile),
        (student_rows, *student_protos),
        scratch=[pltpu.VMEM((all_rows, piece), jnp.float32)],
        work=held * all_rows,
    )
    scales, keep, send = call(
        functools.partial(last_kernel, own, rows),
        (f32((8, 2 * held)), message, message),
        (*parts, *weights, student_units, exp_pull, exp_sums),
        scratch=[column, pltpu.VMEM((2, 4, 16, width), jnp.float32)],
        work=held * all_rows,
    )
    last_sums = call(
        last_sums_kernel,
        f32((8, width)),
        (*weights, scales),
        scratch=[column],
        work=held * all_rows,
    )
    *parts, send = lax.optimization_barrier((*parts, send))
    targets, exps, own_units, own_scales, row_units, row_scales = call(
        own_kernel,
        (f32((own, all_rows)), f32((own, all_rows)), *([f32((own, width))] * 2), *([f32((rows, width))] * 2)),
        (*parts, near_rows, far_rows, student_rows, teacher_prototypes, prototypes, student_feat),
        work=own * all_rows,
    )
    total = keep + swap(send, "proto", X_CROSS)
    last_sums = total[4 * rows :] + last_sums
    return call(
        grads_kernel,
        (f32((rows, width)), f32((1, own, width))),
        (
            total,
            last_sums,
            swap(jnp.concatenate([total[2 * rows : 4 * rows], last_sums]), "proto", Y_CROSS),
            targets,
            exps,
            own_units,
            own_scales,
            student_rows,
            row_units,
            row_scales,
        ),
        work=own * all_rows,
    )


def sample_totals(values):
    return lax.psum(values, "proto")


def proto_totals(values):
    return lax.psum(values, "dp")


def on_device_group_rows(student_feat, teacher_feat, prototypes, teacher_prototypes, live_count):
    student_unit, student_length = unit_rows(student_feat)
    teacher_unit, teacher_length = unit_rows(teacher_feat)
    proto_unit, proto_length = unit_rows(prototypes)
    teacher_proto, teacher_proto_length = unit_rows(teacher_prototypes)
    proto_bf = proto_unit.astype(jnp.bfloat16)
    teacher_proto_bf = teacher_proto.astype(jnp.bfloat16)
    student_rows, teacher_rows = (
        lax.all_gather(student_unit.astype(jnp.bfloat16), "proto", axis=0, tiled=True),
        lax.all_gather(teacher_unit.astype(jnp.bfloat16), "proto", axis=0, tiled=True),
    )
    group_size = student_rows.shape[0]
    live_rows = live_count[lax.axis_index("dp")]
    live_mask = jnp.arange(group_size, dtype=jnp.int32) < live_rows
    live_column = live_mask[:, None]
    contract_last = (((1,), (1,)), ((), ()))
    logits = (
        lax.dot_general(student_rows, proto_bf, contract_last, preferred_element_type=jnp.float32)
        / student_temp
    )
    teacher_scores = (
        lax.dot_general(
            teacher_rows, teacher_proto_bf, contract_last, preferred_element_type=jnp.float32
        )
        / teacher_temp
    )
    weights = jnp.where(live_column, jnp.exp(teacher_scores), 0.0)
    partition = sample_totals(jnp.sum(jnp.exp(logits), axis=1))
    targets = weights
    for iteration in range(ITERS):
        targets = targets / proto_totals(jnp.sum(targets, axis=0))[None, :]
        row_sums = sample_totals(jnp.sum(targets, axis=1))
        targets = targets / jnp.where(live_mask, row_sums, 1.0)[:, None]
    student_probs = jnp.exp(logits - jnp.log(partition)[:, None])
    grad_block = jnp.where(live_column, (student_probs - targets) / student_temp, 0.0).astype(
        jnp.bfloat16
    )
    pulled = lax.psum_scatter(
        jnp.dot(grad_block, proto_bf, preferred_element_type=jnp.float32),
        "proto",
        scatter_dimension=0,
        tiled=True,
    )
    student_grad = (
        pulled - student_unit * jnp.sum(student_unit * pulled, axis=1, keepdims=True)
    ) / student_length
    own_protos = prototypes.shape[0] // lax.axis_size("dp")
    contract_first = (((0,), (0,)), ((), ()))
    pushed = lax.psum_scatter(
        lax.dot_general(
            grad_block, student_rows, contract_first, preferred_element_type=jnp.float32
        ),
        "dp",
        scatter_dimension=0,
        tiled=True,
    )
    first_proto = lax.axis_index("dp") * own_protos
    own_units = lax.dynamic_slice_in_dim(proto_unit, first_proto, own_protos, 0)
    own_lengths = lax.dynamic_slice_in_dim(proto_length, first_proto, own_protos, 0)
    proto_grad = (
        pushed - own_units * jnp.sum(own_units * pushed, axis=1, keepdims=True)
    ) / own_lengths
    return (student_grad, proto_grad[None])


def on_device(student_feat, teacher_feat, prototypes, teacher_prototypes, live_count):
    n_dp, n_proto = lax.axis_size("dp"), lax.axis_size("proto")
    rows, width = student_feat.shape
    protos = prototypes.shape[0]
    lanes = n_dp * n_proto * rows
    fits = (
        n_proto == 2 * Y
        and n_dp & (n_dp - 1) == 0
        and rows % 4 == 0
        and rows <= 16
        and lanes % LANES == 0
        and lanes <= 8 * LANES
        and width == 2 * LANES
        and protos == n_dp * 2 * LANES
        and 4 * protos * lanes * 4 <= BLOCK_BYTES
    )
    plan = on_device_all_rows if fits else on_device_group_rows
    return plan(student_feat, teacher_feat, prototypes, teacher_prototypes, live_count)


def solution(mesh):
    return jax.shard_map(
        on_device,
        mesh=mesh,
        in_specs=(
            P(("dp", "proto"), None),
            P(("dp", "proto"), None),
            P("proto", None),
            P("proto", None),
            P(),
        ),
        out_specs=(P(("dp", "proto"), None), P("proto", "dp", None)),
        check_vma=False,
    )
```

```python
import functools

import jax
import jax.numpy as jnp
from jax import lax
from jax.experimental import pallas as pl
from jax.experimental.pallas import tpu as pltpu
from jax.sharding import PartitionSpec as P

ITERS = 3

student_temp = 0.1
teacher_temp = 0.07
eps_norm = 1e-06

LANES = 128
BLOCK_BYTES = 8 * 2**20


def unit_rows(values):
    widened = values.astype(jnp.float32)
    length = jnp.sqrt(jnp.sum(widened * widened, axis=1, keepdims=True) + eps_norm)
    return (widened / length, length)


CORE, X, Y = 1, 2, 4
X_CROSS, Y_CROSS = X | CORE, Y | CORE


def block_of(proto):
    return (proto & X) + ((proto >> 2) & 1)


def own_place():
    return lax.axis_index("dp"), lax.axis_index("proto")


def quick_unit(values):
    widened = values.astype(jnp.float32)
    squares = jnp.sum(widened * widened, axis=1, keepdims=True) + eps_norm
    scale = lax.rsqrt(squares)
    return widened * scale, scale


def dp_order(n_dp):
    return [0, *reversed(range(1, n_dp))]


def live_lanes(place_ref, half, lanes, n_dp, rows):
    mine = place_ref[1]
    parity = (mine ^ (mine >> 1) ^ (mine >> 2)) & 1
    lane = lax.broadcasted_iota(jnp.int32, (1, lanes), 1)
    live = jnp.zeros((1, lanes), jnp.float32)
    start = 0
    for t in dp_order(n_dp):
        count = place_ref[2 + (place_ref[0] ^ t)]
        for x in range(2):
            for y in range(2):
                core = parity ^ x ^ y ^ half ^ (1 if t else 0)
                proto = core + X * x + Y * y
                end = start + jnp.clip(count - proto * rows, 0, rows)
                live = jnp.where((lane >= start) & (lane < end), 1.0, live)
                start += rows
    return live


def pack_lanes(values):
    pieces = [values[:, k : k + LANES] for k in range(0, values.shape[1], LANES)]
    return jnp.concatenate(pieces + [jnp.zeros((8 - len(pieces), LANES), jnp.float32)], axis=0)


def unpack_lanes(tile, lanes):
    return jnp.concatenate([tile[k : k + 1, :] for k in range(lanes // LANES)], axis=1)


def as_column(values):
    return jnp.broadcast_to(values, (LANES, values.shape[1])).T


def as_tile(partial):
    return pack_lanes(jnp.sum(partial.T, axis=0, keepdims=True))


def inverse_rows(tile, rows):
    total = unpack_lanes(tile, rows)
    live = total > 0.0
    return jnp.where(live, 1.0 / jnp.where(live, total, 1.0), 0.0)


def place_rows(place, ref, which, rows, scratch):
    mine_x, mine_y = (place[1] >> 1) & 1, (place[1] >> 2) & 1
    start = 0
    for t in range(ref.shape[1]):
        for x in range(2):
            for y in range(2):
                block = ref[mine_y ^ y, t, mine_x ^ x].astype(jnp.float32)
                scratch[start : start + rows, :] = block[which * rows : (which + 1) * rows]
                start += rows
    unit, _ = quick_unit(scratch[...])
    return unit.astype(jnp.bfloat16)


def scores_of(rows_all, units):
    return lax.dot_general(
        rows_all, units, (((1,), (1,)), ((), ())), preferred_element_type=jnp.float32
    )


def twice(column):
    return jnp.concatenate([column, column], axis=1)


def spread(column, lanes):
    return jnp.concatenate([column] * (lanes // LANES), axis=1)


def weighted_rows(panels, scale_ref, part_ref, across_ref=None):
    tiles = panels[0].shape[1] // LANES
    count = tiles if across_ref is None else 2 * tiles
    scales = [scale_ref[:, k * LANES : (k + 1) * LANES] for k in range(count)]
    top = 0
    for ref in panels:

        def body(i, _, ref=ref, top=top):
            at = pl.ds(pl.multiple_of(i * 8, 8), 8)
            to = pl.ds(pl.multiple_of(i * 8 + top, 8), 8)
            sums = [None] * 4
            for k in range(count):
                own = k < tiles
                j = k if own else k - tiles
                lanes = slice(j * LANES, (j + 1) * LANES)
                term = (ref[at, lanes] if own else across_ref[to, lanes]) * scales[k]
                sums[k % 4] = term if sums[k % 4] is None else sums[k % 4] + term
            part_ref[to, :] = (sums[0] + sums[1]) + (sums[2] + sums[3])
            return 0

        lax.fori_loop(0, ref.shape[0] // 8, body, 0, unroll=24)
        top += ref.shape[0]


def column_scales(panels, left, row_ref, scale_ref):
    tiles = panels[0].shape[1] // LANES
    sums = [jnp.zeros((8, LANES), jnp.float32)] * tiles
    top = 0
    for ref in panels:

        def body(i, sums, ref=ref, top=top):
            at = pl.ds(pl.multiple_of(i * 8, 8), 8)
            row = row_ref[pl.ds(pl.multiple_of(i * 8 + top, 8), 8), :]
            return [
                total + ref[at, k * LANES : (k + 1) * LANES] * row for k, total in enumerate(sums)
            ]

        sums = lax.fori_loop(0, ref.shape[0] // 8, body, sums, unroll=24)
        top += ref.shape[0]
    for k, total in enumerate(sums):
        inverse = 1.0 / jnp.sum(total, axis=0, keepdims=True)
        at = slice(left + k * LANES, left + (k + 1) * LANES)
        scale_ref[:, at] = jnp.broadcast_to(inverse, (8, LANES))


def weights_of(rows, units, live):
    weights = jnp.exp(scores_of(rows, units) * (1 / teacher_temp)) * live
    return weights, fold(weights)


def fold(values):
    return jnp.sum(values.reshape(values.shape[0] // 8, 8, values.shape[1]), axis=0)


def units_kernel(n_dp, rows, place_ref, proto_ref, units_ref, *live_refs):
    units_ref[...] = quick_unit(proto_ref[...])[0].astype(jnp.bfloat16)
    for k, live_ref in enumerate(live_refs):
        live_ref[...] = as_column(live_lanes(place_ref, k, live_ref.shape[0], n_dp, rows))


def near_kernel(chunk, near_ref, live_ref, own_units_ref, proto_ref, *refs):
    weights_ref, sums_ref, rows_ref, units_ref, scratch = refs
    rows = near_ref.shape[3] // 2
    rows_near = place_rows(own_place(), near_ref, 0, rows, scratch)
    rows_ref[...] = rows_near
    live = spread(live_ref[...], chunk)
    protos = own_units_ref.shape[0]
    for start in range(0, 2 * protos, chunk):
        at = slice(start, start + chunk)
        if start < protos:
            units = own_units_ref[at, :]
        else:
            here = slice(start - protos, start - protos + chunk)
            units = quick_unit(proto_ref[here, :])[0].astype(jnp.bfloat16)
            units_ref[here, :] = units
        weights_ref[:, at], sums_ref[:, at] = weights_of(rows_near, units, live)


def far_kernel(chunk, far_ref, live_ref, near_weights_ref, near_sums_ref, *refs):
    *unit_refs, weights_ref, rows_ref, sums_ref, scratch, scale_ref, part_ref = refs
    rows = far_ref.shape[3] // 2
    rows_far = place_rows(own_place(), far_ref, 0, rows, scratch)
    rows_ref[...] = rows_far
    live = spread(live_ref[...], chunk)
    protos = unit_refs[0].shape[0]
    for k, unit_ref in enumerate(unit_refs):
        for start in range(0, protos, chunk):
            at = slice(k * protos + start, k * protos + start + chunk)
            weights, sums = weights_of(rows_far, unit_ref[start : start + chunk, :], live)
            weights_ref[:, at] = weights
            inverse = 1.0 / jnp.sum(near_sums_ref[:, at] + sums, axis=0, keepdims=True)
            scale_ref[:, at] = jnp.broadcast_to(inverse, (8, chunk))
    weighted_rows([near_weights_ref, weights_ref], scale_ref, part_ref)
    sums_ref[...] = as_tile(part_ref[...])


def across_kernel(chunk, near_ref, far_ref, *refs):
    near_rows_ref, far_rows_ref, near_live_ref, far_live_ref, *refs = refs
    *proto_refs, weights_ref, student_ref, scratch = refs
    protos = proto_refs[0].shape[0]
    rows_all = jnp.concatenate([near_rows_ref[...], far_rows_ref[...]], axis=0)
    live = spread(jnp.concatenate([near_live_ref[...], far_live_ref[...]], axis=0), chunk)
    for k, proto_ref in enumerate(proto_refs):
        for start in range(0, protos, chunk):
            units = quick_unit(proto_ref[start : start + chunk, :])[0].astype(jnp.bfloat16)
            at = slice(k * protos + start, k * protos + start + chunk)
            weights_ref[:, at], _ = weights_of(rows_all, units, live)
    half = student_ref.shape[0] // 2
    for k, ref in enumerate((near_ref, far_ref)):
        rows_half = place_rows(own_place(), ref, 1, ref.shape[3] // 2, scratch)
        student_ref[k * half : (k + 1) * half, :] = rows_half


def scale_columns(sums, near_ref, far_ref, across_ref, row_ref, scale_ref):
    row_ref[...] = as_column(inverse_rows(sums, row_ref.shape[0]))
    column_scales([near_ref, far_ref], 0, row_ref, scale_ref)
    column_scales([across_ref], near_ref.shape[1], row_ref, scale_ref)


def next_sums(near_ref, far_ref, across_ref, scale_ref, part_ref):
    weighted_rows([near_ref, far_ref], scale_ref, part_ref, across_ref)
    return as_tile(part_ref[...])


def step_kernel(mine_ref, other_ref, near_ref, far_ref, across_ref, sums_ref, *scratch):
    row_ref, scale_ref, part_ref = scratch
    sums = mine_ref[...] + other_ref[...]
    scale_columns(sums, near_ref, far_ref, across_ref, row_ref, scale_ref)
    sums_ref[...] = next_sums(near_ref, far_ref, across_ref, scale_ref, part_ref)


def split(values):
    high = values.astype(jnp.bfloat16)
    low = (values - high.astype(jnp.float32)).astype(jnp.bfloat16)
    return jnp.concatenate([high, low], axis=0)


def exps_kernel(chunk, rows_ref, *refs):
    *proto_refs, units_ref, pull_ref, sums_ref, exps_ref = refs
    all_rows = rows_ref.shape[0]
    protos = proto_refs[0].shape[0]
    first = pull_ref.shape[0]
    rows_all = rows_ref[...]
    part = jnp.zeros((all_rows, LANES), jnp.float32)
    pull = jnp.zeros((2 * first, pull_ref.shape[1]), jnp.float32)
    for k, proto_ref in enumerate(proto_refs):
        for start in range(0, protos, chunk):
            units = quick_unit(proto_ref[start : start + chunk, :])[0].astype(jnp.bfloat16)
            units_ref[k * protos + start : k * protos + start + chunk, :] = units
            exps_ref[...] = jnp.exp(scores_of(rows_all, units) * (1 / student_temp))
            for at in range(0, chunk, LANES):
                part = part + exps_ref[:, at : at + LANES]
            exps = split(exps_ref[:first, :])
            pull = pull + jnp.dot(exps, units, preferred_element_type=jnp.float32)
    pull_ref[...] = pull[:first] + pull[first:]
    sums_ref[...] = as_tile(part)


def last_kernel(chunk, rows, mine_ref, other_ref, near_ref, far_ref, across_ref, *refs):
    units_ref, exp_pull_ref, exp_sums_ref, scale_ref, keep_ref, send_ref, row_ref, blocks_ref = refs
    first = exp_pull_ref.shape[0]
    sums = mine_ref[...] + other_ref[...]
    scale_columns(sums, near_ref, far_ref, across_ref, row_ref, scale_ref)
    pull = jnp.zeros((2 * first, exp_pull_ref.shape[1]), jnp.float32)
    for start in range(0, units_ref.shape[0], chunk):
        at = slice(start, start + chunk)
        scaled = split(near_ref[:first, at] * scale_ref[:1, at])
        pull = pull + jnp.dot(scaled, units_ref[at, :], preferred_element_type=jnp.float32)
    pulls = (pull[:first] + pull[first:], exp_pull_ref[...])
    for k, pull in enumerate(pulls):
        for block in range(4):
            blocks_ref[k, block, :rows, :] = pull[block * rows : (block + 1) * rows]
    _, mine = own_place()
    for ref, proto in ((keep_ref, mine), (send_ref, mine ^ X)):
        for j, owner in enumerate((proto, proto ^ Y)):
            for k in range(2):
                start = (2 * j + k) * rows
                ref[start : start + rows, :] = blocks_ref[k, block_of(owner), :rows, :]
        ref[4 * rows :, :LANES] = exp_sums_ref[...]
        ref[4 * rows :, LANES:] = jnp.zeros_like(exp_sums_ref)


def last_sums_kernel(near_ref, far_ref, across_ref, scale_ref, sums_ref, part_ref):
    sums_ref[:, :LANES] = jnp.zeros_like(sums_ref[:, :LANES])
    sums_ref[:, LANES:] = next_sums(near_ref, far_ref, across_ref, scale_ref, part_ref)


def own_kernel(mine_ref, other_ref, near_rows_ref, far_rows_ref, *refs):
    student_rows_ref, teacher_proto_ref, proto_ref, feat_ref, *refs = refs
    targets_ref, exps_ref, unit_ref, scale_ref, row_unit_ref, row_scale_ref = refs
    teacher_rows = jnp.concatenate([near_rows_ref[...], far_rows_ref[...]], axis=0)
    own, all_rows = targets_ref.shape
    row_scale = inverse_rows(mine_ref[...] + other_ref[...], all_rows)
    live = jnp.where(row_scale > 0.0, 1.0, 0.0)
    first = pl.ds(pl.multiple_of(own_place()[0] * own, own), own)
    units = quick_unit(teacher_proto_ref[first, :])[0].astype(jnp.bfloat16)
    weights = jnp.exp(scores_of(units, teacher_rows) * (1 / teacher_temp)) * live
    inverse = 1.0 / jnp.sum(weights * row_scale, axis=1, keepdims=True)
    targets_ref[...] = weights * (inverse * (1 / student_temp))
    unit, scale = quick_unit(proto_ref[first, :])
    unit_ref[...] = unit
    scale_ref[...] = jnp.broadcast_to(scale, scale_ref.shape)
    units = unit.astype(jnp.bfloat16)
    exps = jnp.exp(scores_of(units, student_rows_ref[...]) * (1 / student_temp))
    exps_ref[...] = exps * (1 / student_temp)
    unit, scale = quick_unit(feat_ref[...])
    row_unit_ref[...] = unit
    row_scale_ref[...] = jnp.broadcast_to(scale, row_scale_ref.shape)


def grads_kernel(mine_ref, sums_ref, other_ref, targets_ref, exps_ref, *refs):
    unit_ref, scale_ref, rows_ref, row_unit_ref, row_scale_ref, *refs = refs
    student_out_ref, proto_out_ref = refs
    all_rows = targets_ref.shape[1]
    rows = row_unit_ref.shape[0]
    sums = sums_ref[...] + other_ref[2 * rows :, :]
    target_scale = inverse_rows(sums[:, LANES:], all_rows)
    exp_scale = jnp.where(target_scale > 0.0, 1.0 / unpack_lanes(sums[:, :LANES], all_rows), 0.0)

    grad = exps_ref[...] * exp_scale - targets_ref[...] * target_scale
    pushed = jnp.dot(grad.astype(jnp.bfloat16), rows_ref[...], preferred_element_type=jnp.float32)
    unit = unit_ref[...]
    along = jnp.sum(unit * pushed, axis=1, keepdims=True)
    proto_out_ref[0] = (pushed - unit * along) * scale_ref[...]

    row = lax.broadcasted_iota(jnp.int32, (rows, LANES), 0) + block_of(own_place()[1]) * rows
    here = lax.broadcasted_iota(jnp.int32, (rows, LANES), 1) == row
    target_column, exp_column = [
        jnp.sum(jnp.where(here, scale[:, :LANES], 0.0), axis=1, keepdims=True) * (1 / student_temp)
        for scale in (target_scale, exp_scale)
    ]
    target_pull, exp_pull = [
        mine_ref[k * rows : (k + 1) * rows, :] + other_ref[k * rows : (k + 1) * rows, :]
        for k in range(2)
    ]
    pulled = exp_pull * exp_column - target_pull * target_column
    unit = row_unit_ref[...]
    student_out_ref[...] = (
        pulled - unit * jnp.sum(unit * pulled, axis=1, keepdims=True)
    ) * row_scale_ref[...]


def call(kernel, out_shape, operands, smem=0, scratch=(), work=0):
    vmem = pl.BlockSpec(memory_space=pltpu.VMEM)
    return pl.pallas_call(
        kernel,
        out_shape=out_shape,
        in_specs=[pl.BlockSpec(memory_space=pltpu.SMEM)] * smem + [vmem] * (len(operands) - smem),
        out_specs=jax.tree.map(lambda _: vmem, out_shape),
        scratch_shapes=scratch,
        compiler_params=pltpu.CompilerParams(vmem_limit_bytes=24 * 2**20),
        cost_estimate=pl.CostEstimate(
            flops=512 * work, bytes_accessed=4 * work, transcendentals=work
        ),
    )(*operands)


def swap(values, axis, distance):
    others = [(k, k ^ distance) for k in range(lax.axis_size(axis))]
    return lax.ppermute(values, axis, others)


def swap_dp(values, t):
    n_dp, n_proto = lax.axis_size("dp"), lax.axis_size("proto")
    others = [
        (d * n_proto + p, (d ^ t) * n_proto + (p ^ CORE)) for d in range(n_dp) for p in range(n_proto)
    ]
    return lax.ppermute(values, ("dp", "proto"), others)


def on_device_all_rows(student_feat, teacher_feat, prototypes, teacher_prototypes, live_count):
    n_dp, n_proto = lax.axis_size("dp"), lax.axis_size("proto")
    rows, width = student_feat.shape
    protos = prototypes.shape[0]
    own = protos // n_dp
    piece = 2 * own
    all_rows = n_dp * n_proto * rows
    half = all_rows // 2
    first = 4 * rows
    held = 2 * protos
    f32 = functools.partial(jax.ShapeDtypeStruct, dtype=jnp.float32)
    bf16 = functools.partial(jax.ShapeDtypeStruct, dtype=jnp.bfloat16)
    place = jnp.stack([lax.axis_index("dp"), lax.axis_index("proto")]).astype(jnp.int32)
    place = jnp.concatenate([place, live_count])
    tile = f32((8, LANES))
    message = f32((4 * rows + 8, width))
    row_scratch = pltpu.VMEM((half, width), jnp.float32)
    column = pltpu.VMEM((all_rows, LANES), jnp.float32)
    scale_row = pltpu.VMEM((8, held), jnp.float32)
    sweep_scratch = [column, pltpu.VMEM((8, 2 * held), jnp.float32), column]

    both = lax.optimization_barrier(jnp.concatenate([teacher_feat, student_feat], axis=0))
    across_x = swap(both, "proto", X_CROSS)
    across_x, late_protos, place = lax.optimization_barrier((across_x, teacher_prototypes, place))
    across_protos = swap(late_protos, "proto", X_CROSS)
    student_protos = (prototypes, swap(prototypes, "proto", CORE))
    teacher_protos = swap(late_protos, "proto", CORE)
    near = jnp.stack([both, across_x])
    near = jnp.stack([near] + [swap_dp(near, t) for t in dp_order(n_dp)[1:]])
    near, own_protos = lax.optimization_barrier((near, teacher_prototypes))
    live = f32((half, LANES))
    teacher_units, near_live, far_live = call(
        functools.partial(units_kernel, n_dp, rows),
        (bf16((protos, width)), live, live),
        (place, own_protos),
        smem=1,
        work=protos * width,
    )
    near = jnp.stack([near, swap(near, "proto", Y_CROSS)])
    near, teacher_units = lax.optimization_barrier((near, teacher_units))
    far = swap(near, "proto", CORE)

    near_weights, near_sums, near_rows, other_units = call(
        functools.partial(near_kernel, piece),
        (
            f32((half, held)),
            f32((8, held)),
            bf16((half, width)),
            bf16((protos, width)),
        ),
        (near, near_live, teacher_units, teacher_protos),
        scratch=[row_scratch],
        work=held * half,
    )
    far_weights, far_rows, sums = call(
        functools.partial(far_kernel, piece),
        (f32((half, held)), bf16((half, width)), tile),
        (far, far_live, near_weights, near_sums, teacher_units, other_units),
        scratch=[row_scratch, scale_row, column],
        work=held * half,
    )
    sums = sums + swap(sums, "proto", Y_CROSS)
    sums, across_protos = lax.optimization_barrier((sums, across_protos))
    parts = (sums, swap(sums, "proto", X_CROSS))
    across_weights, student_rows = call(
        functools.partial(across_kernel, piece),
        (f32((all_rows, held)), bf16((all_rows, width))),
        (
            near,
            far,
            near_rows,
            far_rows,
            near_live,
            far_live,
            across_protos,
            swap(across_protos, "proto", CORE),
        ),
        scratch=[row_scratch],
        work=held * all_rows,
    )
    weights = (near_weights, far_weights, across_weights)
    for _ in range(ITERS - 2):
        sums = call(
            step_kernel,
            tile,
            (*parts, *weights),
            scratch=sweep_scratch,
            work=held * all_rows,
        )
        sums, student_rows, *student_protos = lax.optimization_barrier(
            (sums, student_rows, *student_protos)
        )
        parts = (sums, swap(sums, "proto", Y_CROSS))
    student_units, exp_pull, exp_sums = call(
        functools.partial(exps_kernel, piece),
        (bf16((held, width)), f32((first, width)), tile),
        (student_rows, *student_protos),
        scratch=[pltpu.VMEM((all_rows, piece), jnp.float32)],
        work=held * all_rows,
    )
    scales, keep, send = call(
        functools.partial(last_kernel, own, rows),
        (f32((8, 2 * held)), message, message),
        (*parts, *weights, student_units, exp_pull, exp_sums),
        scratch=[column, pltpu.VMEM((2, 4, 16, width), jnp.float32)],
        work=held * all_rows,
    )
    last_sums = call(
        last_sums_kernel,
        f32((8, width)),
        (*weights, scales),
        scratch=[column],
        work=held * all_rows,
    )
    *parts, send = lax.optimization_barrier((*parts, send))
    targets, exps, own_units, own_scales, row_units, row_scales = call(
        own_kernel,
        (f32((own, all_rows)), f32((own, all_rows)), *([f32((own, width))] * 2), *([f32((rows, width))] * 2)),
        (*parts, near_rows, far_rows, student_rows, teacher_prototypes, prototypes, student_feat),
        work=own * all_rows,
    )
    total = keep + swap(send, "proto", X_CROSS)
    last_sums = total[4 * rows :] + last_sums
    return call(
        grads_kernel,
        (f32((rows, width)), f32((1, own, width))),
        (
            total,
            last_sums,
            swap(jnp.concatenate([total[2 * rows : 4 * rows], last_sums]), "proto", Y_CROSS),
            targets,
            exps,
            own_units,
            own_scales,
            student_rows,
            row_units,
            row_scales,
        ),
        work=own * all_rows,
    )


def sample_totals(values):
    return lax.psum(values, "proto")


def proto_totals(values):
    return lax.psum(values, "dp")


def on_device_group_rows(student_feat, teacher_feat, prototypes, teacher_prototypes, live_count):
    student_unit, student_length = unit_rows(student_feat)
    teacher_unit, teacher_length = unit_rows(teacher_feat)
    proto_unit, proto_length = unit_rows(prototypes)
    teacher_proto, teacher_proto_length = unit_rows(teacher_prototypes)
    proto_bf = proto_unit.astype(jnp.bfloat16)
    teacher_proto_bf = teacher_proto.astype(jnp.bfloat16)
    student_rows, teacher_rows = (
        lax.all_gather(student_unit.astype(jnp.bfloat16), "proto", axis=0, tiled=True),
        lax.all_gather(teacher_unit.astype(jnp.bfloat16), "proto", axis=0, tiled=True),
    )
    group_size = student_rows.shape[0]
    live_rows = live_count[lax.axis_index("dp")]
    live_mask = jnp.arange(group_size, dtype=jnp.int32) < live_rows
    live_column = live_mask[:, None]
    contract_last = (((1,), (1,)), ((), ()))
    logits = (
        lax.dot_general(student_rows, proto_bf, contract_last, preferred_element_type=jnp.float32)
        / student_temp
    )
    teacher_scores = (
        lax.dot_general(
            teacher_rows, teacher_proto_bf, contract_last, preferred_element_type=jnp.float32
        )
        / teacher_temp
    )
    weights = jnp.where(live_column, jnp.exp(teacher_scores), 0.0)
    partition = sample_totals(jnp.sum(jnp.exp(logits), axis=1))
    targets = weights
    for iteration in range(ITERS):
        targets = targets / proto_totals(jnp.sum(targets, axis=0))[None, :]
        row_sums = sample_totals(jnp.sum(targets, axis=1))
        targets = targets / jnp.where(live_mask, row_sums, 1.0)[:, None]
    student_probs = jnp.exp(logits - jnp.log(partition)[:, None])
    grad_block = jnp.where(live_column, (student_probs - targets) / student_temp, 0.0).astype(
        jnp.bfloat16
    )
    pulled = lax.psum_scatter(
        jnp.dot(grad_block, proto_bf, preferred_element_type=jnp.float32),
        "proto",
        scatter_dimension=0,
        tiled=True,
    )
    student_grad = (
        pulled - student_unit * jnp.sum(student_unit * pulled, axis=1, keepdims=True)
    ) / student_length
    own_protos = prototypes.shape[0] // lax.axis_size("dp")
    contract_first = (((0,), (0,)), ((), ()))
    pushed = lax.psum_scatter(
        lax.dot_general(
            grad_block, student_rows, contract_first, preferred_element_type=jnp.float32
        ),
        "dp",
        scatter_dimension=0,
        tiled=True,
    )
    first_proto = lax.axis_index("dp") * own_protos
    own_units = lax.dynamic_slice_in_dim(proto_unit, first_proto, own_protos, 0)
    own_lengths = lax.dynamic_slice_in_dim(proto_length, first_proto, own_protos, 0)
    proto_grad = (
        pushed - own_units * jnp.sum(own_units * pushed, axis=1, keepdims=True)
    ) / own_lengths
    return (student_grad, proto_grad[None])


def on_device(student_feat, teacher_feat, prototypes, teacher_prototypes, live_count):
    n_dp, n_proto = lax.axis_size("dp"), lax.axis_size("proto")
    rows, width = student_feat.shape
    protos = prototypes.shape[0]
    lanes = n_dp * n_proto * rows
    fits = (
        n_proto == 2 * Y
        and n_dp & (n_dp - 1) == 0
        and rows % 4 == 0
        and rows <= 16
        and lanes % LANES == 0
        and lanes <= 8 * LANES
        and width == 2 * LANES
        and protos == n_dp * 2 * LANES
        and 4 * protos * lanes * 4 <= BLOCK_BYTES
    )
    plan = on_device_all_rows if fits else on_device_group_rows
    return plan(student_feat, teacher_feat, prototypes, teacher_prototypes, live_count)


def solution(mesh):
    return jax.shard_map(
        on_device,
        mesh=mesh,
        in_specs=(
            P(("dp", "proto"), None),
            P(("dp", "proto"), None),
            P("proto", None),
            P("proto", None),
            P(),
        ),
        out_specs=(P(("dp", "proto"), None), P("proto", "dp", None)),
        check_vma=False,
    )
```

```python
import functools

import jax
import jax.numpy as jnp
from jax import lax
from jax.experimental import pallas as pl
from jax.experimental.pallas import tpu as pltpu
from jax.sharding import PartitionSpec as P

ITERS = 3

student_temp = 0.1
teacher_temp = 0.07
eps_norm = 1e-06

LANES = 128
BLOCK_BYTES = 8 * 2**20


def unit_rows(values):
    widened = values.astype(jnp.float32)
    length = jnp.sqrt(jnp.sum(widened * widened, axis=1, keepdims=True) + eps_norm)
    return (widened / length, length)


CORE, X, Y = 1, 2, 4
X_CROSS, Y_CROSS = X | CORE, Y | CORE


def block_of(proto):
    return (proto & X) + ((proto >> 2) & 1)


def own_place():
    return lax.axis_index("dp"), lax.axis_index("proto")


def quick_unit(values):
    widened = values.astype(jnp.float32)
    squares = jnp.sum(widened * widened, axis=1, keepdims=True) + eps_norm
    scale = lax.rsqrt(squares)
    return widened * scale, scale


def dp_order(n_dp):
    return [0, *reversed(range(1, n_dp))]


def live_lanes(place_ref, half, lanes, n_dp, rows):
    mine = place_ref[1]
    parity = (mine ^ (mine >> 1) ^ (mine >> 2)) & 1
    lane = lax.broadcasted_iota(jnp.int32, (1, lanes), 1)
    live = jnp.zeros((1, lanes), jnp.float32)
    start = 0
    for t in dp_order(n_dp):
        count = place_ref[2 + (place_ref[0] ^ t)]
        for x in range(2):
            for y in range(2):
                core = parity ^ x ^ y ^ half ^ (1 if t else 0)
                proto = core + X * x + Y * y
                end = start + jnp.clip(count - proto * rows, 0, rows)
                live = jnp.where((lane >= start) & (lane < end), 1.0, live)
                start += rows
    return live


def pack_lanes(values):
    pieces = [values[:, k : k + LANES] for k in range(0, values.shape[1], LANES)]
    return jnp.concatenate(pieces + [jnp.zeros((8 - len(pieces), LANES), jnp.float32)], axis=0)


def unpack_lanes(tile, lanes):
    return jnp.concatenate([tile[k : k + 1, :] for k in range(lanes // LANES)], axis=1)


def as_column(values):
    return jnp.broadcast_to(values, (LANES, values.shape[1])).T


def as_tile(partial):
    return pack_lanes(jnp.sum(partial.T, axis=0, keepdims=True))


def inverse_rows(tile, rows):
    total = unpack_lanes(tile, rows)
    live = total > 0.0
    return jnp.where(live, 1.0 / jnp.where(live, total, 1.0), 0.0)


def place_rows(place, ref, which, rows, scratch):
    mine_x, mine_y = (place[1] >> 1) & 1, (place[1] >> 2) & 1
    start = 0
    for t in range(ref.shape[1]):
        for x in range(2):
            for y in range(2):
                block = ref[mine_y ^ y, t, mine_x ^ x].astype(jnp.float32)
                scratch[start : start + rows, :] = block[which * rows : (which + 1) * rows]
                start += rows
    unit, _ = quick_unit(scratch[...])
    return unit.astype(jnp.bfloat16)


def scores_of(rows_all, units):
    return lax.dot_general(
        rows_all, units, (((1,), (1,)), ((), ())), preferred_element_type=jnp.float32
    )


def twice(column):
    return jnp.concatenate([column, column], axis=1)


def spread(column, lanes):
    return jnp.concatenate([column] * (lanes // LANES), axis=1)


def weighted_rows(panels, scale_ref, part_ref, across_ref=None):
    tiles = panels[0].shape[1] // LANES
    count = tiles if across_ref is None else 2 * tiles
    scales = [scale_ref[:, k * LANES : (k + 1) * LANES] for k in range(count)]
    top = 0
    for ref in panels:

        def body(i, _, ref=ref, top=top):
            at = pl.ds(pl.multiple_of(i * 8, 8), 8)
            to = pl.ds(pl.multiple_of(i * 8 + top, 8), 8)
            sums = [None] * 4
            for k in range(count):
                own = k < tiles
                j = k if own else k - tiles
                lanes = slice(j * LANES, (j + 1) * LANES)
                term = (ref[at, lanes] if own else across_ref[to, lanes]) * scales[k]
                sums[k % 4] = term if sums[k % 4] is None else sums[k % 4] + term
            part_ref[to, :] = (sums[0] + sums[1]) + (sums[2] + sums[3])
            return 0

        lax.fori_loop(0, ref.shape[0] // 8, body, 0, unroll=24)
        top += ref.shape[0]


def column_scales(panels, across_ref, row_ref, scale_ref):
    tiles = panels[0].shape[1] // LANES
    sums = [jnp.zeros((8, LANES), jnp.float32)] * (2 * tiles)
    top = 0
    for ref in panels:

        def body(i, sums, ref=ref, top=top):
            at = pl.ds(pl.multiple_of(i * 8, 8), 8)
            to = pl.ds(pl.multiple_of(i * 8 + top, 8), 8)
            row = row_ref[to, :]
            cut = [slice(k * LANES, (k + 1) * LANES) for k in range(tiles)]
            terms = [ref[at, lanes] * row for lanes in cut]
            terms += [across_ref[to, lanes] * row for lanes in cut]
            return [total + term for total, term in zip(sums, terms)]

        sums = lax.fori_loop(0, ref.shape[0] // 8, body, sums, unroll=8)
        top += ref.shape[0]
    for k, total in enumerate(sums):
        inverse = 1.0 / jnp.sum(total, axis=0, keepdims=True)
        scale_ref[:, k * LANES : (k + 1) * LANES] = jnp.broadcast_to(inverse, (8, LANES))


def weights_of(rows, units, live):
    weights = jnp.exp(scores_of(rows, units) * (1 / teacher_temp)) * live
    return weights, fold(weights)


def fold(values):
    return jnp.sum(values.reshape(values.shape[0] // 8, 8, values.shape[1]), axis=0)


def units_kernel(n_dp, rows, place_ref, proto_ref, units_ref, *live_refs):
    units_ref[...] = quick_unit(proto_ref[...])[0].astype(jnp.bfloat16)
    for k, live_ref in enumerate(live_refs):
        live_ref[...] = as_column(live_lanes(place_ref, k, live_ref.shape[0], n_dp, rows))


def near_kernel(chunk, near_ref, live_ref, own_units_ref, proto_ref, *refs):
    weights_ref, sums_ref, rows_ref, units_ref, scratch = refs
    rows = near_ref.shape[3] // 2
    rows_near = place_rows(own_place(), near_ref, 0, rows, scratch)
    rows_ref[...] = rows_near
    live = spread(live_ref[...], chunk)
    protos = own_units_ref.shape[0]
    for start in range(0, 2 * protos, chunk):
        at = slice(start, start + chunk)
        if start < protos:
            units = own_units_ref[at, :]
        else:
            here = slice(start - protos, start - protos + chunk)
            units = quick_unit(proto_ref[here, :])[0].astype(jnp.bfloat16)
            units_ref[here, :] = units
        weights_ref[:, at], sums_ref[:, at] = weights_of(rows_near, units, live)


def far_kernel(chunk, far_ref, live_ref, near_weights_ref, near_sums_ref, *refs):
    *unit_refs, weights_ref, rows_ref, sums_ref, scratch, scale_ref, part_ref = refs
    rows = far_ref.shape[3] // 2
    rows_far = place_rows(own_place(), far_ref, 0, rows, scratch)
    rows_ref[...] = rows_far
    live = spread(live_ref[...], chunk)
    protos = unit_refs[0].shape[0]
    for k, unit_ref in enumerate(unit_refs):
        for start in range(0, protos, chunk):
            at = slice(k * protos + start, k * protos + start + chunk)
            weights, sums = weights_of(rows_far, unit_ref[start : start + chunk, :], live)
            weights_ref[:, at] = weights
            inverse = 1.0 / jnp.sum(near_sums_ref[:, at] + sums, axis=0, keepdims=True)
            scale_ref[:, at] = jnp.broadcast_to(inverse, (8, chunk))
    weighted_rows([near_weights_ref, weights_ref], scale_ref, part_ref)
    sums_ref[...] = as_tile(part_ref[...])


def across_kernel(chunk, near_ref, far_ref, *refs):
    near_rows_ref, far_rows_ref, near_live_ref, far_live_ref, *refs = refs
    *proto_refs, weights_ref, student_ref, scratch = refs
    protos = proto_refs[0].shape[0]
    rows_all = jnp.concatenate([near_rows_ref[...], far_rows_ref[...]], axis=0)
    live = spread(jnp.concatenate([near_live_ref[...], far_live_ref[...]], axis=0), chunk)
    for k, proto_ref in enumerate(proto_refs):
        for start in range(0, protos, chunk):
            units = quick_unit(proto_ref[start : start + chunk, :])[0].astype(jnp.bfloat16)
            at = slice(k * protos + start, k * protos + start + chunk)
            weights_ref[:, at], _ = weights_of(rows_all, units, live)
    half = student_ref.shape[0] // 2
    for k, ref in enumerate((near_ref, far_ref)):
        rows_half = place_rows(own_place(), ref, 1, ref.shape[3] // 2, scratch)
        student_ref[k * half : (k + 1) * half, :] = rows_half


def scale_columns(sums, near_ref, far_ref, across_ref, row_ref, scale_ref):
    row_ref[...] = as_column(inverse_rows(sums, row_ref.shape[0]))
    column_scales([near_ref, far_ref], across_ref, row_ref, scale_ref)


def next_sums(near_ref, far_ref, across_ref, scale_ref, part_ref):
    weighted_rows([near_ref, far_ref], scale_ref, part_ref, across_ref)
    return as_tile(part_ref[...])


def step_kernel(mine_ref, other_ref, near_ref, far_ref, across_ref, sums_ref, *scratch):
    row_ref, scale_ref, part_ref = scratch
    sums = mine_ref[...] + other_ref[...]
    scale_columns(sums, near_ref, far_ref, across_ref, row_ref, scale_ref)
    sums_ref[...] = next_sums(near_ref, far_ref, across_ref, scale_ref, part_ref)


def split(values):
    high = values.astype(jnp.bfloat16)
    low = (values - high.astype(jnp.float32)).astype(jnp.bfloat16)
    return jnp.concatenate([high, low], axis=0)


def exps_kernel(chunk, rows_ref, *refs):
    *proto_refs, units_ref, pull_ref, sums_ref, exps_ref = refs
    all_rows = rows_ref.shape[0]
    protos = proto_refs[0].shape[0]
    first = pull_ref.shape[0]
    rows_all = rows_ref[...]
    part = jnp.zeros((all_rows, LANES), jnp.float32)
    pull = jnp.zeros((2 * first, pull_ref.shape[1]), jnp.float32)
    for k, proto_ref in enumerate(proto_refs):
        for start in range(0, protos, chunk):
            units = quick_unit(proto_ref[start : start + chunk, :])[0].astype(jnp.bfloat16)
            units_ref[k * protos + start : k * protos + start + chunk, :] = units
            exps_ref[...] = jnp.exp(scores_of(rows_all, units) * (1 / student_temp))
            for at in range(0, chunk, LANES):
                part = part + exps_ref[:, at : at + LANES]
            exps = split(exps_ref[:first, :])
            pull = pull + jnp.dot(exps, units, preferred_element_type=jnp.float32)
    pull_ref[...] = pull[:first] + pull[first:]
    sums_ref[...] = as_tile(part)


def last_kernel(chunk, rows, mine_ref, other_ref, near_ref, far_ref, across_ref, *refs):
    units_ref, exp_pull_ref, exp_sums_ref, scale_ref, keep_ref, send_ref, row_ref, blocks_ref = refs
    first = exp_pull_ref.shape[0]
    sums = mine_ref[...] + other_ref[...]
    scale_columns(sums, near_ref, far_ref, across_ref, row_ref, scale_ref)
    pull = jnp.zeros((2 * first, exp_pull_ref.shape[1]), jnp.float32)
    for start in range(0, units_ref.shape[0], chunk):
        at = slice(start, start + chunk)
        scaled = split(near_ref[:first, at] * scale_ref[:1, at])
        pull = pull + jnp.dot(scaled, units_ref[at, :], preferred_element_type=jnp.float32)
    pulls = (pull[:first] + pull[first:], exp_pull_ref[...])
    for k, pull in enumerate(pulls):
        for block in range(4):
            blocks_ref[k, block, :rows, :] = pull[block * rows : (block + 1) * rows]
    _, mine = own_place()
    for ref, proto in ((keep_ref, mine), (send_ref, mine ^ X)):
        for j, owner in enumerate((proto, proto ^ Y)):
            for k in range(2):
                start = (2 * j + k) * rows
                ref[start : start + rows, :] = blocks_ref[k, block_of(owner), :rows, :]
        ref[4 * rows :, :LANES] = exp_sums_ref[...]
        ref[4 * rows :, LANES:] = jnp.zeros_like(exp_sums_ref)


def last_sums_kernel(near_ref, far_ref, across_ref, scale_ref, sums_ref, part_ref):
    sums_ref[:, :LANES] = jnp.zeros_like(sums_ref[:, :LANES])
    sums_ref[:, LANES:] = next_sums(near_ref, far_ref, across_ref, scale_ref, part_ref)


def own_kernel(mine_ref, other_ref, near_rows_ref, far_rows_ref, *refs):
    student_rows_ref, teacher_proto_ref, proto_ref, feat_ref, *refs = refs
    targets_ref, exps_ref, unit_ref, scale_ref, row_unit_ref, row_scale_ref = refs
    teacher_rows = jnp.concatenate([near_rows_ref[...], far_rows_ref[...]], axis=0)
    own, all_rows = targets_ref.shape
    row_scale = inverse_rows(mine_ref[...] + other_ref[...], all_rows)
    live = jnp.where(row_scale > 0.0, 1.0, 0.0)
    first = pl.ds(pl.multiple_of(own_place()[0] * own, own), own)
    units = quick_unit(teacher_proto_ref[first, :])[0].astype(jnp.bfloat16)
    weights = jnp.exp(scores_of(units, teacher_rows) * (1 / teacher_temp)) * live
    inverse = 1.0 / jnp.sum(weights * row_scale, axis=1, keepdims=True)
    targets_ref[...] = weights * (inverse * (1 / student_temp))
    unit, scale = quick_unit(proto_ref[first, :])
    unit_ref[...] = unit
    scale_ref[...] = jnp.broadcast_to(scale, scale_ref.shape)
    units = unit.astype(jnp.bfloat16)
    exps = jnp.exp(scores_of(units, student_rows_ref[...]) * (1 / student_temp))
    exps_ref[...] = exps * (1 / student_temp)
    unit, scale = quick_unit(feat_ref[...])
    row_unit_ref[...] = unit
    row_scale_ref[...] = jnp.broadcast_to(scale, row_scale_ref.shape)


def grads_kernel(mine_ref, sums_ref, other_ref, targets_ref, exps_ref, *refs):
    unit_ref, scale_ref, rows_ref, row_unit_ref, row_scale_ref, *refs = refs
    student_out_ref, proto_out_ref = refs
    all_rows = targets_ref.shape[1]
    rows = row_unit_ref.shape[0]
    sums = sums_ref[...] + other_ref[2 * rows :, :]
    target_scale = inverse_rows(sums[:, LANES:], all_rows)
    exp_scale = jnp.where(target_scale > 0.0, 1.0 / unpack_lanes(sums[:, :LANES], all_rows), 0.0)

    grad = exps_ref[...] * exp_scale - targets_ref[...] * target_scale
    pushed = jnp.dot(grad.astype(jnp.bfloat16), rows_ref[...], preferred_element_type=jnp.float32)
    unit = unit_ref[...]
    along = jnp.sum(unit * pushed, axis=1, keepdims=True)
    proto_out_ref[0] = (pushed - unit * along) * scale_ref[...]

    row = lax.broadcasted_iota(jnp.int32, (rows, LANES), 0) + block_of(own_place()[1]) * rows
    here = lax.broadcasted_iota(jnp.int32, (rows, LANES), 1) == row
    target_column, exp_column = [
        jnp.sum(jnp.where(here, scale[:, :LANES], 0.0), axis=1, keepdims=True) * (1 / student_temp)
        for scale in (target_scale, exp_scale)
    ]
    target_pull, exp_pull = [
        mine_ref[k * rows : (k + 1) * rows, :] + other_ref[k * rows : (k + 1) * rows, :]
        for k in range(2)
    ]
    pulled = exp_pull * exp_column - target_pull * target_column
    unit = row_unit_ref[...]
    student_out_ref[...] = (
        pulled - unit * jnp.sum(unit * pulled, axis=1, keepdims=True)
    ) * row_scale_ref[...]


def call(kernel, out_shape, operands, smem=0, scratch=(), work=0):
    vmem = pl.BlockSpec(memory_space=pltpu.VMEM)
    return pl.pallas_call(
        kernel,
        out_shape=out_shape,
        in_specs=[pl.BlockSpec(memory_space=pltpu.SMEM)] * smem + [vmem] * (len(operands) - smem),
        out_specs=jax.tree.map(lambda _: vmem, out_shape),
        scratch_shapes=scratch,
        compiler_params=pltpu.CompilerParams(vmem_limit_bytes=24 * 2**20),
        cost_estimate=pl.CostEstimate(
            flops=512 * work, bytes_accessed=4 * work, transcendentals=work
        ),
    )(*operands)


def swap(values, axis, distance):
    others = [(k, k ^ distance) for k in range(lax.axis_size(axis))]
    return lax.ppermute(values, axis, others)


def swap_dp(values, t):
    n_dp, n_proto = lax.axis_size("dp"), lax.axis_size("proto")
    others = [
        (d * n_proto + p, (d ^ t) * n_proto + (p ^ CORE)) for d in range(n_dp) for p in range(n_proto)
    ]
    return lax.ppermute(values, ("dp", "proto"), others)


def on_device_all_rows(student_feat, teacher_feat, prototypes, teacher_prototypes, live_count):
    n_dp, n_proto = lax.axis_size("dp"), lax.axis_size("proto")
    rows, width = student_feat.shape
    protos = prototypes.shape[0]
    own = protos // n_dp
    piece = 2 * own
    all_rows = n_dp * n_proto * rows
    half = all_rows // 2
    first = 4 * rows
    held = 2 * protos
    f32 = functools.partial(jax.ShapeDtypeStruct, dtype=jnp.float32)
    bf16 = functools.partial(jax.ShapeDtypeStruct, dtype=jnp.bfloat16)
    place = jnp.stack([lax.axis_index("dp"), lax.axis_index("proto")]).astype(jnp.int32)
    place = jnp.concatenate([place, live_count])
    tile = f32((8, LANES))
    message = f32((4 * rows + 8, width))
    row_scratch = pltpu.VMEM((half, width), jnp.float32)
    column = pltpu.VMEM((all_rows, LANES), jnp.float32)
    scale_row = pltpu.VMEM((8, held), jnp.float32)
    sweep_scratch = [column, pltpu.VMEM((8, 2 * held), jnp.float32), column]

    both = lax.optimization_barrier(jnp.concatenate([teacher_feat, student_feat], axis=0))
    across_x = swap(both, "proto", X_CROSS)
    across_x, late_protos, place = lax.optimization_barrier((across_x, teacher_prototypes, place))
    across_protos = swap(late_protos, "proto", X_CROSS)
    student_protos = (prototypes, swap(prototypes, "proto", CORE))
    teacher_protos = swap(late_protos, "proto", CORE)
    near = jnp.stack([both, across_x])
    near = jnp.stack([near] + [swap_dp(near, t) for t in dp_order(n_dp)[1:]])
    near, own_protos = lax.optimization_barrier((near, teacher_prototypes))
    live = f32((half, LANES))
    teacher_units, near_live, far_live = call(
        functools.partial(units_kernel, n_dp, rows),
        (bf16((protos, width)), live, live),
        (place, own_protos),
        smem=1,
        work=protos * width,
    )
    near = jnp.stack([near, swap(near, "proto", Y_CROSS)])
    near, teacher_units = lax.optimization_barrier((near, teacher_units))
    far = swap(near, "proto", CORE)

    near_weights, near_sums, near_rows, other_units = call(
        functools.partial(near_kernel, piece),
        (
            f32((half, held)),
            f32((8, held)),
            bf16((half, width)),
            bf16((protos, width)),
        ),
        (near, near_live, teacher_units, teacher_protos),
        scratch=[row_scratch],
        work=held * half,
    )
    far_weights, far_rows, sums = call(
        functools.partial(far_kernel, piece),
        (f32((half, held)), bf16((half, width)), tile),
        (far, far_live, near_weights, near_sums, teacher_units, other_units),
        scratch=[row_scratch, scale_row, column],
        work=held * half,
    )
    sums = sums + swap(sums, "proto", Y_CROSS)
    sums, across_protos = lax.optimization_barrier((sums, across_protos))
    parts = (sums, swap(sums, "proto", X_CROSS))
    across_weights, student_rows = call(
        functools.partial(across_kernel, piece),
        (f32((all_rows, held)), bf16((all_rows, width))),
        (
            near,
            far,
            near_rows,
            far_rows,
            near_live,
            far_live,
            across_protos,
            swap(across_protos, "proto", CORE),
        ),
        scratch=[row_scratch],
        work=held * all_rows,
    )
    weights = (near_weights, far_weights, across_weights)
    for _ in range(ITERS - 2):
        sums = call(
            step_kernel,
            tile,
            (*parts, *weights),
            scratch=sweep_scratch,
            work=held * all_rows,
        )
        sums, student_rows, *student_protos = lax.optimization_barrier(
            (sums, student_rows, *student_protos)
        )
        parts = (sums, swap(sums, "proto", Y_CROSS))
    student_units, exp_pull, exp_sums = call(
        functools.partial(exps_kernel, piece),
        (bf16((held, width)), f32((first, width)), tile),
        (student_rows, *student_protos),
        scratch=[pltpu.VMEM((all_rows, piece), jnp.float32)],
        work=held * all_rows,
    )
    scales, keep, send = call(
        functools.partial(last_kernel, own, rows),
        (f32((8, 2 * held)), message, message),
        (*parts, *weights, student_units, exp_pull, exp_sums),
        scratch=[column, pltpu.VMEM((2, 4, 16, width), jnp.float32)],
        work=held * all_rows,
    )
    last_sums = call(
        last_sums_kernel,
        f32((8, width)),
        (*weights, scales),
        scratch=[column],
        work=held * all_rows,
    )
    *parts, send = lax.optimization_barrier((*parts, send))
    targets, exps, own_units, own_scales, row_units, row_scales = call(
        own_kernel,
        (f32((own, all_rows)), f32((own, all_rows)), *([f32((own, width))] * 2), *([f32((rows, width))] * 2)),
        (*parts, near_rows, far_rows, student_rows, teacher_prototypes, prototypes, student_feat),
        work=own * all_rows,
    )
    total = keep + swap(send, "proto", X_CROSS)
    last_sums = total[4 * rows :] + last_sums
    return call(
        grads_kernel,
        (f32((rows, width)), f32((1, own, width))),
        (
            total,
            last_sums,
            swap(jnp.concatenate([total[2 * rows : 4 * rows], last_sums]), "proto", Y_CROSS),
            targets,
            exps,
            own_units,
            own_scales,
            student_rows,
            row_units,
            row_scales,
        ),
        work=own * all_rows,
    )


def sample_totals(values):
    return lax.psum(values, "proto")


def proto_totals(values):
    return lax.psum(values, "dp")


def on_device_group_rows(student_feat, teacher_feat, prototypes, teacher_prototypes, live_count):
    student_unit, student_length = unit_rows(student_feat)
    teacher_unit, teacher_length = unit_rows(teacher_feat)
    proto_unit, proto_length = unit_rows(prototypes)
    teacher_proto, teacher_proto_length = unit_rows(teacher_prototypes)
    proto_bf = proto_unit.astype(jnp.bfloat16)
    teacher_proto_bf = teacher_proto.astype(jnp.bfloat16)
    student_rows, teacher_rows = (
        lax.all_gather(student_unit.astype(jnp.bfloat16), "proto", axis=0, tiled=True),
        lax.all_gather(teacher_unit.astype(jnp.bfloat16), "proto", axis=0, tiled=True),
    )
    group_size = student_rows.shape[0]
    live_rows = live_count[lax.axis_index("dp")]
    live_mask = jnp.arange(group_size, dtype=jnp.int32) < live_rows
    live_column = live_mask[:, None]
    contract_last = (((1,), (1,)), ((), ()))
    logits = (
        lax.dot_general(student_rows, proto_bf, contract_last, preferred_element_type=jnp.float32)
        / student_temp
    )
    teacher_scores = (
        lax.dot_general(
            teacher_rows, teacher_proto_bf, contract_last, preferred_element_type=jnp.float32
        )
        / teacher_temp
    )
    weights = jnp.where(live_column, jnp.exp(teacher_scores), 0.0)
    partition = sample_totals(jnp.sum(jnp.exp(logits), axis=1))
    targets = weights
    for iteration in range(ITERS):
        targets = targets / proto_totals(jnp.sum(targets, axis=0))[None, :]
        row_sums = sample_totals(jnp.sum(targets, axis=1))
        targets = targets / jnp.where(live_mask, row_sums, 1.0)[:, None]
    student_probs = jnp.exp(logits - jnp.log(partition)[:, None])
    grad_block = jnp.where(live_column, (student_probs - targets) / student_temp, 0.0).astype(
        jnp.bfloat16
    )
    pulled = lax.psum_scatter(
        jnp.dot(grad_block, proto_bf, preferred_element_type=jnp.float32),
        "proto",
        scatter_dimension=0,
        tiled=True,
    )
    student_grad = (
        pulled - student_unit * jnp.sum(student_unit * pulled, axis=1, keepdims=True)
    ) / student_length
    own_protos = prototypes.shape[0] // lax.axis_size("dp")
    contract_first = (((0,), (0,)), ((), ()))
    pushed = lax.psum_scatter(
        lax.dot_general(
            grad_block, student_rows, contract_first, preferred_element_type=jnp.float32
        ),
        "dp",
        scatter_dimension=0,
        tiled=True,
    )
    first_proto = lax.axis_index("dp") * own_protos
    own_units = lax.dynamic_slice_in_dim(proto_unit, first_proto, own_protos, 0)
    own_lengths = lax.dynamic_slice_in_dim(proto_length, first_proto, own_protos, 0)
    proto_grad = (
        pushed - own_units * jnp.sum(own_units * pushed, axis=1, keepdims=True)
    ) / own_lengths
    return (student_grad, proto_grad[None])


def on_device(student_feat, teacher_feat, prototypes, teacher_prototypes, live_count):
    n_dp, n_proto = lax.axis_size("dp"), lax.axis_size("proto")
    rows, width = student_feat.shape
    protos = prototypes.shape[0]
    lanes = n_dp * n_proto * rows
    fits = (
        n_proto == 2 * Y
        and n_dp & (n_dp - 1) == 0
        and rows % 4 == 0
        and rows <= 16
        and lanes % LANES == 0
        and lanes <= 8 * LANES
        and width == 2 * LANES
        and protos == n_dp * 2 * LANES
        and 4 * protos * lanes * 4 <= BLOCK_BYTES
    )
    plan = on_device_all_rows if fits else on_device_group_rows
    return plan(student_feat, teacher_feat, prototypes, teacher_prototypes, live_count)


def solution(mesh):
    return jax.shard_map(
        on_device,
        mesh=mesh,
        in_specs=(
            P(("dp", "proto"), None),
            P(("dp", "proto"), None),
            P("proto", None),
            P("proto", None),
            P(),
        ),
        out_specs=(P(("dp", "proto"), None), P("proto", "dp", None)),
        check_vma=False,
    )
```
